32 devices in a mesh: path: 2 (over core), lon: 8 (over z, x), lat: 2 (over y).
Axes of the slice: x: 2, y: 2, z: 4, core: 2. Of those that a mesh axis runs over, the one named last changes fastest.
Arguments:
- observed: bfloat16 [128, 32, 384], P('lon', 'lat'), may hold values from -6 to 6
- baseline: bfloat16 [128, 32, 384], P('lon', 'lat'), may hold values from -6 to 6
- cotangent: bfloat16 [128, 32, 384], P('lon', 'lat'), may hold values from -6 to 6
- first_weight: bfloat16 [9, 384, 384], P(None, 'path'), may hold values from -0.109375 to 0.109375
- first_bias: float32 [384], replicated, may hold values from -3 to 3
- second_weight: bfloat16 [9, 384, 384], P(None, 'path'), may hold values from -0.109375 to 0.109375
- second_bias: float32 [384], replicated, may hold values from -3 to 3
Outputs:
- attribution: bfloat16 [128, 32, 384], P(('lon', 'path'), 'lat')
The draws below stay inside these ranges and needn't reach their ends.
All inputs are finite; a program needn't handle non-finite values.
Results may differ from the reference program's by a relative error of at most 0.0038.
Values may be sent and summed in bfloat16 or wider, within the bound.
No kernel may reach another device: no remote copies, remote signals or barrier semaphores. Data moves between devices by JAX's collectives and lax.ppermute only.
A program may use at most 64 MiB of HBM per device.

```python
import jax
import jax.numpy as jnp

C = 384
NEAR = 4
FAR = 16
NLON = 128
NLAT = 32
N_PATH = 2


def block_levels(key, extent, split, least, high):
    def one(dim, shards_of):
        draws = jax.random.uniform(jax.random.fold_in(jax.random.fold_in(key, 6), dim), (shards_of,), jnp.float32, least / len(split), high / len(split))
        return jnp.repeat(jnp.exp(draws), extent[dim] // shards_of).reshape((-1,) + (1,) * (len(extent) - dim - 1))

    loudness = one(*split[0])
    for cut in split[1:]:
        loudness = loudness * one(*cut)
    return loudness


def bell_draw(rng, dims, deviation, most, cuts=(), held_as=jnp.bfloat16):
    gain = block_levels(rng, dims, cuts, -0.22, 0.18) if cuts else 1.0
    values = jax.random.normal(rng, dims, jnp.float32) * deviation * gain
    return jnp.minimum(jnp.maximum(values, -most), most).astype(held_as)


def setup_inputs(seed: int = 0) -> dict:
    key_list = jax.random.split(jax.random.key(seed), 8)
    observed = bell_draw(key_list[0], (NLON, NLAT, C), 1.0, 6.0, ((0, 8), (1, 2)))
    baseline = bell_draw(key_list[1], (NLON, NLAT, C), 1.0, 6.0, ((0, 8), (1, 2)))
    cotangent = bell_draw(key_list[2], (NLON, NLAT, C), 1.0, 6.0, ((0, 8), (1, 2)))
    first_weight = bell_draw(key_list[3], (9, C, C), (9 * C) ** -0.5, 0.109375, ((1, 2),))
    first_bias = bell_draw(key_list[4], (C,), 0.5, 3.0, (), jnp.float32)
    second_weight = bell_draw(key_list[5], (9, C, C), (9 * C) ** -0.5, 0.109375, ((1, 2),))
    second_bias = bell_draw(key_list[6], (C,), 0.5, 3.0, (), jnp.float32)
    return {"observed": observed, "baseline": baseline, "cotangent": cotangent, "first_weight": first_weight, "first_bias": first_bias, "second_weight": second_weight, "second_bias": second_bias}


def smooth_act(value):
    return jax.nn.gelu(value, approximate=True)

def act_adjoint(pre_value, upstream):
    unused, pullback = jax.vjp(smooth_act, pre_value)
    return pullback(upstream)[0]

def stencil(field, weights, dilation, forward):
    rows, cols = (field.shape[0], field.shape[1])
    padded = jnp.pad(field, ((dilation, dilation), (dilation, dilation), (0, 0)))
    accumulated = jnp.zeros((rows, cols, weights.shape[1]), jnp.float32)
    for offset_row in (-1, 0, 1):
        for offset_col in (-1, 0, 1):
            tap_index = (offset_row + 1) * 3 + offset_col + 1
            sign = 1 if forward else -1
            start_row = dilation + sign * offset_row * dilation
            start_col = dilation + sign * offset_col * dilation
            window = padded[start_row:start_row + rows, start_col:start_col + cols, :].astype(jnp.float32)
            kernel = weights[tap_index].astype(jnp.float32)
            if forward:
                accumulated = accumulated + jnp.einsum('lmc,co->lmo', window, kernel)
            else:
                accumulated = accumulated + jnp.einsum('lmo,co->lmc', window, kernel)
    return accumulated

def reference(observed, baseline, cotangent, first_weight, first_bias, second_weight, second_bias):
    diff = observed.astype(jnp.float32) - baseline.astype(jnp.float32)
    upstream = cotangent.astype(jnp.float32)
    grad_sum = jnp.zeros(diff.shape, jnp.float32)
    for point in range(N_PATH):
        mix_weight = (point + 0.5) / N_PATH
        point_field = (baseline.astype(jnp.float32) + mix_weight * diff).astype(jnp.bfloat16)
        first_pre = stencil(point_field, first_weight, NEAR, True) + first_bias
        hidden = (point_field.astype(jnp.float32) + smooth_act(first_pre)).astype(jnp.bfloat16)
        second_pre = stencil(hidden, second_weight, FAR, True) + second_bias
        second_adj = act_adjoint(second_pre, upstream).astype(jnp.bfloat16)
        hidden_adj = upstream + stencil(second_adj, second_weight, FAR, False)
        first_adj = act_adjoint(first_pre, hidden_adj).astype(jnp.bfloat16)
        point_grad = hidden_adj + stencil(first_adj, first_weight, NEAR, False)
        grad_sum = grad_sum + point_grad
    return (diff * grad_sum / N_PATH).astype(jnp.bfloat16)
```

```python
import math

import jax
import jax.numpy as jnp
from jax import lax
from jax.sharding import PartitionSpec as P

NEAR = 4
FAR = 16


def smooth_act(value):
    return jax.nn.gelu(value, approximate=True)


def act_adjoint(pre_value, upstream):
    unused, pullback = jax.vjp(smooth_act, pre_value)
    return pullback(upstream)[0]


def group_sizes():
    lat = math.gcd(lax.axis_size("lat"), NEAR * NEAR)
    return NEAR * NEAR // lat, lat


def swap(chunks):
    group_lon, group_lat = group_sizes()
    lon, lat = lax.axis_size("lon"), lax.axis_size("lat")
    if (lon, lat) == (group_lon, group_lat):
        return lax.all_to_all(chunks, ("lon", "lat"), 0, 0, tiled=True)
    chunks = chunks.reshape((group_lon, group_lat) + chunks.shape[1:])
    for axis, dim, size in (("lon", 0, group_lon), ("lat", 1, group_lat)):
        count = lax.axis_size(axis)
        groups = [list(range(i, i + size)) for i in range(0, count, size)]
        chunks = lax.all_to_all(chunks, axis, dim, dim, tiled=True, axis_index_groups=groups)
    return chunks.reshape((group_lon * group_lat,) + chunks.shape[2:])


def to_classes(cells):
    rows, cols, depth = cells.shape
    cells = cells.reshape(rows // NEAR, NEAR, cols // NEAR, NEAR, depth).transpose(1, 3, 0, 2, 4)
    return cells.reshape(NEAR * NEAR, rows // NEAR, cols // NEAR, depth)


def padded(cells, width):
    for axis, dim, step in zip(("lon", "lat"), (0, 1), group_sizes()):
        count = lax.axis_size(axis)
        head = lax.slice_in_dim(cells, 0, width, axis=dim)
        tail = lax.slice_in_dim(cells, cells.shape[dim] - width, cells.shape[dim], axis=dim)
        if count == step:
            before, after = jnp.zeros_like(tail), jnp.zeros_like(head)
        else:
            before = lax.ppermute(tail, axis, [(i, i + step) for i in range(count - step)])
            after = lax.ppermute(head, axis, [(i + step, i) for i in range(count - step)])
        cells = jnp.concatenate([before, cells, after], axis=dim)
    return cells


def stencil(cells, weights, step, forward):
    rows, cols, depth = cells.shape
    around = padded(cells, step)
    total = jnp.zeros((rows, cols, depth), jnp.float32)
    for tap in range(9):
        sign = step if forward else -step
        row, col = step + (tap // 3 - 1) * sign, step + (tap % 3 - 1) * sign
        window = around[row : row + rows, col : col + cols]
        dims = (((2,), (0 if forward else 1,)), ((), ()))
        total = total + lax.dot_general(window, weights[tap], dims, preferred_element_type=jnp.float32)
    return total


def shards(observed, baseline, cotangent, first_weight, first_bias, second_weight, second_bias):
    rows, cols, depth = observed.shape
    points, point = lax.axis_size("path"), lax.axis_index("path")
    group_lon, group_lat = group_sizes()
    row_part, col_part = rows // NEAR, cols // NEAR
    ring = [(i, (i + 1) % points) for i in range(points)]

    def whole_weight(part):
        held = jnp.zeros((part.shape[0], points) + part.shape[1:], part.dtype)
        for step in range(points):
            held = lax.dynamic_update_slice_in_dim(held, part[:, None], (point - step) % points, 1)
            if step < points - 1:
                part = lax.ppermute(part, "path", ring)
        return held.reshape(held.shape[0], -1, held.shape[3])

    first_full, second_full = whole_weight(first_weight), whole_weight(second_weight)
    diff = observed.astype(jnp.float32) - baseline.astype(jnp.float32)
    mix = (point.astype(jnp.float32) + 0.5) / points
    field = (baseline.astype(jnp.float32) + mix * diff).astype(jnp.bfloat16)
    sent = jnp.stack([to_classes(field), to_classes(cotangent)], axis=1)
    got = swap(sent).reshape(group_lon, group_lat, 2, row_part, col_part, depth)
    got = got.transpose(2, 0, 3, 1, 4, 5).reshape(2, group_lon * row_part, group_lat * col_part, depth)
    field, upstream = got[0], got[1].astype(jnp.float32)

    first_pre = stencil(field, first_full, 1, True) + first_bias
    hidden = (field.astype(jnp.float32) + smooth_act(first_pre)).astype(jnp.bfloat16)
    second_pre = stencil(hidden, second_full, FAR // NEAR, True) + second_bias
    second_adj = act_adjoint(second_pre, upstream).astype(jnp.bfloat16)
    hidden_adj = upstream + stencil(second_adj, second_full, FAR // NEAR, False)
    first_adj = act_adjoint(first_pre, hidden_adj).astype(jnp.bfloat16)
    grad = hidden_adj + stencil(first_adj, first_full, 1, False)

    part = row_part // points
    grad = grad.reshape(group_lon, points, part, group_lat, col_part, depth).transpose(1, 0, 3, 2, 4, 5)
    grad = grad.reshape(points, group_lon * group_lat, part, col_part, depth)
    total = lax.dynamic_index_in_dim(grad, point, 0, keepdims=False)
    for step in range(1, points):
        other = lax.dynamic_index_in_dim(grad, (point + step) % points, 0, keepdims=False)
        total = total + lax.ppermute(other, "path", [(i, (i + step) % points) for i in range(points)])
    home = swap(total.astype(jnp.bfloat16)).reshape(NEAR, NEAR, part, col_part, depth)
    home = home.transpose(2, 0, 3, 1, 4).reshape(rows // points, cols, depth).astype(jnp.float32)
    diff_rows = lax.dynamic_slice_in_dim(diff, point * (rows // points), rows // points, 0)
    return (diff_rows * home / points).astype(jnp.bfloat16)


def solution(mesh):
    placed = (
        P("lon", "lat", None),
        P("lon", "lat", None),
        P("lon", "lat", None),
        P(None, "path", None),
        P(),
        P(None, "path", None),
        P(),
    )
    return jax.shard_map(
        shards,
        mesh=mesh,
        in_specs=placed,
        out_specs=P(("lon", "path"), "lat", None),
        check_vma=False,
    )
```

```python
import math

import jax
import jax.numpy as jnp
import numpy as np
from jax import lax
from jax.experimental import pallas as pl
from jax.experimental.pallas import tpu as pltpu
from jax.sharding import PartitionSpec as P

NEAR = 4
FAR = 16
EDGE = 8
LANES = 128
F32, BF16 = jnp.float32, jnp.bfloat16
VMEM = pl.BlockSpec(memory_space=pltpu.VMEM)
ANY = pl.BlockSpec(memory_space=pl.ANY)

def smooth_act(value):
    return jax.nn.gelu(value, approximate=True)


def act_adjoint(pre_value, upstream):
    unused, pullback = jax.vjp(smooth_act, pre_value)
    return pullback(upstream)[0]


def group_sizes():
    lat = math.gcd(lax.axis_size("lat"), NEAR * NEAR)
    return NEAR * NEAR // lat, lat


def swap(chunks):
    group_lon, group_lat = group_sizes()
    lon, lat = lax.axis_size("lon"), lax.axis_size("lat")
    if (lon, lat) == (group_lon, group_lat):
        return lax.all_to_all(chunks, ("lon", "lat"), 0, 0, tiled=True)
    chunks = chunks.reshape((group_lon, group_lat) + chunks.shape[1:])
    for axis, dim, size in (("lon", 0, group_lon), ("lat", 1, group_lat)):
        count = lax.axis_size(axis)
        groups = [list(range(i, i + size)) for i in range(0, count, size)]
        chunks = lax.all_to_all(chunks, axis, dim, dim, tiled=True, axis_index_groups=groups)
    return chunks.reshape((group_lon * group_lat,) + chunks.shape[2:])


def to_classes(cells):
    rows, cols, depth = cells.shape
    cells = cells.reshape(rows // NEAR, NEAR, cols // NEAR, NEAR, depth).transpose(1, 3, 0, 2, 4)
    return cells.reshape(NEAR * NEAR, rows // NEAR, cols // NEAR, depth)


def padded(cells, width):
    for axis, dim, step in zip(("lon", "lat"), (0, 1), group_sizes()):
        count = lax.axis_size(axis)
        head = lax.slice_in_dim(cells, 0, width, axis=dim)
        tail = lax.slice_in_dim(cells, cells.shape[dim] - width, cells.shape[dim], axis=dim)
        if count == step:
            before, after = jnp.zeros_like(tail), jnp.zeros_like(head)
        else:
            before = lax.ppermute(tail, axis, [(i, i + step) for i in range(count - step)])
            after = lax.ppermute(head, axis, [(i + step, i) for i in range(count - step)])
        cells = jnp.concatenate([before, cells, after], axis=dim)
    return cells


def stencil(cells, weights, step, forward):
    rows, cols, depth = cells.shape
    around = padded(cells, step)
    total = jnp.zeros((rows, cols, depth), jnp.float32)
    for tap in range(9):
        sign = step if forward else -step
        row, col = step + (tap // 3 - 1) * sign, step + (tap % 3 - 1) * sign
        window = around[row : row + rows, col : col + cols]
        dims = (((2,), (0 if forward else 1,)), ((), ()))
        total = total + lax.dot_general(window, weights[tap], dims, preferred_element_type=jnp.float32)
    return total


def one_hot(source):
    return jnp.asarray(np.eye(source.size, dtype=np.float32)[source.reshape(-1)], BF16)


def gelu_and_slope(value):
    scale, cubic = math.sqrt(2 / math.pi), 0.044715
    square = value * value
    bent = jnp.tanh(scale * value * (1 + cubic * square))
    half = 0.5 * (1 + bent)
    return value * half, half + 0.5 * value * (1 - bent * bent) * (scale * (1 + 3 * cubic * square))


def call(kernel, outs, scratch, name, megabytes, *args, specs=None):
    shapes = [jax.ShapeDtypeStruct(shape, dtype) for shape, dtype in outs]
    return pl.pallas_call(
        kernel,
        out_shape=shapes,
        in_specs=specs or [VMEM] * len(args),
        out_specs=[VMEM] * len(outs),
        scratch_shapes=scratch,
        compiler_params=pltpu.CompilerParams(vmem_limit_bytes=megabytes << 20),
        name=name,
    )(*args)


def pack_classes(observed, baseline, cotangent):
    rows, cols, depth = observed.shape
    points, point = lax.axis_size("path"), lax.axis_index("path")
    cells, part = rows * cols, rows * cols // (NEAR * NEAR)
    index = np.arange(cells).reshape(rows // NEAR, NEAR, cols // NEAR, NEAR).transpose(1, 3, 0, 2)
    order = one_hot(index)

    def kernel(order, observed, baseline, cotangent, sent, diff_rows, held, sems):
        copies = [
            pltpu.make_async_copy(ref, held.at[i], sems.at[i])
            for i, ref in enumerate((observed, baseline, cotangent))
        ]
        for copy in copies:
            copy.start()
        for copy in copies:
            copy.wait()
        mine = lax.axis_index("path")
        mix = (mine.astype(F32) + 0.5) / points
        base = held[1].astype(F32)
        diff = held[0].astype(F32) - base
        field = (base + mix * diff).astype(BF16)
        for i, values in enumerate((field, held[2])):
            moved = jnp.dot(order[...], values, preferred_element_type=F32)
            sent[:, i * part : (i + 1) * part, :] = moved.reshape(NEAR * NEAR, part, depth).astype(BF16)
        half = pl.ds(pl.multiple_of(mine * (cells // points), cells // points), cells // points)
        own = held[1, half, :].astype(F32)
        diff_rows[...] = (held[0, half, :].astype(F32) - own) * (1 / points)

    return call(
        kernel,
        [((NEAR * NEAR, 2 * part, depth), BF16), ((cells // points, depth), F32)],
        [pltpu.VMEM((3, cells, depth), BF16), pltpu.SemaphoreType.DMA((3,))],
        "pack_classes",
        8,
        order,
        *(x.reshape(cells, depth) for x in (observed, baseline, cotangent)),
        specs=[VMEM, ANY, ANY, ANY],
    )


def join_weights(halves):
    points = len(halves[0])
    taps, width, depth = halves[0][0].shape
    side = math.isqrt(taps)

    def kernel(*refs):
        parts, wholes, sems = refs[: 2 * points], refs[2 * points : 2 * points + 2], refs[-1]
        mine = lax.axis_index("path")
        copies = []
        for k in range(2 * points):
            owner = lax.rem(mine + points - k % points, points)
            span = pl.ds(pl.multiple_of(owner * width, width), width)
            for col in range(side):
                copies.append(
                    pltpu.make_async_copy(
                        parts[k].at[:, col], wholes[k // points].at[col, :, span, :], sems.at[k, col]
                    )
                )
        for copy in copies:
            copy.start()
        for copy in copies:
            copy.wait()

    shape = (side, side, width * points, depth)
    args = [x.reshape(side, side, width, depth) for parts in halves for x in parts]
    return call(
        kernel,
        [(shape, BF16)] * 2,
        [pltpu.SemaphoreType.DMA((2 * points, side))],
        "join_weights",
        16,
        *args,
        specs=[ANY] * len(args),
    )


def adjoint_of_class(got, first, first_bias, second, second_bias, sizes):
    group_lon, group_lat, row_part, col_part = sizes
    points = lax.axis_size("path")
    depth = got.shape[-1]
    rows, cols = group_lon * row_part, group_lat * col_part
    cells, part = rows * cols, row_part * col_part
    span = row_part // points
    index = np.arange(cells).reshape(group_lon, group_lat, row_part, col_part).transpose(1, 3, 0, 2)
    order = one_hot(index)

    def kernel(order, got, first, first_bias, second, second_bias, kept, sent, edged, taps, slope, grad, laned):
        def spread(values, step):
            edged[:, EDGE : EDGE + rows, :] = values.reshape(cols, rows, depth)
            for i in range(3):
                start = EDGE + (i - 1) * step
                taps[:, i * depth : (i + 1) * depth] = (
                    edged[:, start : start + rows, :].reshape(cells, depth).astype(BF16)
                )

        def both_sides(weigh, step):
            shift = step * rows
            fill = jnp.zeros((shift, depth), F32)
            after = weigh(taps[shift:, :], 2)
            before = weigh(taps[: cells - shift, :], 0)
            return (
                weigh(taps[...], 1)
                + jnp.concatenate([after, fill], axis=0)
                + jnp.concatenate([fill, before], axis=0)
            )

        def forward(weights, step):
            def weigh(values, col):
                return jnp.dot(values, weights[col].reshape(3 * depth, depth), preferred_element_type=F32)

            return both_sides(weigh, step)

        def backward(weights, step):
            def weigh(values, col):
                total = None
                for i in range(3):
                    term = lax.dot_general(
                        values[:, i * depth : (i + 1) * depth],
                        weights[2 - col, 2 - i],
                        (((1,), (1,)), ((), ())),
                        preferred_element_type=F32,
                    )
                    total = term if total is None else total + term
                return total

            return both_sides(weigh, step)

        edged[:, :EDGE, :] = jnp.zeros((cols, EDGE, depth), F32)
        edged[:, EDGE + rows :, :] = jnp.zeros((cols, EDGE, depth), F32)
        field, upstream = (
            jnp.dot(order[...], got[:, i * part : (i + 1) * part, :].reshape(cells, depth), preferred_element_type=F32)
            for i in range(2)
        )
        spread(field, 1)
        act, slope[...] = gelu_and_slope(forward(first, 1) + first_bias[...])
        spread(field + act, FAR // NEAR)
        second_pre = forward(second, FAR // NEAR) + second_bias[...]
        spread(gelu_and_slope(second_pre)[1] * upstream, FAR // NEAR)
        hidden_adj = upstream + backward(second, FAR // NEAR)
        grad[...] = hidden_adj
        spread(slope[...] * hidden_adj, 1)
        grad[...] += backward(first, 1)
        for b in range(depth // LANES):
            laned[b] = grad[:, b * LANES : (b + 1) * LANES].reshape(cols, rows, LANES)
        mine = lax.axis_index("path")
        for k in range(points):
            owner = lax.rem(mine + k, points)
            for i in range(span):
                target = kept if k == 0 else sent.at[k - 1]
                place = slice(i * (cells // row_part), (i + 1) * (cells // row_part))
                for b in range(depth // LANES):
                    rows_of = laned[b, :, pl.ds(owner * span + i, group_lon, stride=row_part), :]
                    target[place, b * LANES : (b + 1) * LANES] = rows_of.reshape(-1, LANES)

    share = cells // points
    return call(
        kernel,
        [((share, depth), F32), ((points - 1, share, depth), F32)],
        [
            pltpu.VMEM((cols, rows + 2 * EDGE, depth), F32),
            pltpu.VMEM((cells, 3 * depth), BF16),
            pltpu.VMEM((cells, depth), F32),
            pltpu.VMEM((cells, depth), F32),
            pltpu.VMEM((depth // LANES, cols, rows, LANES), F32),
        ],
        "adjoint_of_class",
        24,
        order,
        got,
        first,
        first_bias.reshape(1, depth),
        second,
        second_bias.reshape(1, depth),
    )


def total_for_homes(kept, others, sizes):
    group_lon, group_lat, row_part, col_part = sizes
    share, depth = kept.shape
    span = row_part // lax.axis_size("path")
    part = span * col_part
    index = np.arange(share).reshape(span, group_lat, col_part, group_lon).transpose(3, 1, 0, 2)

    def kernel(order, kept, *refs):
        others, sent = refs[:-1], refs[-1]
        total = kept[...]
        for other in others:
            total = total + other[...]
        moved = jnp.dot(order[...], total.astype(BF16), preferred_element_type=F32)
        sent[...] = moved.reshape(share // part, part, depth).astype(BF16)

    return call(kernel, [((share // part, part, depth), BF16)], [], "total_for_homes", 4, one_hot(index), kept, *others)[0]


def attribution_rows(home, diff_rows, rows, cols):
    depth = home.shape[-1]
    cells = rows * cols
    index = np.arange(cells).reshape(NEAR, NEAR, rows // NEAR, cols // NEAR).transpose(2, 0, 3, 1)

    def kernel(order, home, diff_rows, out):
        values = home[...].astype(F32).reshape(cells, depth).astype(BF16)
        moved = jnp.dot(order[...], values, preferred_element_type=F32)
        out[...] = (diff_rows[...] * moved).reshape(rows, cols, depth).astype(BF16)

    return call(kernel, [((rows, cols, depth), BF16)], [], "attribution_rows", 4, one_hot(index), home, diff_rows)[0]


def one_group(observed, baseline, cotangent, first_weight, first_bias, second_weight, second_bias):
    rows, cols, depth = observed.shape
    points = lax.axis_size("path")
    sizes = group_sizes() + (rows // NEAR, cols // NEAR)

    def turned(values, step):
        return lax.ppermute(values, "path", [(i, (i + step) % points) for i in range(points)])

    halves = [[part] + [turned(part, step) for step in range(1, points)] for part in (first_weight, second_weight)]
    sent, diff_rows = pack_classes(observed, baseline, cotangent)
    got = swap(sent)
    first, second = join_weights(halves)
    kept, others = adjoint_of_class(got, first, first_bias, second, second_bias, sizes)
    others = [turned(others[step - 1], step) for step in range(1, points)]
    home = swap(total_for_homes(kept, others, sizes))
    return attribution_rows(home, diff_rows, rows // points, cols)


def several_groups(observed, baseline, cotangent, first_weight, first_bias, second_weight, second_bias):
    rows, cols, depth = observed.shape
    points, point = lax.axis_size("path"), lax.axis_index("path")
    group_lon, group_lat = group_sizes()
    row_part, col_part = rows // NEAR, cols // NEAR
    ring = [(i, (i + 1) % points) for i in range(points)]

    def whole_weight(part):
        held = jnp.zeros((part.shape[0], points) + part.shape[1:], part.dtype)
        for step in range(points):
            held = lax.dynamic_update_slice_in_dim(held, part[:, None], (point - step) % points, 1)
            if step < points - 1:
                part = lax.ppermute(part, "path", ring)
        return held.reshape(held.shape[0], -1, held.shape[3])

    first_full, second_full = whole_weight(first_weight), whole_weight(second_weight)
    diff = observed.astype(jnp.float32) - baseline.astype(jnp.float32)
    mix = (point.astype(jnp.float32) + 0.5) / points
    field = (baseline.astype(jnp.float32) + mix * diff).astype(jnp.bfloat16)
    sent = jnp.stack([to_classes(field), to_classes(cotangent)], axis=1)
    got = swap(sent).reshape(group_lon, group_lat, 2, row_part, col_part, depth)
    got = got.transpose(2, 0, 3, 1, 4, 5).reshape(2, group_lon * row_part, group_lat * col_part, depth)
    field, upstream = got[0], got[1].astype(jnp.float32)

    first_pre = stencil(field, first_full, 1, True) + first_bias
    hidden = (field.astype(jnp.float32) + smooth_act(first_pre)).astype(jnp.bfloat16)
    second_pre = stencil(hidden, second_full, FAR // NEAR, True) + second_bias
    second_adj = act_adjoint(second_pre, upstream).astype(jnp.bfloat16)
    hidden_adj = upstream + stencil(second_adj, second_full, FAR // NEAR, False)
    first_adj = act_adjoint(first_pre, hidden_adj).astype(jnp.bfloat16)
    grad = hidden_adj + stencil(first_adj, first_full, 1, False)

    part = row_part // points
    grad = grad.reshape(group_lon, points, part, group_lat, col_part, depth).transpose(1, 0, 3, 2, 4, 5)
    grad = grad.reshape(points, group_lon * group_lat, part, col_part, depth)
    total = lax.dynamic_index_in_dim(grad, point, 0, keepdims=False)
    for step in range(1, points):
        other = lax.dynamic_index_in_dim(grad, (point + step) % points, 0, keepdims=False)
        total = total + lax.ppermute(other, "path", [(i, (i + step) % points) for i in range(points)])
    home = swap(total.astype(jnp.bfloat16)).reshape(NEAR, NEAR, part, col_part, depth)
    home = home.transpose(2, 0, 3, 1, 4).reshape(rows // points, cols, depth).astype(jnp.float32)
    diff_rows = lax.dynamic_slice_in_dim(diff, point * (rows // points), rows // points, 0)
    return (diff_rows * home / points).astype(jnp.bfloat16)


def shards(*args):
    if group_sizes() == (lax.axis_size("lon"), lax.axis_size("lat")):
        return one_group(*args)
    return several_groups(*args)


def solution(mesh):
    placed = (
        P("lon", "lat", None),
        P("lon", "lat", None),
        P("lon", "lat", None),
        P(None, "path", None),
        P(),
        P(None, "path", None),
        P(),
    )
    return jax.shard_map(
        shards,
        mesh=mesh,
        in_specs=placed,
        out_specs=P(("lon", "path"), "lat", None),
        check_vma=False,
    )
```

```python
import math

import jax
import jax.numpy as jnp
from jax import lax
from jax.experimental import pallas as pl
from jax.experimental.pallas import tpu as pltpu
from jax.sharding import PartitionSpec as P

NEAR = 4
FAR = 16
EDGE = 8
LANES = 128
F32, BF16 = jnp.float32, jnp.bfloat16
VMEM = pl.BlockSpec(memory_space=pltpu.VMEM)
HBM = pl.BlockSpec(memory_space=pltpu.HBM)

def smooth_act(value):
    return jax.nn.gelu(value, approximate=True)


def act_adjoint(pre_value, upstream):
    unused, pullback = jax.vjp(smooth_act, pre_value)
    return pullback(upstream)[0]


def group_sizes():
    lat = math.gcd(lax.axis_size("lat"), NEAR * NEAR)
    return NEAR * NEAR // lat, lat


def swap(chunks):
    group_lon, group_lat = group_sizes()
    lon, lat = lax.axis_size("lon"), lax.axis_size("lat")
    if (lon, lat) == (group_lon, group_lat):
        return lax.all_to_all(chunks, ("lon", "lat"), 0, 0, tiled=True)
    chunks = chunks.reshape((group_lon, group_lat) + chunks.shape[1:])
    for axis, dim, size in (("lon", 0, group_lon), ("lat", 1, group_lat)):
        count = lax.axis_size(axis)
        groups = [list(range(i, i + size)) for i in range(0, count, size)]
        chunks = lax.all_to_all(chunks, axis, dim, dim, tiled=True, axis_index_groups=groups)
    return chunks.reshape((group_lon * group_lat,) + chunks.shape[2:])


def to_classes(cells):
    rows, cols, depth = cells.shape
    cells = cells.reshape(rows // NEAR, NEAR, cols // NEAR, NEAR, depth).transpose(1, 3, 0, 2, 4)
    return cells.reshape(NEAR * NEAR, rows // NEAR, cols // NEAR, depth)


def padded(cells, width):
    for axis, dim, step in zip(("lon", "lat"), (0, 1), group_sizes()):
        count = lax.axis_size(axis)
        head = lax.slice_in_dim(cells, 0, width, axis=dim)
        tail = lax.slice_in_dim(cells, cells.shape[dim] - width, cells.shape[dim], axis=dim)
        if count == step:
            before, after = jnp.zeros_like(tail), jnp.zeros_like(head)
        else:
            before = lax.ppermute(tail, axis, [(i, i + step) for i in range(count - step)])
            after = lax.ppermute(head, axis, [(i + step, i) for i in range(count - step)])
        cells = jnp.concatenate([before, cells, after], axis=dim)
    return cells


def stencil(cells, weights, step, forward):
    rows, cols, depth = cells.shape
    around = padded(cells, step)
    total = jnp.zeros((rows, cols, depth), jnp.float32)
    for tap in range(9):
        sign = step if forward else -step
        row, col = step + (tap // 3 - 1) * sign, step + (tap % 3 - 1) * sign
        window = around[row : row + rows, col : col + cols]
        dims = (((2,), (0 if forward else 1,)), ((), ()))
        total = total + lax.dot_general(window, weights[tap], dims, preferred_element_type=jnp.float32)
    return total


def ordering(dims, axes):
    cells = math.prod(dims)
    place = lax.broadcasted_iota(jnp.int32, (cells, 1), 0)
    source, stride = jnp.zeros((cells, 1), jnp.int32), 1
    for axis in reversed(axes):
        source += lax.rem(lax.div(place, jnp.int32(stride)), jnp.int32(dims[axis])) * math.prod(dims[axis + 1 :])
        stride *= dims[axis]
    return (lax.broadcasted_iota(jnp.int32, (cells, cells), 1) == source).astype(F32).astype(BF16)


def gelu_and_slope(value):
    scale, cubic = math.sqrt(2 / math.pi), 0.044715
    square = value * value
    bent = jnp.tanh(scale * value * (1 + cubic * square))
    half = 0.5 * (1 + bent)
    return value * half, half + 0.5 * value * (1 - bent * bent) * (scale * (1 + 3 * cubic * square))


def call(kernel, outs, scratch, name, megabytes, *args, specs=None, flops=0):
    specs = specs or [VMEM] * len(args)
    args = [pltpu.with_memory_space_constraint(x, spec.memory_space) for x, spec in zip(args, specs)]
    return pl.pallas_call(
        kernel,
        out_shape=[pltpu.VMEM(shape, dtype) for shape, dtype in outs],
        in_specs=specs,
        out_specs=[VMEM] * len(outs),
        scratch_shapes=scratch,
        compiler_params=pltpu.CompilerParams(vmem_limit_bytes=megabytes << 20),
        cost_estimate=pl.CostEstimate(flops=flops, bytes_accessed=sum(x.size * x.dtype.itemsize for x in args), transcendentals=0),
        name=name,
    )(*args)


def pack_classes(observed, baseline, cotangent):
    rows, cols, depth = observed.shape
    points, point = lax.axis_size("path"), lax.axis_index("path")
    cells, part = rows * cols, rows * cols // (NEAR * NEAR)

    def kernel(observed, baseline, cotangent, sent, diff_rows, held, sems):
        copies = [
            pltpu.make_async_copy(ref, held.at[i], sems.at[i])
            for i, ref in enumerate((observed, baseline, cotangent))
        ]
        for copy in copies:
            copy.start()
        order = ordering((rows // NEAR, NEAR, cols // NEAR, NEAR), (1, 3, 0, 2))
        for copy in copies:
            copy.wait()
        mine = lax.axis_index("path")
        mix = (mine.astype(F32) + 0.5) / points
        base = held[1].astype(F32)
        diff = held[0].astype(F32) - base
        field = (base + mix * diff).astype(BF16)
        for i, values in enumerate((field, held[2])):
            moved = jnp.dot(order, values, preferred_element_type=F32)
            sent[:, i * part : (i + 1) * part, :] = moved.reshape(NEAR * NEAR, part, depth).astype(BF16)
        half = pl.ds(pl.multiple_of(mine * (cells // points), cells // points), cells // points)
        own = held[1, half, :].astype(F32)
        diff_rows[...] = (held[0, half, :].astype(F32) - own) * (1 / points)

    return call(
        kernel,
        [((NEAR * NEAR, 2 * part, depth), BF16), ((cells // points, depth), F32)],
        [pltpu.VMEM((3, cells, depth), BF16), pltpu.SemaphoreType.DMA((3,))],
        "pack_classes",
        8,
        *(x.reshape(cells, depth) for x in (observed, baseline, cotangent)),
        specs=[HBM] * 3,
        flops=4 * 10**9,
    )


def adjoint_of_class(got, first_halves, first_bias, second_halves, second_bias, sizes):
    group_lon, group_lat, row_part, col_part = sizes
    points = lax.axis_size("path")
    depth = got.shape[-1]
    rows, cols = group_lon * row_part, group_lat * col_part
    cells, part = rows * cols, row_part * col_part
    span = row_part // points

    def kernel(got, first_bias, second_bias, *refs):
        mine = lax.axis_index("path")
        for owner in range(points):
            inputs = [(owner - k) % points for k in range(points)]
            first, second = ([refs[j * points + k] for k in inputs] for j in range(2))
            pl.when(mine == owner)(lambda: run(owner, got, first, first_bias, second, second_bias, *refs[2 * points :]))

    def run(mine, got, first, first_bias, second, second_bias, kept, sent, edged, taps, slope, grad, laned):
        order = ordering((group_lon, group_lat, row_part, col_part), (1, 3, 0, 2))

        def tap_weight(parts, row, col):
            return jnp.concatenate([part[row, col] for part in parts], axis=0)

        def spread(values, step):
            edged[:, EDGE : EDGE + rows, :] = values.reshape(cols, rows, depth)
            for i in range(3):
                start = EDGE + (i - 1) * step
                taps[:, i * depth : (i + 1) * depth] = (
                    edged[:, start : start + rows, :].reshape(cells, depth).astype(BF16)
                )

        def both_sides(weigh, step):
            shift = step * rows
            fill = jnp.zeros((shift, depth), F32)
            same = weigh(taps[...], 1)
            after = weigh(taps[shift:, :], 2)
            before = weigh(taps[: cells - shift, :], 0)
            return same + jnp.concatenate([after, fill], axis=0) + jnp.concatenate([fill, before], axis=0)

        def forward(weights, step):
            def weigh(values, col):
                column = jnp.concatenate([tap_weight(weights, i, col) for i in range(3)], axis=0)
                return jnp.dot(values, column, preferred_element_type=F32)

            return both_sides(weigh, step)

        def backward(weights, step):
            def weigh(values, col):
                total = None
                for i in range(3):
                    term = lax.dot_general(
                        values[:, i * depth : (i + 1) * depth],
                        tap_weight(weights, 2 - i, 2 - col),
                        (((1,), (1,)), ((), ())),
                        preferred_element_type=F32,
                    )
                    total = term if total is None else total + term
                return total

            return both_sides(weigh, step)

        edged[:, :EDGE, :] = jnp.zeros((cols, EDGE, depth), F32)
        edged[:, EDGE + rows :, :] = jnp.zeros((cols, EDGE, depth), F32)
        field, upstream = (
            jnp.dot(order, got[:, i * part : (i + 1) * part, :].reshape(cells, depth), preferred_element_type=F32)
            for i in range(2)
        )
        spread(field, 1)
        act, slope[...] = gelu_and_slope(forward(first, 1) + first_bias[...].reshape(1, depth))
        spread(field + act, FAR // NEAR)
        second_pre = forward(second, FAR // NEAR) + second_bias[...].reshape(1, depth)
        spread(gelu_and_slope(second_pre)[1] * upstream, FAR // NEAR)
        hidden_adj = upstream + backward(second, FAR // NEAR)
        grad[...] = hidden_adj
        spread(slope[...] * hidden_adj, 1)
        grad[...] += backward(first, 1)
        for b in range(depth // LANES):
            laned[b] = grad[:, b * LANES : (b + 1) * LANES].reshape(cols, rows, LANES)
        for k in range(points):
            owner = (mine + k) % points
            for i in range(span):
                target = kept if k == 0 else sent.at[k - 1]
                place = slice(i * (cells // row_part), (i + 1) * (cells // row_part))
                for b in range(depth // LANES):
                    rows_of = laned[b, :, pl.ds(owner * span + i, group_lon, stride=row_part), :]
                    target[place, b * LANES : (b + 1) * LANES] = rows_of.reshape(-1, LANES)

    share = cells // points
    return call(
        kernel,
        [((share, depth), F32), ((points - 1, share, depth), F32)],
        [
            pltpu.VMEM((cols, rows + 2 * EDGE, depth), F32),
            pltpu.VMEM((cells, 3 * depth), BF16),
            pltpu.VMEM((cells, depth), F32),
            pltpu.VMEM((cells, depth), F32),
            pltpu.VMEM((depth // LANES, cols, rows, LANES), F32),
        ],
        "adjoint_of_class",
        24,
        got,
        first_bias,
        second_bias,
        *first_halves,
        *second_halves,
    )


def total_for_homes(kept, others, sizes):
    group_lon, group_lat, row_part, col_part = sizes
    share, depth = kept.shape
    span = row_part // lax.axis_size("path")
    part = span * col_part

    def kernel(kept, *refs):
        order = ordering((span, group_lat, col_part, group_lon), (3, 1, 0, 2))
        others, sent = refs[:-1], refs[-1]
        total = kept[...]
        for other in others:
            total = total + other[...]
        moved = jnp.dot(order, total.astype(BF16), preferred_element_type=F32)
        sent[...] = moved.reshape(share // part, part, depth).astype(BF16)

    return call(kernel, [((share // part, part, depth), BF16)], [], "total_for_homes", 4, kept, *others)[0]


def attribution_rows(home, diff_rows, rows, cols):
    depth = home.shape[-1]
    cells = rows * cols

    def kernel(home, diff_rows, out):
        order = ordering((NEAR, NEAR, rows // NEAR, cols // NEAR), (2, 0, 3, 1))
        values = home[...].astype(F32).reshape(cells, depth).astype(BF16)
        moved = jnp.dot(order, values, preferred_element_type=F32)
        out[...] = (diff_rows[...] * moved).reshape(rows, cols, depth).astype(BF16)

    return call(kernel, [((rows, cols, depth), BF16)], [], "attribution_rows", 4, home, diff_rows)[0]


def one_group(observed, baseline, cotangent, first_weight, first_bias, second_weight, second_bias):
    rows, cols, depth = observed.shape
    points = lax.axis_size("path")
    sizes = group_sizes() + (rows // NEAR, cols // NEAR)

    def turned(values, step):
        return lax.ppermute(values, "path", [(i, (i + step) % points) for i in range(points)])

    side = math.isqrt(first_weight.shape[0])
    halves = [
        [x.reshape((side, side) + x.shape[1:]) for x in [part] + [turned(part, step) for step in range(1, points)]]
        for part in (first_weight, second_weight)
    ]
    sent, diff_rows = pack_classes(observed, baseline, cotangent)
    got = swap(sent)
    kept, others = adjoint_of_class(got, halves[0], first_bias, halves[1], second_bias, sizes)
    others = [turned(others[step - 1], step) for step in range(1, points)]
    home = swap(total_for_homes(kept, others, sizes))
    return attribution_rows(home, diff_rows, rows // points, cols)


def several_groups(observed, baseline, cotangent, first_weight, first_bias, second_weight, second_bias):
    rows, cols, depth = observed.shape
    points, point = lax.axis_size("path"), lax.axis_index("path")
    group_lon, group_lat = group_sizes()
    row_part, col_part = rows // NEAR, cols // NEAR
    ring = [(i, (i + 1) % points) for i in range(points)]

    def whole_weight(part):
        held = jnp.zeros((part.shape[0], points) + part.shape[1:], part.dtype)
        for step in range(points):
            held = lax.dynamic_update_slice_in_dim(held, part[:, None], (point - step) % points, 1)
            if step < points - 1:
                part = lax.ppermute(part, "path", ring)
        return held.reshape(held.shape[0], -1, held.shape[3])

    first_full, second_full = whole_weight(first_weight), whole_weight(second_weight)
    diff = observed.astype(jnp.float32) - baseline.astype(jnp.float32)
    mix = (point.astype(jnp.float32) + 0.5) / points
    field = (baseline.astype(jnp.float32) + mix * diff).astype(jnp.bfloat16)
    sent = jnp.stack([to_classes(field), to_classes(cotangent)], axis=1)
    got = swap(sent).reshape(group_lon, group_lat, 2, row_part, col_part, depth)
    got = got.transpose(2, 0, 3, 1, 4, 5).reshape(2, group_lon * row_part, group_lat * col_part, depth)
    field, upstream = got[0], got[1].astype(jnp.float32)

    first_pre = stencil(field, first_full, 1, True) + first_bias
    hidden = (field.astype(jnp.float32) + smooth_act(first_pre)).astype(jnp.bfloat16)
    second_pre = stencil(hidden, second_full, FAR // NEAR, True) + second_bias
    second_adj = act_adjoint(second_pre, upstream).astype(jnp.bfloat16)
    hidden_adj = upstream + stencil(second_adj, second_full, FAR // NEAR, False)
    first_adj = act_adjoint(first_pre, hidden_adj).astype(jnp.bfloat16)
    grad = hidden_adj + stencil(first_adj, first_full, 1, False)

    part = row_part // points
    grad = grad.reshape(group_lon, points, part, group_lat, col_part, depth).transpose(1, 0, 3, 2, 4, 5)
    grad = grad.reshape(points, group_lon * group_lat, part, col_part, depth)
    total = lax.dynamic_index_in_dim(grad, point, 0, keepdims=False)
    for step in range(1, points):
        other = lax.dynamic_index_in_dim(grad, (point + step) % points, 0, keepdims=False)
        total = total + lax.ppermute(other, "path", [(i, (i + step) % points) for i in range(points)])
    home = swap(total.astype(jnp.bfloat16)).reshape(NEAR, NEAR, part, col_part, depth)
    home = home.transpose(2, 0, 3, 1, 4).reshape(rows // points, cols, depth).astype(jnp.float32)
    diff_rows = lax.dynamic_slice_in_dim(diff, point * (rows // points), rows // points, 0)
    return (diff_rows * home / points).astype(jnp.bfloat16)


def shards(*args):
    if group_sizes() == (lax.axis_size("lon"), lax.axis_size("lat")):
        return one_group(*args)
    return several_groups(*args)


def solution(mesh):
    placed = (
        P("lon", "lat", None),
        P("lon", "lat", None),
        P("lon", "lat", None),
        P(None, "path", None),
        P(),
        P(None, "path", None),
        P(),
    )
    return jax.shard_map(
        shards,
        mesh=mesh,
        in_specs=placed,
        out_specs=P(("lon", "path"), "lat", None),
        check_vma=False,
    )
```

```python
import functools
import math

import jax
import jax.numpy as jnp
from jax import lax
from jax.experimental import pallas as pl
from jax.experimental.pallas import tpu as pltpu
from jax.sharding import PartitionSpec as P

NEAR = 4
FAR = 16
EDGE = 8
LANES = 128
F32, BF16 = jnp.float32, jnp.bfloat16
VMEM = pl.BlockSpec(memory_space=pltpu.VMEM)
HBM = pl.BlockSpec(memory_space=pltpu.HBM)

def smooth_act(value):
    return jax.nn.gelu(value, approximate=True)


def act_adjoint(pre_value, upstream):
    unused, pullback = jax.vjp(smooth_act, pre_value)
    return pullback(upstream)[0]


def group_sizes():
    lat = math.gcd(lax.axis_size("lat"), NEAR * NEAR)
    return NEAR * NEAR // lat, lat


def swap(chunks):
    group_lon, group_lat = group_sizes()
    lon, lat = lax.axis_size("lon"), lax.axis_size("lat")
    if (lon, lat) == (group_lon, group_lat):
        return lax.all_to_all(chunks, ("lon", "lat"), 0, 0, tiled=True)
    chunks = chunks.reshape((group_lon, group_lat) + chunks.shape[1:])
    for axis, dim, size in (("lon", 0, group_lon), ("lat", 1, group_lat)):
        count = lax.axis_size(axis)
        groups = [list(range(i, i + size)) for i in range(0, count, size)]
        chunks = lax.all_to_all(chunks, axis, dim, dim, tiled=True, axis_index_groups=groups)
    return chunks.reshape((group_lon * group_lat,) + chunks.shape[2:])


def to_classes(cells):
    rows, cols, depth = cells.shape
    cells = cells.reshape(rows // NEAR, NEAR, cols // NEAR, NEAR, depth).transpose(1, 3, 0, 2, 4)
    return cells.reshape(NEAR * NEAR, rows // NEAR, cols // NEAR, depth)


def padded(cells, width):
    for axis, dim, step in zip(("lon", "lat"), (0, 1), group_sizes()):
        count = lax.axis_size(axis)
        head = lax.slice_in_dim(cells, 0, width, axis=dim)
        tail = lax.slice_in_dim(cells, cells.shape[dim] - width, cells.shape[dim], axis=dim)
        if count == step:
            before, after = jnp.zeros_like(tail), jnp.zeros_like(head)
        else:
            before = lax.ppermute(tail, axis, [(i, i + step) for i in range(count - step)])
            after = lax.ppermute(head, axis, [(i + step, i) for i in range(count - step)])
        cells = jnp.concatenate([before, cells, after], axis=dim)
    return cells


def stencil(cells, weights, step, forward):
    rows, cols, depth = cells.shape
    around = padded(cells, step)
    total = jnp.zeros((rows, cols, depth), jnp.float32)
    for tap in range(9):
        sign = step if forward else -step
        row, col = step + (tap // 3 - 1) * sign, step + (tap % 3 - 1) * sign
        window = around[row : row + rows, col : col + cols]
        dims = (((2,), (0 if forward else 1,)), ((), ()))
        total = total + lax.dot_general(window, weights[tap], dims, preferred_element_type=jnp.float32)
    return total


def ordering(dims, axes):
    cells = math.prod(dims)
    place = lax.broadcasted_iota(jnp.int32, (cells, 1), 0)
    source, stride = jnp.zeros((cells, 1), jnp.int32), 1
    for axis in reversed(axes):
        source += lax.rem(lax.div(place, jnp.int32(stride)), jnp.int32(dims[axis])) * math.prod(dims[axis + 1 :])
        stride *= dims[axis]
    return (lax.broadcasted_iota(jnp.int32, (cells, cells), 1) == source).astype(F32).astype(BF16)


def gelu_and_slope(value):
    scale, cubic = math.sqrt(2 / math.pi), 0.044715
    square = value * value
    bent = jnp.tanh(scale * value * (1 + cubic * square))
    half = 0.5 * (1 + bent)
    return value * half, half + 0.5 * value * (1 - bent * bent) * (scale * (1 + 3 * cubic * square))


def call(kernel, outs, scratch, name, megabytes, *args, specs=None, flops=0):
    specs = specs or [VMEM] * len(args)
    args = [pltpu.with_memory_space_constraint(x, spec.memory_space) for x, spec in zip(args, specs)]
    return pl.pallas_call(
        kernel,
        out_shape=[pltpu.VMEM(shape, dtype) for shape, dtype in outs],
        in_specs=specs,
        out_specs=[VMEM] * len(outs),
        scratch_shapes=scratch,
        compiler_params=pltpu.CompilerParams(vmem_limit_bytes=megabytes << 20),
        cost_estimate=pl.CostEstimate(flops=flops, bytes_accessed=sum(x.size * x.dtype.itemsize for x in args), transcendentals=0),
        name=name,
    )(*args)


def pack_classes(observed, baseline, cotangent):
    rows, cols, depth = observed.shape
    points, point = lax.axis_size("path"), lax.axis_index("path")
    cells, part = rows * cols, rows * cols // (NEAR * NEAR)

    def kernel(observed, baseline, cotangent, sent, diff_rows, held, sems):
        copies = [
            pltpu.make_async_copy(ref, held.at[i], sems.at[i])
            for i, ref in enumerate((observed, baseline, cotangent))
        ]
        for copy in copies:
            copy.start()
        order = ordering((rows // NEAR, NEAR, cols // NEAR, NEAR), (1, 3, 0, 2))
        for copy in copies:
            copy.wait()
        mine = lax.axis_index("path")
        mix = (mine.astype(F32) + 0.5) / points
        base = held[1].astype(F32)
        diff = held[0].astype(F32) - base
        field = (base + mix * diff).astype(BF16)
        moved = jnp.dot(order, field, preferred_element_type=F32)
        sent[:, :part, :] = moved.reshape(NEAR * NEAR, part, depth).astype(BF16)
        moved = jnp.dot(order, held[2], preferred_element_type=F32).reshape(NEAR * NEAR, points, part // points, depth)
        own = moved[:, 0]
        for k in range(1, points):
            own = jnp.where(mine == k, moved[:, k], own)
        sent[:, part:, :] = own.astype(BF16)
        half = pl.ds(pl.multiple_of(mine * (cells // points), cells // points), cells // points)
        own = held[1, half, :].astype(F32)
        diff_rows[...] = (held[0, half, :].astype(F32) - own) * (1 / points)

    return call(
        kernel,
        [((NEAR * NEAR, part + part // points, depth), BF16), ((cells // points, depth), F32)],
        [pltpu.VMEM((3, cells, depth), BF16), pltpu.SemaphoreType.DMA((3,))],
        "pack_classes",
        8,
        *(x.reshape(cells, depth) for x in (observed, baseline, cotangent)),
        specs=[HBM] * 3,
        flops=4 * 10**9,
    )


def class_tools(sizes, depth, edged):
    group_lon, group_lat, row_part, col_part = sizes
    rows, cols = group_lon * row_part, group_lat * col_part
    cells = rows * cols

    def spread(values, step, at, target):
        span = slice(at, at + values.shape[1])
        edged[:, EDGE : EDGE + rows, span] = values.reshape(cols, rows, -1)
        for i in range(3):
            start = EDGE + (i - 1) * step
            shifted = edged[:, start : start + rows, span].reshape(cells, -1)
            target[:, i * depth + at : i * depth + at + values.shape[1]] = shifted.astype(BF16)

    def stencil_part(source, weights, step, at, end, forward):
        def weigh(values, col):
            if forward:
                blocks = [part[i, col, :, at:end] for i in range(3) for part in weights]
                return jnp.dot(values, jnp.concatenate(blocks, axis=0), preferred_element_type=F32)
            taps_of = [jnp.concatenate([part[2 - i, 2 - col] for part in weights], axis=0)[at:end] for i in range(3)]
            return lax.dot_general(
                values, jnp.concatenate(taps_of, axis=1), (((1,), (1,)), ((), ())), preferred_element_type=F32
            )

        shift = step * rows
        fill = jnp.zeros((shift, end - at), F32)
        same = weigh(source[...], 1)
        after = weigh(source[shift:, :], 2)
        before = weigh(source[: cells - shift, :], 0)
        return same + jnp.concatenate([after, fill], axis=0) + jnp.concatenate([fill, before], axis=0)

    edged[:, :EDGE, :] = jnp.zeros((cols, EDGE, depth), F32)
    edged[:, EDGE + rows :, :] = jnp.zeros((cols, EDGE, depth), F32)
    return spread, stencil_part


def by_place(points, run, *halves):
    for place in range(points):
        owners = [(place - k) % points for k in range(points)]
        lists = [[parts[k] for k in owners] for parts in halves]
        pl.when(lax.axis_index("path") == place)(functools.partial(run, place, *lists))


def channel_parts(depth):
    return [(at, min(at + 2 * LANES, depth)) for at in range(0, depth, 2 * LANES)]


def slopes_of_class(got, first_halves, first_bias, second_halves, second_bias, sizes):
    group_lon, group_lat, row_part, col_part = sizes
    points, depth = len(first_halves), got.shape[-1]
    rows, cols, part = group_lon * row_part, group_lat * col_part, row_part * col_part
    cells = rows * cols

    def kernel(got, first_bias, second_bias, *refs):
        first_slope, second_slope, edged, near_taps, far_taps = refs[2 * points :]

        def run(place, first, second):
            spread, stencil_part = class_tools(sizes, depth, edged)
            order = ordering((group_lon, group_lat, row_part, col_part), (1, 3, 0, 2))
            field = jnp.dot(order, got[:, :part, :].reshape(cells, depth), preferred_element_type=F32)
            spread(field, 1, 0, near_taps)
            for at, end in channel_parts(depth):
                pre = stencil_part(near_taps, first, 1, at, end, True) + first_bias[at:end].reshape(1, -1)
                act, first_slope[:, at:end] = gelu_and_slope(pre)
                spread(field[:, at:end] + act, FAR // NEAR, at, far_taps)
            for at, end in channel_parts(depth):
                pre = stencil_part(far_taps, second, FAR // NEAR, at, end, True) + second_bias[at:end].reshape(1, -1)
                second_slope[:, at:end] = gelu_and_slope(pre)[1]

        by_place(points, run, refs[:points], refs[points : 2 * points])

    return call(
        kernel,
        [((cells, depth), F32)] * 2,
        [pltpu.VMEM((cols, rows + 2 * EDGE, depth), F32)] + [pltpu.VMEM((cells, 3 * depth), BF16)] * 2,
        "slopes_of_class",
        16,
        got,
        first_bias,
        second_bias,
        *first_halves,
        *second_halves,
    )


def adjoint_of_class(cotangents, first_slope, second_slope, first_halves, second_halves, sizes):
    group_lon, group_lat, row_part, col_part = sizes
    points, depth = len(first_halves), first_slope.shape[-1]
    rows, cols = group_lon * row_part, group_lat * col_part
    cells, span = rows * cols, row_part // points

    def kernel(first_slope, second_slope, *refs):
        kept, sent, edged, near_taps, far_taps, grad, laned = refs[3 * points :]

        def run(place, cotangent, first, second):
            spread, stencil_part = class_tools(sizes, depth, edged)
            order = ordering((group_lon, group_lat, row_part, col_part), (1, 3, 0, 2))
            upstream = jnp.concatenate([share[...].astype(F32) for share in cotangent], axis=1)
            upstream = jnp.dot(order, upstream.reshape(cells, depth).astype(BF16), preferred_element_type=F32)
            spread(second_slope[...] * upstream, FAR // NEAR, 0, far_taps)
            for at, end in channel_parts(depth):
                hidden_adj = upstream[:, at:end] + stencil_part(far_taps, second, FAR // NEAR, at, end, False)
                grad[:, at:end] = hidden_adj
                spread(first_slope[:, at:end] * hidden_adj, 1, at, near_taps)
            for at, end in channel_parts(depth):
                grad[:, at:end] += stencil_part(near_taps, first, 1, at, end, False)
                for b in range(at // LANES, end // LANES):
                    laned[b] = grad[:, b * LANES : (b + 1) * LANES].reshape(cols, rows, LANES)
            for k in range(points):
                owner = (place + k) % points
                target = kept if k == 0 else sent.at[k - 1]
                for i in range(span):
                    here = slice(i * (cells // row_part), (i + 1) * (cells // row_part))
                    for b in range(depth // LANES):
                        rows_of = laned[b, :, pl.ds(owner * span + i, group_lon, stride=row_part), :]
                        target[here, b * LANES : (b + 1) * LANES] = rows_of.reshape(-1, LANES)

        by_place(points, run, refs[:points], refs[points : 2 * points], refs[2 * points : 3 * points])

    share = cells // points
    return call(
        kernel,
        [((share, depth), F32), ((points - 1, share, depth), F32)],
        [pltpu.VMEM((cols, rows + 2 * EDGE, depth), F32)]
        + [pltpu.VMEM((cells, 3 * depth), BF16)] * 2
        + [pltpu.VMEM((cells, depth), F32), pltpu.VMEM((depth // LANES, cols, rows, LANES), F32)],
        "adjoint_of_class",
        16,
        first_slope,
        second_slope,
        *cotangents,
        *first_halves,
        *second_halves,
    )


def total_for_homes(kept, others, sizes):
    group_lon, group_lat, row_part, col_part = sizes
    share, depth = kept.shape
    span = row_part // lax.axis_size("path")
    part = span * col_part

    def kernel(kept, *refs):
        order = ordering((span, group_lat, col_part, group_lon), (3, 1, 0, 2))
        others, sent = refs[:-1], refs[-1]
        total = kept[...]
        for other in others:
            total = total + other[...]
        moved = jnp.dot(order, total.astype(BF16), preferred_element_type=F32)
        sent[...] = moved.reshape(share // part, part, depth).astype(BF16)

    return call(kernel, [((share // part, part, depth), BF16)], [], "total_for_homes", 4, kept, *others)[0]


def attribution_rows(home, diff_rows, rows, cols):
    depth = home.shape[-1]
    cells = rows * cols

    def kernel(home, diff_rows, out):
        order = ordering((NEAR, NEAR, rows // NEAR, cols // NEAR), (2, 0, 3, 1))
        values = home[...].astype(F32).reshape(cells, depth).astype(BF16)
        moved = jnp.dot(order, values, preferred_element_type=F32)
        out[...] = (diff_rows[...] * moved).reshape(rows, cols, depth).astype(BF16)

    return call(kernel, [((rows, cols, depth), BF16)], [], "attribution_rows", 4, home, diff_rows)[0]


def one_group(observed, baseline, cotangent, first_weight, first_bias, second_weight, second_bias):
    rows, cols, depth = observed.shape
    points = lax.axis_size("path")
    sizes = group_sizes() + (rows // NEAR, cols // NEAR)

    def turned(values, step):
        return lax.ppermute(values, "path", [(i, (i + step) % points) for i in range(points)])

    side = math.isqrt(first_weight.shape[0])
    halves = [
        [x.reshape((side, side) + x.shape[1:]) for x in [part] + [turned(part, step) for step in range(1, points)]]
        for part in (first_weight, second_weight)
    ]
    sent, diff_rows = pack_classes(observed, baseline, cotangent)
    got = swap(sent)
    own = got[:, sizes[2] * sizes[3] :, :]
    cotangents = [own] + [turned(own, step) for step in range(1, points)]
    first_slope, second_slope = slopes_of_class(got, halves[0], first_bias, halves[1], second_bias, sizes)
    kept, others = adjoint_of_class(cotangents, first_slope, second_slope, *halves, sizes)
    others = [turned(others[step - 1], step) for step in range(1, points)]
    home = swap(total_for_homes(kept, others, sizes))
    return attribution_rows(home, diff_rows, rows // points, cols)


def several_groups(observed, baseline, cotangent, first_weight, first_bias, second_weight, second_bias):
    rows, cols, depth = observed.shape
    points, point = lax.axis_size("path"), lax.axis_index("path")
    group_lon, group_lat = group_sizes()
    row_part, col_part = rows // NEAR, cols // NEAR
    ring = [(i, (i + 1) % points) for i in range(points)]

    def whole_weight(part):
        held = jnp.zeros((part.shape[0], points) + part.shape[1:], part.dtype)
        for step in range(points):
            held = lax.dynamic_update_slice_in_dim(held, part[:, None], (point - step) % points, 1)
            if step < points - 1:
                part = lax.ppermute(part, "path", ring)
        return held.reshape(held.shape[0], -1, held.shape[3])

    first_full, second_full = whole_weight(first_weight), whole_weight(second_weight)
    diff = observed.astype(jnp.float32) - baseline.astype(jnp.float32)
    mix = (point.astype(jnp.float32) + 0.5) / points
    field = (baseline.astype(jnp.float32) + mix * diff).astype(jnp.bfloat16)
    sent = jnp.stack([to_classes(field), to_classes(cotangent)], axis=1)
    got = swap(sent).reshape(group_lon, group_lat, 2, row_part, col_part, depth)
    got = got.transpose(2, 0, 3, 1, 4, 5).reshape(2, group_lon * row_part, group_lat * col_part, depth)
    field, upstream = got[0], got[1].astype(jnp.float32)

    first_pre = stencil(field, first_full, 1, True) + first_bias
    hidden = (field.astype(jnp.float32) + smooth_act(first_pre)).astype(jnp.bfloat16)
    second_pre = stencil(hidden, second_full, FAR // NEAR, True) + second_bias
    second_adj = act_adjoint(second_pre, upstream).astype(jnp.bfloat16)
    hidden_adj = upstream + stencil(second_adj, second_full, FAR // NEAR, False)
    first_adj = act_adjoint(first_pre, hidden_adj).astype(jnp.bfloat16)
    grad = hidden_adj + stencil(first_adj, first_full, 1, False)

    part = row_part // points
    grad = grad.reshape(group_lon, points, part, group_lat, col_part, depth).transpose(1, 0, 3, 2, 4, 5)
    grad = grad.reshape(points, group_lon * group_lat, part, col_part, depth)
    total = lax.dynamic_index_in_dim(grad, point, 0, keepdims=False)
    for step in range(1, points):
        other = lax.dynamic_index_in_dim(grad, (point + step) % points, 0, keepdims=False)
        total = total + lax.ppermute(other, "path", [(i, (i + step) % points) for i in range(points)])
    home = swap(total.astype(jnp.bfloat16)).reshape(NEAR, NEAR, part, col_part, depth)
    home = home.transpose(2, 0, 3, 1, 4).reshape(rows // points, cols, depth).astype(jnp.float32)
    diff_rows = lax.dynamic_slice_in_dim(diff, point * (rows // points), rows // points, 0)
    return (diff_rows * home / points).astype(jnp.bfloat16)


def shards(*args):
    if group_sizes() == (lax.axis_size("lon"), lax.axis_size("lat")):
        return one_group(*args)
    return several_groups(*args)


def solution(mesh):
    placed = (
        P("lon", "lat", None),
        P("lon", "lat", None),
        P("lon", "lat", None),
        P(None, "path", None),
        P(),
        P(None, "path", None),
        P(),
    )
    return jax.shard_map(
        shards,
        mesh=mesh,
        in_specs=placed,
        out_specs=P(("lon", "path"), "lat", None),
        check_vma=False,
    )
```

```python
import functools
import math

import jax
import jax.numpy as jnp
from jax import lax
from jax.experimental import pallas as pl
from jax.experimental.pallas import tpu as pltpu
from jax.sharding import PartitionSpec as P

NEAR = 4
FAR = 16
EDGE = 8
LANES = 128
F32, BF16 = jnp.float32, jnp.bfloat16
VMEM = pl.BlockSpec(memory_space=pltpu.VMEM)

def smooth_act(value):
    return jax.nn.gelu(value, approximate=True)


def act_adjoint(pre_value, upstream):
    unused, pullback = jax.vjp(smooth_act, pre_value)
    return pullback(upstream)[0]


def group_sizes():
    lat = math.gcd(lax.axis_size("lat"), NEAR * NEAR)
    return NEAR * NEAR // lat, lat


def swap(chunks):
    group_lon, group_lat = group_sizes()
    lon, lat = lax.axis_size("lon"), lax.axis_size("lat")
    if (lon, lat) == (group_lon, group_lat):
        return lax.all_to_all(chunks, ("lon", "lat"), 0, 0, tiled=True)
    chunks = chunks.reshape((group_lon, group_lat) + chunks.shape[1:])
    for axis, dim, size in (("lon", 0, group_lon), ("lat", 1, group_lat)):
        count = lax.axis_size(axis)
        groups = [list(range(i, i + size)) for i in range(0, count, size)]
        chunks = lax.all_to_all(chunks, axis, dim, dim, tiled=True, axis_index_groups=groups)
    return chunks.reshape((group_lon * group_lat,) + chunks.shape[2:])


def to_classes(cells):
    rows, cols, depth = cells.shape
    cells = cells.reshape(rows // NEAR, NEAR, cols // NEAR, NEAR, depth).transpose(1, 3, 0, 2, 4)
    return cells.reshape(NEAR * NEAR, rows // NEAR, cols // NEAR, depth)


def padded(cells, width):
    for axis, dim, step in zip(("lon", "lat"), (0, 1), group_sizes()):
        count = lax.axis_size(axis)
        head = lax.slice_in_dim(cells, 0, width, axis=dim)
        tail = lax.slice_in_dim(cells, cells.shape[dim] - width, cells.shape[dim], axis=dim)
        if count == step:
            before, after = jnp.zeros_like(tail), jnp.zeros_like(head)
        else:
            before = lax.ppermute(tail, axis, [(i, i + step) for i in range(count - step)])
            after = lax.ppermute(head, axis, [(i + step, i) for i in range(count - step)])
        cells = jnp.concatenate([before, cells, after], axis=dim)
    return cells


def stencil(cells, weights, step, forward):
    rows, cols, depth = cells.shape
    around = padded(cells, step)
    total = jnp.zeros((rows, cols, depth), jnp.float32)
    for tap in range(9):
        sign = step if forward else -step
        row, col = step + (tap // 3 - 1) * sign, step + (tap % 3 - 1) * sign
        window = around[row : row + rows, col : col + cols]
        dims = (((2,), (0 if forward else 1,)), ((), ()))
        total = total + lax.dot_general(window, weights[tap], dims, preferred_element_type=jnp.float32)
    return total


def ordering(dims, axes):
    cells = math.prod(dims)
    place = lax.broadcasted_iota(jnp.int32, (cells, 1), 0)
    source, stride = jnp.zeros((cells, 1), jnp.int32), 1
    for axis in reversed(axes):
        source += lax.rem(lax.div(place, jnp.int32(stride)), jnp.int32(dims[axis])) * math.prod(dims[axis + 1 :])
        stride *= dims[axis]
    return (lax.broadcasted_iota(jnp.int32, (cells, cells), 1) == source).astype(F32).astype(BF16)


def gelu_and_slope(value):
    scale, cubic = math.sqrt(2 / math.pi), 0.044715
    square = value * value
    bent = jnp.tanh(scale * value * (1 + cubic * square))
    half = 0.5 * (1 + bent)
    return value * half, half + 0.5 * value * (1 - bent * bent) * (scale * (1 + 3 * cubic * square))


def call(kernel, outs, scratch, name, megabytes, *args, specs=None, flops=0):
    specs = specs or [VMEM] * len(args)
    args = [pltpu.with_memory_space_constraint(x, spec.memory_space) for x, spec in zip(args, specs)]
    return pl.pallas_call(
        kernel,
        out_shape=[pltpu.VMEM(shape, dtype) for shape, dtype in outs],
        in_specs=specs,
        out_specs=[VMEM] * len(outs),
        scratch_shapes=scratch,
        compiler_params=pltpu.CompilerParams(vmem_limit_bytes=megabytes << 20),
        cost_estimate=pl.CostEstimate(flops=flops, bytes_accessed=sum(x.size * x.dtype.itemsize for x in args), transcendentals=0),
        name=name,
    )(*args)


def row_orders(rows, cols, sizes):
    group_lon, group_lat, row_part, col_part = sizes
    cells = rows * cols

    def kernel(to_classes, to_grid):
        to_classes[...] = ordering((row_part, NEAR, col_part, NEAR), (1, 3, 0, 2))
        to_grid[...] = ordering((group_lon, group_lat, row_part, col_part), (1, 3, 0, 2))

    return call(kernel, [((cells, cells), BF16)] * 2, [], "row_orders", 4, flops=4 * 10**9)


def pack_classes(order, observed, baseline, cotangent):
    rows, cols, depth = observed.shape
    points = lax.axis_size("path")
    cells, part = rows * cols, rows * cols // (NEAR * NEAR)

    def kernel(order, observed, baseline, cotangent, sent, diff_rows):
        mine = lax.axis_index("path")
        mix = (mine.astype(F32) + 0.5) / points
        base = baseline[...].astype(F32)
        diff = observed[...].astype(F32) - base
        field = (base + mix * diff).astype(BF16)
        moved = jnp.dot(order[...], field, preferred_element_type=F32)
        sent[:, :part, :] = moved.reshape(NEAR * NEAR, part, depth).astype(BF16)
        moved = jnp.dot(order[...], cotangent[...], preferred_element_type=F32)
        moved = moved.reshape(NEAR * NEAR, points, part // points, depth)
        own = moved[:, 0]
        for k in range(1, points):
            own = jnp.where(mine == k, moved[:, k], own)
        sent[:, part:, :] = own.astype(BF16)
        half = pl.ds(pl.multiple_of(mine * (cells // points), cells // points), cells // points)
        diff_rows[...] = (observed[half, :].astype(F32) - baseline[half, :].astype(F32)) * (1 / points)

    return call(
        kernel,
        [((NEAR * NEAR, part + part // points, depth), BF16), ((cells // points, depth), F32)],
        [],
        "pack_classes",
        8,
        order,
        *(x.reshape(cells, depth) for x in (observed, baseline, cotangent)),
        flops=4 * 10**9,
    )


def class_tools(sizes, depth, edged):
    group_lon, group_lat, row_part, col_part = sizes
    rows, cols = group_lon * row_part, group_lat * col_part
    cells = rows * cols

    def spread(values, step, at, target):
        span = slice(at, at + values.shape[1])
        edged[:, EDGE : EDGE + rows, span] = values.reshape(cols, rows, -1)
        for i in range(3):
            start = EDGE + (i - 1) * step
            shifted = edged[:, start : start + rows, span].reshape(cells, -1)
            target[:, i * depth + at : i * depth + at + values.shape[1]] = shifted.astype(BF16)

    def stencil_part(source, weights, step, at, end, forward):
        def weigh(values, col):
            if forward:
                blocks = [part[i, col, :, at:end] for i in range(3) for part in weights]
                return jnp.dot(values, jnp.concatenate(blocks, axis=0), preferred_element_type=F32)
            taps_of = [jnp.concatenate([part[2 - i, 2 - col] for part in weights], axis=0)[at:end] for i in range(3)]
            return lax.dot_general(
                values, jnp.concatenate(taps_of, axis=1), (((1,), (1,)), ((), ())), preferred_element_type=F32
            )

        shift = step * rows
        fill = jnp.zeros((shift, end - at), F32)
        same = weigh(source[...], 1)
        after = weigh(source[shift:, :], 2)
        before = weigh(source[: cells - shift, :], 0)
        return same + jnp.concatenate([after, fill], axis=0) + jnp.concatenate([fill, before], axis=0)

    edged[:, :EDGE, :] = jnp.zeros((cols, EDGE, depth), F32)
    edged[:, EDGE + rows :, :] = jnp.zeros((cols, EDGE, depth), F32)
    return spread, stencil_part


def by_place(points, run, *halves):
    for place in range(points):
        owners = [(place - k) % points for k in range(points)]
        lists = [[parts[k] for k in owners] for parts in halves]
        pl.when(lax.axis_index("path") == place)(functools.partial(run, place, *lists))


def channel_parts(depth):
    return [(at, min(at + 2 * LANES, depth)) for at in range(0, depth, 2 * LANES)]


def slopes_of_class(order, got, first_halves, first_bias, second_halves, second_bias, sizes):
    group_lon, group_lat, row_part, col_part = sizes
    points, depth = len(first_halves), got.shape[-1]
    rows, cols, part = group_lon * row_part, group_lat * col_part, row_part * col_part
    cells = rows * cols

    def kernel(order, got, first_bias, second_bias, *refs):
        first_slope, second_slope, edged, near_taps, far_taps = refs[2 * points :]

        def run(place, first, second):
            spread, stencil_part = class_tools(sizes, depth, edged)
            field = jnp.dot(order[...], got[:, :part, :].reshape(cells, depth), preferred_element_type=F32)
            spread(field, 1, 0, near_taps)
            for at, end in channel_parts(depth):
                pre = stencil_part(near_taps, first, 1, at, end, True) + first_bias[at:end].reshape(1, -1)
                act, first_slope[:, at:end] = gelu_and_slope(pre)
                spread(field[:, at:end] + act, FAR // NEAR, at, far_taps)
            for at, end in channel_parts(depth):
                pre = stencil_part(far_taps, second, FAR // NEAR, at, end, True) + second_bias[at:end].reshape(1, -1)
                second_slope[:, at:end] = gelu_and_slope(pre)[1]

        by_place(points, run, refs[:points], refs[points : 2 * points])

    return call(
        kernel,
        [((cells, depth), F32)] * 2,
        [pltpu.VMEM((cols, rows + 2 * EDGE, depth), F32)] + [pltpu.VMEM((cells, 3 * depth), BF16)] * 2,
        "slopes_of_class",
        16,
        order,
        got,
        first_bias,
        second_bias,
        *first_halves,
        *second_halves,
    )


def adjoint_of_class(order, cotangents, first_slope, second_slope, first_halves, second_halves, sizes):
    group_lon, group_lat, row_part, col_part = sizes
    points, depth = len(first_halves), first_slope.shape[-1]
    rows, cols = group_lon * row_part, group_lat * col_part
    cells, span = rows * cols, row_part // points

    def kernel(order, first_slope, second_slope, *refs):
        kept, sent, edged, near_taps, far_taps, grad, laned = refs[3 * points :]

        def run(place, cotangent, first, second):
            spread, stencil_part = class_tools(sizes, depth, edged)
            upstream = jnp.concatenate([share[...].astype(F32) for share in cotangent], axis=1)
            upstream = jnp.dot(order[...], upstream.reshape(cells, depth).astype(BF16), preferred_element_type=F32)
            spread(second_slope[...] * upstream, FAR // NEAR, 0, far_taps)
            for at, end in channel_parts(depth):
                hidden_adj = upstream[:, at:end] + stencil_part(far_taps, second, FAR // NEAR, at, end, False)
                grad[:, at:end] = hidden_adj
                spread(first_slope[:, at:end] * hidden_adj, 1, at, near_taps)
            for at, end in channel_parts(depth):
                grad[:, at:end] += stencil_part(near_taps, first, 1, at, end, False)
                for b in range(at // LANES, end // LANES):
                    laned[b] = grad[:, b * LANES : (b + 1) * LANES].reshape(cols, rows, LANES)
            for k in range(points):
                owner = (place + k) % points
                target = kept if k == 0 else sent.at[k - 1]
                for i in range(span):
                    here = slice(i * (cells // row_part), (i + 1) * (cells // row_part))
                    for b in range(depth // LANES):
                        rows_of = laned[b, :, pl.ds(owner * span + i, group_lon, stride=row_part), :]
                        target[here, b * LANES : (b + 1) * LANES] = rows_of.reshape(-1, LANES)

        by_place(points, run, refs[:points], refs[points : 2 * points], refs[2 * points : 3 * points])

    share = cells // points
    return call(
        kernel,
        [((share, depth), F32), ((points - 1, share, depth), F32)],
        [pltpu.VMEM((cols, rows + 2 * EDGE, depth), F32)]
        + [pltpu.VMEM((cells, 3 * depth), BF16)] * 2
        + [pltpu.VMEM((cells, depth), F32), pltpu.VMEM((depth // LANES, cols, rows, LANES), F32)],
        "adjoint_of_class",
        16,
        order,
        first_slope,
        second_slope,
        *cotangents,
        *first_halves,
        *second_halves,
    )


def total_for_homes(kept, others, sizes):
    group_lon, group_lat, row_part, col_part = sizes
    share, depth = kept.shape
    span = row_part // lax.axis_size("path")
    part = span * col_part

    def kernel(kept, *refs):
        order = ordering((span, group_lat, col_part, group_lon), (3, 1, 0, 2))
        others, sent = refs[:-1], refs[-1]
        total = kept[...]
        for other in others:
            total = total + other[...]
        moved = jnp.dot(order, total.astype(BF16), preferred_element_type=F32)
        sent[...] = moved.reshape(share // part, part, depth).astype(BF16)

    return call(kernel, [((share // part, part, depth), BF16)], [], "total_for_homes", 4, kept, *others)[0]


def attribution_rows(home, diff_rows, rows, cols):
    depth = home.shape[-1]
    cells = rows * cols

    def kernel(home, diff_rows, out):
        order = ordering((NEAR, NEAR, rows // NEAR, cols // NEAR), (2, 0, 3, 1))
        values = home[...].astype(F32).reshape(cells, depth).astype(BF16)
        moved = jnp.dot(order, values, preferred_element_type=F32)
        out[...] = (diff_rows[...] * moved).reshape(rows, cols, depth).astype(BF16)

    return call(kernel, [((rows, cols, depth), BF16)], [], "attribution_rows", 4, home, diff_rows)[0]


def one_group(observed, baseline, cotangent, first_weight, first_bias, second_weight, second_bias):
    rows, cols, depth = observed.shape
    points = lax.axis_size("path")
    sizes = group_sizes() + (rows // NEAR, cols // NEAR)

    def turned(values, step):
        return lax.ppermute(values, "path", [(i, (i + step) % points) for i in range(points)])

    side = math.isqrt(first_weight.shape[0])
    halves = [
        [x.reshape((side, side) + x.shape[1:]) for x in [part] + [turned(part, step) for step in range(1, points)]]
        for part in (first_weight, second_weight)
    ]
    to_classes, to_grid = row_orders(rows, cols, sizes)
    sent, diff_rows = pack_classes(to_classes, observed, baseline, cotangent)
    got = swap(sent)
    own = got[:, sizes[2] * sizes[3] :, :]
    cotangents = [own] + [turned(own, step) for step in range(1, points)]
    first_slope, second_slope = slopes_of_class(to_grid, got, halves[0], first_bias, halves[1], second_bias, sizes)
    kept, others = adjoint_of_class(to_grid, cotangents, first_slope, second_slope, *halves, sizes)
    others = [turned(others[step - 1], step) for step in range(1, points)]
    home = swap(total_for_homes(kept, others, sizes))
    return attribution_rows(home, diff_rows, rows // points, cols)


def several_groups(observed, baseline, cotangent, first_weight, first_bias, second_weight, second_bias):
    rows, cols, depth = observed.shape
    points, point = lax.axis_size("path"), lax.axis_index("path")
    group_lon, group_lat = group_sizes()
    row_part, col_part = rows // NEAR, cols // NEAR
    ring = [(i, (i + 1) % points) for i in range(points)]

    def whole_weight(part):
        held = jnp.zeros((part.shape[0], points) + part.shape[1:], part.dtype)
        for step in range(points):
            held = lax.dynamic_update_slice_in_dim(held, part[:, None], (point - step) % points, 1)
            if step < points - 1:
                part = lax.ppermute(part, "path", ring)
        return held.reshape(held.shape[0], -1, held.shape[3])

    first_full, second_full = whole_weight(first_weight), whole_weight(second_weight)
    diff = observed.astype(jnp.float32) - baseline.astype(jnp.float32)
    mix = (point.astype(jnp.float32) + 0.5) / points
    field = (baseline.astype(jnp.float32) + mix * diff).astype(jnp.bfloat16)
    sent = jnp.stack([to_classes(field), to_classes(cotangent)], axis=1)
    got = swap(sent).reshape(group_lon, group_lat, 2, row_part, col_part, depth)
    got = got.transpose(2, 0, 3, 1, 4, 5).reshape(2, group_lon * row_part, group_lat * col_part, depth)
    field, upstream = got[0], got[1].astype(jnp.float32)

    first_pre = stencil(field, first_full, 1, True) + first_bias
    hidden = (field.astype(jnp.float32) + smooth_act(first_pre)).astype(jnp.bfloat16)
    second_pre = stencil(hidden, second_full, FAR // NEAR, True) + second_bias
    second_adj = act_adjoint(second_pre, upstream).astype(jnp.bfloat16)
    hidden_adj = upstream + stencil(second_adj, second_full, FAR // NEAR, False)
    first_adj = act_adjoint(first_pre, hidden_adj).astype(jnp.bfloat16)
    grad = hidden_adj + stencil(first_adj, first_full, 1, False)

    part = row_part // points
    grad = grad.reshape(group_lon, points, part, group_lat, col_part, depth).transpose(1, 0, 3, 2, 4, 5)
    grad = grad.reshape(points, group_lon * group_lat, part, col_part, depth)
    total = lax.dynamic_index_in_dim(grad, point, 0, keepdims=False)
    for step in range(1, points):
        other = lax.dynamic_index_in_dim(grad, (point + step) % points, 0, keepdims=False)
        total = total + lax.ppermute(other, "path", [(i, (i + step) % points) for i in range(points)])
    home = swap(total.astype(jnp.bfloat16)).reshape(NEAR, NEAR, part, col_part, depth)
    home = home.transpose(2, 0, 3, 1, 4).reshape(rows // points, cols, depth).astype(jnp.float32)
    diff_rows = lax.dynamic_slice_in_dim(diff, point * (rows // points), rows // points, 0)
    return (diff_rows * home / points).astype(jnp.bfloat16)


def shards(*args):
    if group_sizes() == (lax.axis_size("lon"), lax.axis_size("lat")):
        return one_group(*args)
    return several_groups(*args)


def solution(mesh):
    placed = (
        P("lon", "lat", None),
        P("lon", "lat", None),
        P("lon", "lat", None),
        P(None, "path", None),
        P(),
        P(None, "path", None),
        P(),
    )
    return jax.shard_map(
        shards,
        mesh=mesh,
        in_specs=placed,
        out_specs=P(("lon", "path"), "lat", None),
        check_vma=False,
    )
```

```python
import functools
import math

import jax
import jax.numpy as jnp
from jax import lax
from jax.experimental import pallas as pl
from jax.experimental.pallas import tpu as pltpu
from jax.sharding import PartitionSpec as P

NEAR = 4
FAR = 16
EDGE = 8
LANES = 128
F32, BF16 = jnp.float32, jnp.bfloat16
VMEM = pl.BlockSpec(memory_space=pltpu.VMEM)

def smooth_act(value):
    return jax.nn.gelu(value, approximate=True)


def act_adjoint(pre_value, upstream):
    unused, pullback = jax.vjp(smooth_act, pre_value)
    return pullback(upstream)[0]


def group_sizes():
    lat = math.gcd(lax.axis_size("lat"), NEAR * NEAR)
    return NEAR * NEAR // lat, lat


def swap(chunks):
    group_lon, group_lat = group_sizes()
    lon, lat = lax.axis_size("lon"), lax.axis_size("lat")
    if (lon, lat) == (group_lon, group_lat):
        return lax.all_to_all(chunks, ("lon", "lat"), 0, 0, tiled=True)
    chunks = chunks.reshape((group_lon, group_lat) + chunks.shape[1:])
    for axis, dim, size in (("lon", 0, group_lon), ("lat", 1, group_lat)):
        count = lax.axis_size(axis)
        groups = [list(range(i, i + size)) for i in range(0, count, size)]
        chunks = lax.all_to_all(chunks, axis, dim, dim, tiled=True, axis_index_groups=groups)
    return chunks.reshape((group_lon * group_lat,) + chunks.shape[2:])


def to_classes(cells):
    rows, cols, depth = cells.shape
    cells = cells.reshape(rows // NEAR, NEAR, cols // NEAR, NEAR, depth).transpose(1, 3, 0, 2, 4)
    return cells.reshape(NEAR * NEAR, rows // NEAR, cols // NEAR, depth)


def padded(cells, width):
    for axis, dim, step in zip(("lon", "lat"), (0, 1), group_sizes()):
        count = lax.axis_size(axis)
        head = lax.slice_in_dim(cells, 0, width, axis=dim)
        tail = lax.slice_in_dim(cells, cells.shape[dim] - width, cells.shape[dim], axis=dim)
        if count == step:
            before, after = jnp.zeros_like(tail), jnp.zeros_like(head)
        else:
            before = lax.ppermute(tail, axis, [(i, i + step) for i in range(count - step)])
            after = lax.ppermute(head, axis, [(i + step, i) for i in range(count - step)])
        cells = jnp.concatenate([before, cells, after], axis=dim)
    return cells


def stencil(cells, weights, step, forward):
    rows, cols, depth = cells.shape
    around = padded(cells, step)
    total = jnp.zeros((rows, cols, depth), jnp.float32)
    for tap in range(9):
        sign = step if forward else -step
        row, col = step + (tap // 3 - 1) * sign, step + (tap % 3 - 1) * sign
        window = around[row : row + rows, col : col + cols]
        dims = (((2,), (0 if forward else 1,)), ((), ()))
        total = total + lax.dot_general(window, weights[tap], dims, preferred_element_type=jnp.float32)
    return total


def ordering(dims, axes):
    cells = math.prod(dims)
    place = lax.broadcasted_iota(jnp.int32, (cells, 1), 0)
    source, stride = jnp.zeros((cells, 1), jnp.int32), 1
    for axis in reversed(axes):
        source += lax.rem(lax.div(place, jnp.int32(stride)), jnp.int32(dims[axis])) * math.prod(dims[axis + 1 :])
        stride *= dims[axis]
    return (lax.broadcasted_iota(jnp.int32, (cells, cells), 1) == source).astype(F32).astype(BF16)


def gelu_and_slope(value):
    scale, cubic = math.sqrt(2 / math.pi), 0.044715
    square = value * value
    bent = jnp.tanh(scale * value * (1 + cubic * square))
    half = 0.5 * (1 + bent)
    return value * half, half + 0.5 * value * (1 - bent * bent) * (scale * (1 + 3 * cubic * square))


def call(kernel, outs, scratch, name, megabytes, *args, specs=None, flops=0):
    specs = specs or [VMEM] * len(args)
    args = [pltpu.with_memory_space_constraint(x, spec.memory_space) for x, spec in zip(args, specs)]
    return pl.pallas_call(
        kernel,
        out_shape=[pltpu.VMEM(shape, dtype) for shape, dtype in outs],
        in_specs=specs,
        out_specs=[VMEM] * len(outs),
        scratch_shapes=scratch,
        compiler_params=pltpu.CompilerParams(vmem_limit_bytes=megabytes << 20),
        cost_estimate=pl.CostEstimate(flops=flops, bytes_accessed=sum(x.size * x.dtype.itemsize for x in args), transcendentals=0),
        name=name,
    )(*args)


def row_orders(rows, cols, sizes):
    group_lon, group_lat, row_part, col_part = sizes
    cells = rows * cols

    def kernel(to_classes, to_grid):
        to_classes[...] = ordering((row_part, NEAR, col_part, NEAR), (1, 3, 0, 2))
        to_grid[...] = ordering((group_lon, group_lat, row_part, col_part), (1, 3, 0, 2))

    return call(kernel, [((cells, cells), BF16)] * 2, [], "row_orders", 4, flops=4 * 10**9)


def pack_classes(order, observed, baseline, cotangent):
    rows, cols, depth = observed.shape
    points = lax.axis_size("path")
    cells, part = rows * cols, rows * cols // (NEAR * NEAR)

    def kernel(order, observed, baseline, cotangent, sent, diff_rows):
        mine = lax.axis_index("path")
        mix = (mine.astype(F32) + 0.5) / points
        base = baseline[...].astype(F32)
        diff = observed[...].astype(F32) - base
        field = (base + mix * diff).astype(BF16)
        moved = jnp.dot(order[...], field, preferred_element_type=F32)
        sent[:, :part, :] = moved.reshape(NEAR * NEAR, part, depth).astype(BF16)
        moved = jnp.dot(order[...], cotangent[...], preferred_element_type=F32)
        moved = moved.reshape(NEAR * NEAR, points, part // points, depth)
        own = moved[:, 0]
        for k in range(1, points):
            own = jnp.where(mine == k, moved[:, k], own)
        sent[:, part:, :] = own.astype(BF16)
        half = pl.ds(pl.multiple_of(mine * (cells // points), cells // points), cells // points)
        diff_rows[...] = (observed[half, :].astype(F32) - baseline[half, :].astype(F32)) * (1 / points)

    return call(
        kernel,
        [((NEAR * NEAR, part + part // points, depth), BF16), ((cells // points, depth), F32)],
        [],
        "pack_classes",
        8,
        order,
        *(x.reshape(cells, depth) for x in (observed, baseline, cotangent)),
        flops=4 * 10**9,
    )


def class_tools(sizes, depth, edged):
    group_lon, group_lat, row_part, col_part = sizes
    rows, cols = group_lon * row_part, group_lat * col_part
    cells = rows * cols

    def spread(values, step, at, target):
        span = slice(at, at + values.shape[1])
        edged[:, EDGE : EDGE + rows, span] = values.reshape(cols, rows, -1)
        for i in range(3):
            start = EDGE + (i - 1) * step
            shifted = edged[:, start : start + rows, span].reshape(cells, -1)
            target[:, i * depth + at : i * depth + at + values.shape[1]] = shifted.astype(BF16)

    def stencil_part(source, weights, step, at, end, forward):
        def weigh(values, col):
            if forward:
                blocks = [part[i, col, :, at:end] for i in range(3) for part in weights]
                return jnp.dot(values, jnp.concatenate(blocks, axis=0), preferred_element_type=F32)
            taps_of = [jnp.concatenate([part[2 - i, 2 - col] for part in weights], axis=0)[at:end] for i in range(3)]
            return lax.dot_general(
                values, jnp.concatenate(taps_of, axis=1), (((1,), (1,)), ((), ())), preferred_element_type=F32
            )

        shift = step * rows
        fill = jnp.zeros((shift, end - at), F32)
        same = weigh(source[...], 1)
        after = weigh(source[shift:, :], 2)
        before = weigh(source[: cells - shift, :], 0)
        return same + jnp.concatenate([after, fill], axis=0) + jnp.concatenate([fill, before], axis=0)

    edged[:, :EDGE, :] = jnp.zeros((cols, EDGE, depth), F32)
    edged[:, EDGE + rows :, :] = jnp.zeros((cols, EDGE, depth), F32)
    return spread, stencil_part


def by_place(points, run, *halves):
    for place in range(points):
        owners = [(place - k) % points for k in range(points)]
        lists = [[parts[k] for k in owners] for parts in halves]
        pl.when(lax.axis_index("path") == place)(functools.partial(run, place, *lists))


def channel_parts(depth):
    return [(at, min(at + 2 * LANES, depth)) for at in range(0, depth, 2 * LANES)]


def slopes_of_class(order, got, first_halves, first_bias, second_halves, second_bias, sizes):
    group_lon, group_lat, row_part, col_part = sizes
    points, depth = len(first_halves), got.shape[-1]
    rows, cols, part = group_lon * row_part, group_lat * col_part, row_part * col_part
    cells = rows * cols

    def kernel(order, got, first_bias, second_bias, *refs):
        first_slope, second_slope, edged, near_taps, far_taps = refs[2 * points :]

        def run(place, first, second):
            spread, stencil_part = class_tools(sizes, depth, edged)
            field = jnp.dot(order[...], got[:, :part, :].reshape(cells, depth), preferred_element_type=F32)
            spread(field, 1, 0, near_taps)
            for at, end in channel_parts(depth):
                pre = stencil_part(near_taps, first, 1, at, end, True) + first_bias[at:end].reshape(1, -1)
                act, first_slope[:, at:end] = gelu_and_slope(pre)
                spread(field[:, at:end] + act, FAR // NEAR, at, far_taps)
            for at, end in channel_parts(depth):
                pre = stencil_part(far_taps, second, FAR // NEAR, at, end, True) + second_bias[at:end].reshape(1, -1)
                second_slope[:, at:end] = gelu_and_slope(pre)[1]

        by_place(points, run, refs[:points], refs[points : 2 * points])

    return call(
        kernel,
        [((cells, depth), F32)] * 2,
        [pltpu.VMEM((cols, rows + 2 * EDGE, depth), F32)] + [pltpu.VMEM((cells, 3 * depth), BF16)] * 2,
        "slopes_of_class",
        16,
        order,
        got,
        first_bias,
        second_bias,
        *first_halves,
        *second_halves,
    )


def adjoint_of_class(order, cotangents, first_slope, second_slope, first_halves, second_halves, sizes):
    group_lon, group_lat, row_part, col_part = sizes
    points, depth = len(first_halves), first_slope.shape[-1]
    rows, cols = group_lon * row_part, group_lat * col_part
    cells, part = rows * cols, row_part // points * col_part

    def kernel(order, first_slope, second_slope, *refs):
        sent, edged, near_taps, far_taps, grad = refs[3 * points :]

        def run(place, cotangent, first, second):
            spread, stencil_part = class_tools(sizes, depth, edged)
            upstream = jnp.concatenate([share[...].astype(F32) for share in cotangent], axis=1)
            upstream = jnp.dot(order[...], upstream.reshape(cells, depth).astype(BF16), preferred_element_type=F32)
            spread(second_slope[...] * upstream, FAR // NEAR, 0, far_taps)
            for at, end in channel_parts(depth):
                hidden_adj = upstream[:, at:end] + stencil_part(far_taps, second, FAR // NEAR, at, end, False)
                grad[:, at:end] = hidden_adj
                spread(first_slope[:, at:end] * hidden_adj, 1, at, near_taps)
            home = ordering((group_lat, col_part, group_lon, row_part), (2, 0, 3, 1))
            for at, end in channel_parts(depth):
                grad[:, at:end] += stencil_part(near_taps, first, 1, at, end, False)
            moved = jnp.dot(home, grad[...].astype(BF16), preferred_element_type=F32)
            sent[...] = moved.reshape(cells // part, part, depth).astype(BF16)

        by_place(points, run, refs[:points], refs[points : 2 * points], refs[2 * points : 3 * points])

    return call(
        kernel,
        [((cells // part, part, depth), BF16)],
        [pltpu.VMEM((cols, rows + 2 * EDGE, depth), F32)]
        + [pltpu.VMEM((cells, 3 * depth), BF16)] * 2
        + [pltpu.VMEM((cells, depth), F32)],
        "adjoint_of_class",
        16,
        order,
        first_slope,
        second_slope,
        *cotangents,
        *first_halves,
        *second_halves,
    )[0]


def attribution_rows(home, diff_rows, rows, cols):
    points, depth = lax.axis_size("path"), home.shape[-1]
    cells = rows * cols

    def kernel(home, diff_rows, out):
        order = ordering((NEAR, NEAR, points, rows // NEAR, cols // NEAR), (2, 3, 0, 4, 1))
        order = sum(order[k * cells : (k + 1) * cells] for k in range(points))
        values = home[...].astype(F32).reshape(points * cells, depth).astype(BF16)
        moved = jnp.dot(order, values, preferred_element_type=F32)
        out[...] = (diff_rows[...] * moved).reshape(rows, cols, depth).astype(BF16)

    return call(kernel, [((rows, cols, depth), BF16)], [], "attribution_rows", 4, home, diff_rows)[0]


def one_group(observed, baseline, cotangent, first_weight, first_bias, second_weight, second_bias):
    rows, cols, depth = observed.shape
    points = lax.axis_size("path")
    sizes = group_sizes() + (rows // NEAR, cols // NEAR)

    def turned(values, step):
        return lax.ppermute(values, "path", [(i, (i + step) % points) for i in range(points)])

    side = math.isqrt(first_weight.shape[0])
    halves = [
        [x.reshape((side, side) + x.shape[1:]) for x in [part] + [turned(part, step) for step in range(1, points)]]
        for part in (first_weight, second_weight)
    ]
    to_classes, to_grid = row_orders(rows, cols, sizes)
    sent, diff_rows = pack_classes(to_classes, observed, baseline, cotangent)
    got = swap(sent)
    own = got[:, sizes[2] * sizes[3] :, :]
    cotangents = [own] + [turned(own, step) for step in range(1, points)]
    first_slope, second_slope = slopes_of_class(to_grid, got, halves[0], first_bias, halves[1], second_bias, sizes)
    grad = adjoint_of_class(to_grid, cotangents, first_slope, second_slope, *halves, sizes)
    home = lax.all_to_all(grad, ("lon", "lat", "path"), 0, 0, tiled=True)
    return attribution_rows(home, diff_rows, rows // points, cols)


def several_groups(observed, baseline, cotangent, first_weight, first_bias, second_weight, second_bias):
    rows, cols, depth = observed.shape
    points, point = lax.axis_size("path"), lax.axis_index("path")
    group_lon, group_lat = group_sizes()
    row_part, col_part = rows // NEAR, cols // NEAR
    ring = [(i, (i + 1) % points) for i in range(points)]

    def whole_weight(part):
        held = jnp.zeros((part.shape[0], points) + part.shape[1:], part.dtype)
        for step in range(points):
            held = lax.dynamic_update_slice_in_dim(held, part[:, None], (point - step) % points, 1)
            if step < points - 1:
                part = lax.ppermute(part, "path", ring)
        return held.reshape(held.shape[0], -1, held.shape[3])

    first_full, second_full = whole_weight(first_weight), whole_weight(second_weight)
    diff = observed.astype(jnp.float32) - baseline.astype(jnp.float32)
    mix = (point.astype(jnp.float32) + 0.5) / points
    field = (baseline.astype(jnp.float32) + mix * diff).astype(jnp.bfloat16)
    sent = jnp.stack([to_classes(field), to_classes(cotangent)], axis=1)
    got = swap(sent).reshape(group_lon, group_lat, 2, row_part, col_part, depth)
    got = got.transpose(2, 0, 3, 1, 4, 5).reshape(2, group_lon * row_part, group_lat * col_part, depth)
    field, upstream = got[0], got[1].astype(jnp.float32)

    first_pre = stencil(field, first_full, 1, True) + first_bias
    hidden = (field.astype(jnp.float32) + smooth_act(first_pre)).astype(jnp.bfloat16)
    second_pre = stencil(hidden, second_full, FAR // NEAR, True) + second_bias
    second_adj = act_adjoint(second_pre, upstream).astype(jnp.bfloat16)
    hidden_adj = upstream + stencil(second_adj, second_full, FAR // NEAR, False)
    first_adj = act_adjoint(first_pre, hidden_adj).astype(jnp.bfloat16)
    grad = hidden_adj + stencil(first_adj, first_full, 1, False)

    part = row_part // points
    grad = grad.reshape(group_lon, points, part, group_lat, col_part, depth).transpose(1, 0, 3, 2, 4, 5)
    grad = grad.reshape(points, group_lon * group_lat, part, col_part, depth)
    total = lax.dynamic_index_in_dim(grad, point, 0, keepdims=False)
    for step in range(1, points):
        other = lax.dynamic_index_in_dim(grad, (point + step) % points, 0, keepdims=False)
        total = total + lax.ppermute(other, "path", [(i, (i + step) % points) for i in range(points)])
    home = swap(total.astype(jnp.bfloat16)).reshape(NEAR, NEAR, part, col_part, depth)
    home = home.transpose(2, 0, 3, 1, 4).reshape(rows // points, cols, depth).astype(jnp.float32)
    diff_rows = lax.dynamic_slice_in_dim(diff, point * (rows // points), rows // points, 0)
    return (diff_rows * home / points).astype(jnp.bfloat16)


def shards(*args):
    if group_sizes() == (lax.axis_size("lon"), lax.axis_size("lat")):
        return one_group(*args)
    return several_groups(*args)


def solution(mesh):
    placed = (
        P("lon", "lat", None),
        P("lon", "lat", None),
        P("lon", "lat", None),
        P(None, "path", None),
        P(),
        P(None, "path", None),
        P(),
    )
    return jax.shard_map(
        shards,
        mesh=mesh,
        in_specs=placed,
        out_specs=P(("lon", "path"), "lat", None),
        check_vma=False,
    )
```

```python
import functools
import math

import jax
import jax.numpy as jnp
from jax import lax
from jax.experimental import pallas as pl
from jax.experimental.pallas import tpu as pltpu
from jax.sharding import PartitionSpec as P

NEAR = 4
FAR = 16
EDGE = 8
LANES = 128
F32, BF16 = jnp.float32, jnp.bfloat16
VMEM = pl.BlockSpec(memory_space=pltpu.VMEM)

def smooth_act(value):
    return jax.nn.gelu(value, approximate=True)


def act_adjoint(pre_value, upstream):
    unused, pullback = jax.vjp(smooth_act, pre_value)
    return pullback(upstream)[0]


def group_sizes():
    lat = math.gcd(lax.axis_size("lat"), NEAR * NEAR)
    return NEAR * NEAR // lat, lat


def swap(chunks):
    group_lon, group_lat = group_sizes()
    lon, lat = lax.axis_size("lon"), lax.axis_size("lat")
    if (lon, lat) == (group_lon, group_lat):
        return lax.all_to_all(chunks, ("lon", "lat"), 0, 0, tiled=True)
    chunks = chunks.reshape((group_lon, group_lat) + chunks.shape[1:])
    for axis, dim, size in (("lon", 0, group_lon), ("lat", 1, group_lat)):
        count = lax.axis_size(axis)
        groups = [list(range(i, i + size)) for i in range(0, count, size)]
        chunks = lax.all_to_all(chunks, axis, dim, dim, tiled=True, axis_index_groups=groups)
    return chunks.reshape((group_lon * group_lat,) + chunks.shape[2:])


def to_classes(cells):
    rows, cols, depth = cells.shape
    cells = cells.reshape(rows // NEAR, NEAR, cols // NEAR, NEAR, depth).transpose(1, 3, 0, 2, 4)
    return cells.reshape(NEAR * NEAR, rows // NEAR, cols // NEAR, depth)


def padded(cells, width):
    for axis, dim, step in zip(("lon", "lat"), (0, 1), group_sizes()):
        count = lax.axis_size(axis)
        head = lax.slice_in_dim(cells, 0, width, axis=dim)
        tail = lax.slice_in_dim(cells, cells.shape[dim] - width, cells.shape[dim], axis=dim)
        if count == step:
            before, after = jnp.zeros_like(tail), jnp.zeros_like(head)
        else:
            before = lax.ppermute(tail, axis, [(i, i + step) for i in range(count - step)])
            after = lax.ppermute(head, axis, [(i + step, i) for i in range(count - step)])
        cells = jnp.concatenate([before, cells, after], axis=dim)
    return cells


def stencil(cells, weights, step, forward):
    rows, cols, depth = cells.shape
    around = padded(cells, step)
    total = jnp.zeros((rows, cols, depth), jnp.float32)
    for tap in range(9):
        sign = step if forward else -step
        row, col = step + (tap // 3 - 1) * sign, step + (tap % 3 - 1) * sign
        window = around[row : row + rows, col : col + cols]
        dims = (((2,), (0 if forward else 1,)), ((), ()))
        total = total + lax.dot_general(window, weights[tap], dims, preferred_element_type=jnp.float32)
    return total


def ordering(dims, axes):
    cells = math.prod(dims)
    place = lax.broadcasted_iota(jnp.int32, (cells, 1), 0)
    source, stride = jnp.zeros((cells, 1), jnp.int32), 1
    for axis in reversed(axes):
        source += lax.rem(lax.div(place, jnp.int32(stride)), jnp.int32(dims[axis])) * math.prod(dims[axis + 1 :])
        stride *= dims[axis]
    return (lax.broadcasted_iota(jnp.int32, (cells, cells), 1) == source).astype(F32).astype(BF16)


def gelu_and_slope(value):
    scale, cubic = math.sqrt(2 / math.pi), 0.044715
    square = value * value
    bent = jnp.tanh(scale * value * (1 + cubic * square))
    half = 0.5 * (1 + bent)
    return value * half, half + 0.5 * value * (1 - bent * bent) * (scale * (1 + 3 * cubic * square))


def call(kernel, outs, scratch, name, megabytes, *args, specs=None, flops=0):
    specs = specs or [VMEM] * len(args)
    args = [pltpu.with_memory_space_constraint(x, spec.memory_space) for x, spec in zip(args, specs)]
    return pl.pallas_call(
        kernel,
        out_shape=[pltpu.VMEM(shape, dtype) for shape, dtype in outs],
        in_specs=specs,
        out_specs=[VMEM] * len(outs),
        scratch_shapes=scratch,
        compiler_params=pltpu.CompilerParams(vmem_limit_bytes=megabytes << 20),
        cost_estimate=pl.CostEstimate(flops=flops, bytes_accessed=sum(x.size * x.dtype.itemsize for x in args), transcendentals=0),
        name=name,
    )(*args)


def row_orders(rows, cols, sizes):
    group_lon, group_lat, row_part, col_part = sizes
    cells = rows * cols

    def kernel(to_classes, to_grid):
        to_classes[...] = ordering((row_part, NEAR, col_part, NEAR), (1, 3, 0, 2))
        to_grid[...] = ordering((group_lon, group_lat, row_part, col_part), (1, 3, 0, 2))

    return call(kernel, [((cells, cells), BF16)] * 2, [], "row_orders", 4, flops=4 * 10**9)


def pack_classes(order, observed, baseline, cotangent):
    rows, cols, depth = observed.shape
    points = lax.axis_size("path")
    cells, part = rows * cols, rows * cols // (NEAR * NEAR)

    def kernel(order, observed, baseline, cotangent, sent, diff_rows):
        mine = lax.axis_index("path")
        mix = (mine.astype(F32) + 0.5) / points
        base = baseline[...].astype(F32)
        diff = observed[...].astype(F32) - base
        field = (base + mix * diff).astype(BF16)
        moved = jnp.dot(order[...], field, preferred_element_type=F32)
        sent[:, :part, :] = moved.reshape(NEAR * NEAR, part, depth).astype(BF16)
        moved = jnp.dot(order[...], cotangent[...], preferred_element_type=F32)
        moved = moved.reshape(NEAR * NEAR, points, part // points, depth)
        own = moved[:, 0]
        for k in range(1, points):
            own = jnp.where(mine == k, moved[:, k], own)
        sent[:, part:, :] = own.astype(BF16)
        half = pl.ds(pl.multiple_of(mine * (cells // points), cells // points), cells // points)
        diff_rows[...] = (observed[half, :].astype(F32) - baseline[half, :].astype(F32)) * (1 / points)

    return call(
        kernel,
        [((NEAR * NEAR, part + part // points, depth), BF16), ((cells // points, depth), F32)],
        [],
        "pack_classes",
        8,
        order,
        *(x.reshape(cells, depth) for x in (observed, baseline, cotangent)),
        flops=4 * 10**9,
    )


def class_tools(sizes, depth, edged):
    group_lon, group_lat, row_part, col_part = sizes
    rows, cols = group_lon * row_part, group_lat * col_part
    cells = rows * cols

    def spread(values, step, at, target):
        span = slice(at, at + values.shape[1])
        edged[:, EDGE : EDGE + rows, span] = values.reshape(cols, rows, -1)
        for i in range(3):
            start = EDGE + (i - 1) * step
            shifted = edged[:, start : start + rows, span].reshape(cells, -1)
            target[:, i * depth + at : i * depth + at + values.shape[1]] = shifted.astype(BF16)

    def convolution(source, weights, step):
        shift = step * rows

        def products(values, *columns):
            blocks = [
                jnp.concatenate([part[i, col] for i in range(3) for part in weights], axis=0) for col in columns
            ]
            joint = jnp.dot(values, jnp.concatenate(blocks, axis=1), preferred_element_type=F32)
            return [joint[:, i * depth : (i + 1) * depth] for i in range(len(columns))]

        if 2 * shift == cells:
            same_low, before = products(source[:shift, :], 1, 0)
            same_high, after = products(source[shift:, :], 1, 2)
            return jnp.concatenate([same_low + after, same_high + before], axis=0)
        before, same, after = products(source[...], 0, 1, 2)
        fill = jnp.zeros((shift, depth), F32)
        after = jnp.concatenate([after[shift:], fill], axis=0)
        return same + after + jnp.concatenate([fill, before[: cells - shift]], axis=0)

    def transposed_part(source, weights, step, at, end):
        def weigh(values, col):
            taps_of = [jnp.concatenate([part[2 - i, 2 - col] for part in weights], axis=0)[at:end] for i in range(3)]
            return lax.dot_general(
                values, jnp.concatenate(taps_of, axis=1), (((1,), (1,)), ((), ())), preferred_element_type=F32
            )

        shift = step * rows
        fill = jnp.zeros((shift, end - at), F32)
        same = weigh(source[...], 1)
        after = weigh(source[shift:, :], 2)
        before = weigh(source[: cells - shift, :], 0)
        return same + jnp.concatenate([after, fill], axis=0) + jnp.concatenate([fill, before], axis=0)

    edged[:, :EDGE, :] = jnp.zeros((cols, EDGE, depth), F32)
    edged[:, EDGE + rows :, :] = jnp.zeros((cols, EDGE, depth), F32)
    return spread, convolution, transposed_part


def by_place(points, run, *halves):
    for place in range(points):
        owners = [(place - k) % points for k in range(points)]
        lists = [[parts[k] for k in owners] for parts in halves]
        pl.when(lax.axis_index("path") == place)(functools.partial(run, place, *lists))


def channel_parts(depth):
    return [(at, min(at + 2 * LANES, depth)) for at in range(0, depth, 2 * LANES)]


def slopes_of_class(order, got, first_halves, first_bias, second_halves, second_bias, sizes):
    group_lon, group_lat, row_part, col_part = sizes
    points, depth = len(first_halves), got.shape[-1]
    rows, cols, part = group_lon * row_part, group_lat * col_part, row_part * col_part
    cells = rows * cols

    def kernel(order, got, first_bias, second_bias, *refs):
        first_slope, second_slope, edged, near_taps, far_taps = refs[2 * points :]

        def run(place, first, second):
            spread, convolution, _ = class_tools(sizes, depth, edged)
            field = jnp.dot(order[...], got[:, :part, :].reshape(cells, depth), preferred_element_type=F32)
            spread(field, 1, 0, near_taps)
            act, first_slope[...] = gelu_and_slope(convolution(near_taps, first, 1) + first_bias[...].reshape(1, -1))
            spread(field + act, FAR // NEAR, 0, far_taps)
            pre = convolution(far_taps, second, FAR // NEAR) + second_bias[...].reshape(1, -1)
            second_slope[...] = gelu_and_slope(pre)[1]

        by_place(points, run, refs[:points], refs[points : 2 * points])

    return call(
        kernel,
        [((cells, depth), F32)] * 2,
        [pltpu.VMEM((cols, rows + 2 * EDGE, depth), F32)] + [pltpu.VMEM((cells, 3 * depth), BF16)] * 2,
        "slopes_of_class",
        16,
        order,
        got,
        first_bias,
        second_bias,
        *first_halves,
        *second_halves,
    )


def adjoint_of_class(order, cotangents, first_slope, second_slope, first_halves, second_halves, sizes):
    group_lon, group_lat, row_part, col_part = sizes
    points, depth = len(first_halves), first_slope.shape[-1]
    rows, cols = group_lon * row_part, group_lat * col_part
    cells, part = rows * cols, row_part // points * col_part

    def kernel(order, first_slope, second_slope, *refs):
        sent, edged, near_taps, far_taps, grad = refs[3 * points :]

        def run(place, cotangent, first, second):
            spread, _, transposed_part = class_tools(sizes, depth, edged)
            upstream = jnp.concatenate([share[...].astype(F32) for share in cotangent], axis=1)
            upstream = jnp.dot(order[...], upstream.reshape(cells, depth).astype(BF16), preferred_element_type=F32)
            spread(second_slope[...] * upstream, FAR // NEAR, 0, far_taps)
            for at, end in channel_parts(depth):
                hidden_adj = upstream[:, at:end] + transposed_part(far_taps, second, FAR // NEAR, at, end)
                grad[:, at:end] = hidden_adj
                spread(first_slope[:, at:end] * hidden_adj, 1, at, near_taps)
            home = ordering((group_lat, col_part, group_lon, row_part), (2, 0, 3, 1))
            for at, end in channel_parts(depth):
                grad[:, at:end] += transposed_part(near_taps, first, 1, at, end)
            moved = jnp.dot(home, grad[...].astype(BF16), preferred_element_type=F32)
            sent[...] = moved.reshape(cells // part, part, depth).astype(BF16)

        by_place(points, run, refs[:points], refs[points : 2 * points], refs[2 * points : 3 * points])

    return call(
        kernel,
        [((cells // part, part, depth), BF16)],
        [pltpu.VMEM((cols, rows + 2 * EDGE, depth), F32)]
        + [pltpu.VMEM((cells, 3 * depth), BF16)] * 2
        + [pltpu.VMEM((cells, depth), F32)],
        "adjoint_of_class",
        16,
        order,
        first_slope,
        second_slope,
        *cotangents,
        *first_halves,
        *second_halves,
    )[0]


def attribution_rows(home, diff_rows, rows, cols):
    points, depth = lax.axis_size("path"), home.shape[-1]
    cells = rows * cols

    def kernel(home, diff_rows, out):
        order = ordering((NEAR, NEAR, points, rows // NEAR, cols // NEAR), (2, 3, 0, 4, 1))
        order = sum(order[k * cells : (k + 1) * cells] for k in range(points))
        values = home[...].astype(F32).reshape(points * cells, depth).astype(BF16)
        moved = jnp.dot(order, values, preferred_element_type=F32)
        out[...] = (diff_rows[...] * moved).reshape(rows, cols, depth).astype(BF16)

    return call(kernel, [((rows, cols, depth), BF16)], [], "attribution_rows", 4, home, diff_rows)[0]


def one_group(observed, baseline, cotangent, first_weight, first_bias, second_weight, second_bias):
    rows, cols, depth = observed.shape
    points = lax.axis_size("path")
    sizes = group_sizes() + (rows // NEAR, cols // NEAR)

    def turned(values, step):
        return lax.ppermute(values, "path", [(i, (i + step) % points) for i in range(points)])

    side = math.isqrt(first_weight.shape[0])
    halves = [
        [x.reshape((side, side) + x.shape[1:]) for x in [part] + [turned(part, step) for step in range(1, points)]]
        for part in (first_weight, second_weight)
    ]
    to_classes, to_grid = row_orders(rows, cols, sizes)
    sent, diff_rows = pack_classes(to_classes, observed, baseline, cotangent)
    got = swap(sent)
    own = got[:, sizes[2] * sizes[3] :, :]
    cotangents = [own] + [turned(own, step) for step in range(1, points)]
    first_slope, second_slope = slopes_of_class(to_grid, got, halves[0], first_bias, halves[1], second_bias, sizes)
    grad = adjoint_of_class(to_grid, cotangents, first_slope, second_slope, *halves, sizes)
    home = lax.all_to_all(grad, ("lon", "lat", "path"), 0, 0, tiled=True)
    return attribution_rows(home, diff_rows, rows // points, cols)


def several_groups(observed, baseline, cotangent, first_weight, first_bias, second_weight, second_bias):
    rows, cols, depth = observed.shape
    points, point = lax.axis_size("path"), lax.axis_index("path")
    group_lon, group_lat = group_sizes()
    row_part, col_part = rows // NEAR, cols // NEAR
    ring = [(i, (i + 1) % points) for i in range(points)]

    def whole_weight(part):
        held = jnp.zeros((part.shape[0], points) + part.shape[1:], part.dtype)
        for step in range(points):
            held = lax.dynamic_update_slice_in_dim(held, part[:, None], (point - step) % points, 1)
            if step < points - 1:
                part = lax.ppermute(part, "path", ring)
        return held.reshape(held.shape[0], -1, held.shape[3])

    first_full, second_full = whole_weight(first_weight), whole_weight(second_weight)
    diff = observed.astype(jnp.float32) - baseline.astype(jnp.float32)
    mix = (point.astype(jnp.float32) + 0.5) / points
    field = (baseline.astype(jnp.float32) + mix * diff).astype(jnp.bfloat16)
    sent = jnp.stack([to_classes(field), to_classes(cotangent)], axis=1)
    got = swap(sent).reshape(group_lon, group_lat, 2, row_part, col_part, depth)
    got = got.transpose(2, 0, 3, 1, 4, 5).reshape(2, group_lon * row_part, group_lat * col_part, depth)
    field, upstream = got[0], got[1].astype(jnp.float32)

    first_pre = stencil(field, first_full, 1, True) + first_bias
    hidden = (field.astype(jnp.float32) + smooth_act(first_pre)).astype(jnp.bfloat16)
    second_pre = stencil(hidden, second_full, FAR // NEAR, True) + second_bias
    second_adj = act_adjoint(second_pre, upstream).astype(jnp.bfloat16)
    hidden_adj = upstream + stencil(second_adj, second_full, FAR // NEAR, False)
    first_adj = act_adjoint(first_pre, hidden_adj).astype(jnp.bfloat16)
    grad = hidden_adj + stencil(first_adj, first_full, 1, False)

    part = row_part // points
    grad = grad.reshape(group_lon, points, part, group_lat, col_part, depth).transpose(1, 0, 3, 2, 4, 5)
    grad = grad.reshape(points, group_lon * group_lat, part, col_part, depth)
    total = lax.dynamic_index_in_dim(grad, point, 0, keepdims=False)
    for step in range(1, points):
        other = lax.dynamic_index_in_dim(grad, (point + step) % points, 0, keepdims=False)
        total = total + lax.ppermute(other, "path", [(i, (i + step) % points) for i in range(points)])
    home = swap(total.astype(jnp.bfloat16)).reshape(NEAR, NEAR, part, col_part, depth)
    home = home.transpose(2, 0, 3, 1, 4).reshape(rows // points, cols, depth).astype(jnp.float32)
    diff_rows = lax.dynamic_slice_in_dim(diff, point * (rows // points), rows // points, 0)
    return (diff_rows * home / points).astype(jnp.bfloat16)


def shards(*args):
    if group_sizes() == (lax.axis_size("lon"), lax.axis_size("lat")):
        return one_group(*args)
    return several_groups(*args)


def solution(mesh):
    placed = (
        P("lon", "lat", None),
        P("lon", "lat", None),
        P("lon", "lat", None),
        P(None, "path", None),
        P(),
        P(None, "path", None),
        P(),
    )
    return jax.shard_map(
        shards,
        mesh=mesh,
        in_specs=placed,
        out_specs=P(("lon", "path"), "lat", None),
        check_vma=False,
    )
```

```python
import functools
import math

import jax
import jax.numpy as jnp
from jax import lax
from jax.experimental import pallas as pl
from jax.experimental.pallas import tpu as pltpu
from jax.sharding import PartitionSpec as P

NEAR = 4
FAR = 16
EDGE = 8
LANES = 128
F32, BF16 = jnp.float32, jnp.bfloat16
VMEM = pl.BlockSpec(memory_space=pltpu.VMEM)
AHEAD = 4 * 10**9


def smooth_act(value):
    return jax.nn.gelu(value, approximate=True)


def act_adjoint(pre_value, upstream):
    unused, pullback = jax.vjp(smooth_act, pre_value)
    return pullback(upstream)[0]


def group_sizes():
    lat = math.gcd(lax.axis_size("lat"), NEAR * NEAR)
    return NEAR * NEAR // lat, lat


def swap(chunks):
    group_lon, group_lat = group_sizes()
    lon, lat = lax.axis_size("lon"), lax.axis_size("lat")
    if (lon, lat) == (group_lon, group_lat):
        return lax.all_to_all(chunks, ("lon", "lat"), 0, 0, tiled=True)
    chunks = chunks.reshape((group_lon, group_lat) + chunks.shape[1:])
    for axis, dim, size in (("lon", 0, group_lon), ("lat", 1, group_lat)):
        count = lax.axis_size(axis)
        groups = [list(range(i, i + size)) for i in range(0, count, size)]
        chunks = lax.all_to_all(chunks, axis, dim, dim, tiled=True, axis_index_groups=groups)
    return chunks.reshape((group_lon * group_lat,) + chunks.shape[2:])


def to_classes(cells):
    rows, cols, depth = cells.shape
    cells = cells.reshape(rows // NEAR, NEAR, cols // NEAR, NEAR, depth).transpose(1, 3, 0, 2, 4)
    return cells.reshape(NEAR * NEAR, rows // NEAR, cols // NEAR, depth)


def padded(cells, width):
    for axis, dim, step in zip(("lon", "lat"), (0, 1), group_sizes()):
        count = lax.axis_size(axis)
        head = lax.slice_in_dim(cells, 0, width, axis=dim)
        tail = lax.slice_in_dim(cells, cells.shape[dim] - width, cells.shape[dim], axis=dim)
        if count == step:
            before, after = jnp.zeros_like(tail), jnp.zeros_like(head)
        else:
            before = lax.ppermute(tail, axis, [(i, i + step) for i in range(count - step)])
            after = lax.ppermute(head, axis, [(i + step, i) for i in range(count - step)])
        cells = jnp.concatenate([before, cells, after], axis=dim)
    return cells


def stencil(cells, weights, step, forward):
    rows, cols, depth = cells.shape
    around = padded(cells, step)
    total = jnp.zeros((rows, cols, depth), jnp.float32)
    for tap in range(9):
        sign = step if forward else -step
        row, col = step + (tap // 3 - 1) * sign, step + (tap % 3 - 1) * sign
        window = around[row : row + rows, col : col + cols]
        dims = (((2,), (0 if forward else 1,)), ((), ()))
        total = total + lax.dot_general(window, weights[tap], dims, preferred_element_type=jnp.float32)
    return total


def ordering(dims, axes):
    cells = math.prod(dims)
    place = lax.broadcasted_iota(jnp.int32, (cells, 1), 0)
    source, stride = jnp.zeros((cells, 1), jnp.int32), 1
    for axis in reversed(axes):
        source += lax.rem(lax.div(place, jnp.int32(stride)), jnp.int32(dims[axis])) * math.prod(dims[axis + 1 :])
        stride *= dims[axis]
    return (lax.broadcasted_iota(jnp.int32, (cells, cells), 1) == source).astype(F32).astype(BF16)


def gelu_and_slope(value):
    scale, cubic = math.sqrt(2 / math.pi), 0.044715
    square = value * value
    bent = jnp.tanh(scale * value * (1 + cubic * square))
    half = 0.5 * (1 + bent)
    return value * half, half + 0.5 * value * (1 - bent * bent) * (scale * (1 + 3 * cubic * square))


def call(kernel, outs, scratch, name, megabytes, *args, flops=0):
    args = [pltpu.with_memory_space_constraint(x, pltpu.VMEM) for x in args]
    size = sum(x.size * x.dtype.itemsize for x in args)
    return pl.pallas_call(
        kernel,
        out_shape=[pltpu.VMEM(shape, dtype) for shape, dtype in outs],
        in_specs=[VMEM] * len(args),
        out_specs=[VMEM] * len(outs),
        scratch_shapes=scratch,
        compiler_params=pltpu.CompilerParams(vmem_limit_bytes=megabytes << 20),
        cost_estimate=pl.CostEstimate(flops=flops, bytes_accessed=size, transcendentals=0),
        name=name,
    )(*args)


def row_orders(rows, cols, sizes):
    group_lon, group_lat, row_part, col_part = sizes
    cells = rows * cols

    def kernel(to_classes, to_grid):
        to_classes[...] = ordering((row_part, NEAR, col_part, NEAR), (1, 3, 0, 2))
        to_grid[...] = ordering((group_lon, group_lat, row_part, col_part), (1, 3, 0, 2))

    return call(kernel, [((cells, cells), BF16)] * 2, [], "row_orders", 4, flops=AHEAD)


def pack_classes(order, observed, baseline, cotangent):
    rows, cols, depth = observed.shape
    points = lax.axis_size("path")
    cells, part = rows * cols, rows * cols // (NEAR * NEAR)

    def kernel(order, observed, baseline, cotangent, sent, diff_rows):
        mine = lax.axis_index("path")
        mix = (mine.astype(F32) + 0.5) / points
        base = baseline[...].astype(F32)
        diff = observed[...].astype(F32) - base
        field = (base + mix * diff).astype(BF16)
        moved = jnp.dot(order[...], field, preferred_element_type=F32)
        sent[:, :part, :] = moved.reshape(NEAR * NEAR, part, depth).astype(BF16)
        moved = jnp.dot(order[...], cotangent[...], preferred_element_type=F32)
        moved = moved.reshape(NEAR * NEAR, points, part // points, depth)
        own = moved[:, 0]
        for k in range(1, points):
            own = jnp.where(mine == k, moved[:, k], own)
        sent[:, part:, :] = own.astype(BF16)
        half = pl.ds(pl.multiple_of(mine * (cells // points), cells // points), cells // points)
        diff_rows[...] = (observed[half, :].astype(F32) - baseline[half, :].astype(F32)) * (1 / points)

    return call(
        kernel,
        [((NEAR * NEAR, part + part // points, depth), BF16), ((cells // points, depth), F32)],
        [],
        "pack_classes",
        8,
        order,
        *(x.reshape(cells, depth) for x in (observed, baseline, cotangent)),
        flops=AHEAD,
    )


def class_tools(sizes, depth, edged):
    group_lon, group_lat, row_part, col_part = sizes
    rows, cols = group_lon * row_part, group_lat * col_part
    cells = rows * cols

    def spread(values, step, at, target):
        span = slice(at, at + values.shape[1])
        edged[:, EDGE : EDGE + rows, span] = values.reshape(cols, rows, -1)
        for i in range(3):
            start = EDGE + (i - 1) * step
            shifted = edged[:, start : start + rows, span].reshape(cells, -1)
            target[:, i * depth + at : i * depth + at + values.shape[1]] = shifted.astype(BF16)

    def convolution(source, weights, step):
        shift = step * rows

        def products(values, *columns):
            blocks = [
                jnp.concatenate([part[i, col] for i in range(3) for part in weights], axis=0) for col in columns
            ]
            joint = jnp.dot(values, jnp.concatenate(blocks, axis=1), preferred_element_type=F32)
            return [joint[:, i * depth : (i + 1) * depth] for i in range(len(columns))]

        if 2 * shift == cells:
            same_low, before = products(source[:shift, :], 1, 0)
            same_high, after = products(source[shift:, :], 1, 2)
            return jnp.concatenate([same_low + after, same_high + before], axis=0)
        before, same, after = products(source[...], 0, 1, 2)
        fill = jnp.zeros((shift, depth), F32)
        after = jnp.concatenate([after[shift:], fill], axis=0)
        return same + after + jnp.concatenate([fill, before[: cells - shift]], axis=0)

    def transposed_part(source, weights, step, at, end):
        def weigh(values, col):
            taps_of = [jnp.concatenate([part[2 - i, 2 - col] for part in weights], axis=0)[at:end] for i in range(3)]
            return lax.dot_general(
                values, jnp.concatenate(taps_of, axis=1), (((1,), (1,)), ((), ())), preferred_element_type=F32
            )

        shift = step * rows
        fill = jnp.zeros((shift, end - at), F32)
        same = weigh(source[...], 1)
        after = weigh(source[shift:, :], 2)
        before = weigh(source[: cells - shift, :], 0)
        return same + jnp.concatenate([after, fill], axis=0) + jnp.concatenate([fill, before], axis=0)

    edged[:, :EDGE, :] = jnp.zeros((cols, EDGE, depth), F32)
    edged[:, EDGE + rows :, :] = jnp.zeros((cols, EDGE, depth), F32)
    return spread, convolution, transposed_part


def by_place(points, run, *halves):
    for place in range(points):
        owners = [(place - k) % points for k in range(points)]
        lists = [[parts[k] for k in owners] for parts in halves]
        pl.when(lax.axis_index("path") == place)(functools.partial(run, place, *lists))


def channel_parts(depth):
    return [(at, min(at + 2 * LANES, depth)) for at in range(0, depth, 2 * LANES)]


def slopes_of_class(order, got, first_halves, first_bias, second_halves, second_bias, sizes):
    group_lon, group_lat, row_part, col_part = sizes
    points, depth = len(first_halves), got.shape[-1]
    rows, cols, part = group_lon * row_part, group_lat * col_part, row_part * col_part
    cells = rows * cols

    def kernel(order, got, first_bias, second_bias, *refs):
        first_slope, second_slope, edged, near_taps, far_taps = refs[2 * points :]

        def run(place, first, second):
            spread, convolution, _ = class_tools(sizes, depth, edged)
            field = jnp.dot(order[...], got[:, :part, :].reshape(cells, depth), preferred_element_type=F32)
            spread(field, 1, 0, near_taps)
            act, first_slope[...] = gelu_and_slope(convolution(near_taps, first, 1) + first_bias[...].reshape(1, -1))
            spread(field + act, FAR // NEAR, 0, far_taps)
            pre = convolution(far_taps, second, FAR // NEAR) + second_bias[...].reshape(1, -1)
            second_slope[...] = gelu_and_slope(pre)[1]

        by_place(points, run, refs[:points], refs[points : 2 * points])

    return call(
        kernel,
        [((cells, depth), F32)] * 2,
        [pltpu.VMEM((cols, rows + 2 * EDGE, depth), F32)] + [pltpu.VMEM((cells, 3 * depth), BF16)] * 2,
        "slopes_of_class",
        16,
        order,
        got,
        first_bias,
        second_bias,
        *first_halves,
        *second_halves,
    )


def adjoint_of_class(order, cotangents, first_slope, second_slope, first_halves, second_halves, sizes):
    group_lon, group_lat, row_part, col_part = sizes
    points, depth = len(first_halves), first_slope.shape[-1]
    rows, cols = group_lon * row_part, group_lat * col_part
    cells = rows * cols

    def kernel(order, first_slope, second_slope, *refs):
        sent, edged, near_taps, far_taps, grad = refs[3 * points :]

        def run(place, cotangent, first, second):
            spread, _, transposed_part = class_tools(sizes, depth, edged)
            upstream = jnp.concatenate([share[...].astype(F32) for share in cotangent], axis=1)
            upstream = jnp.dot(order[...], upstream.reshape(cells, depth).astype(BF16), preferred_element_type=F32)
            spread(second_slope[...] * upstream, FAR // NEAR, 0, far_taps)
            for at, end in channel_parts(depth):
                hidden_adj = upstream[:, at:end] + transposed_part(far_taps, second, FAR // NEAR, at, end)
                grad[:, at:end] = hidden_adj
                spread(first_slope[:, at:end] * hidden_adj, 1, at, near_taps)
            home = ordering((group_lat, col_part, group_lon, row_part), (2, 0, 3, 1))
            for at, end in channel_parts(depth):
                grad[:, at:end] += transposed_part(near_taps, first, 1, at, end)
            sent[...] = jnp.dot(home, grad[...].astype(BF16), preferred_element_type=F32).astype(BF16)

        by_place(points, run, refs[:points], refs[points : 2 * points], refs[2 * points : 3 * points])

    return call(
        kernel,
        [((cells, depth), BF16)],
        [pltpu.VMEM((cols, rows + 2 * EDGE, depth), F32)]
        + [pltpu.VMEM((cells, 3 * depth), BF16)] * 2
        + [pltpu.VMEM((cells, depth), F32)],
        "adjoint_of_class",
        16,
        order,
        first_slope,
        second_slope,
        *cotangents,
        *first_halves,
        *second_halves,
    )[0]


def attribution_rows(home, diff_rows, rows, cols):
    points, depth = lax.axis_size("path"), home.shape[-1]
    cells = rows * cols

    def kernel(home, diff_rows, out):
        order = ordering((NEAR, NEAR, points, rows // NEAR, cols // NEAR), (2, 3, 0, 4, 1))
        order = sum(order[k * cells : (k + 1) * cells] for k in range(points))
        moved = jnp.dot(order, home[...], preferred_element_type=F32)
        out[...] = (diff_rows[...] * moved).reshape(rows, cols, depth).astype(BF16)

    return call(kernel, [((rows, cols, depth), BF16)], [], "attribution_rows", 4, home, diff_rows)[0]


def one_group(observed, baseline, cotangent, first_weight, first_bias, second_weight, second_bias):
    rows, cols, depth = observed.shape
    points = lax.axis_size("path")
    sizes = group_sizes() + (rows // NEAR, cols // NEAR)

    def turned(values, step):
        return lax.ppermute(values, "path", [(i, (i + step) % points) for i in range(points)])

    side = math.isqrt(first_weight.shape[0])
    halves = [
        [x.reshape((side, side) + x.shape[1:]) for x in [part] + [turned(part, step) for step in range(1, points)]]
        for part in (first_weight, second_weight)
    ]
    to_classes, to_grid = row_orders(rows, cols, sizes)
    sent, diff_rows = pack_classes(to_classes, observed, baseline, cotangent)
    got = swap(sent)
    own = got[:, sizes[2] * sizes[3] :, :]
    cotangents = [own] + [turned(own, step) for step in range(1, points)]
    first_slope, second_slope = slopes_of_class(to_grid, got, halves[0], first_bias, halves[1], second_bias, sizes)
    grad = adjoint_of_class(to_grid, cotangents, first_slope, second_slope, *halves, sizes)
    chunks = grad.reshape(NEAR * NEAR * points, -1, depth)
    home = lax.all_to_all(chunks, ("lon", "lat", "path"), 0, 0, tiled=True)
    return attribution_rows(home.reshape(grad.shape), diff_rows, rows // points, cols)


def several_groups(observed, baseline, cotangent, first_weight, first_bias, second_weight, second_bias):
    rows, cols, depth = observed.shape
    points, point = lax.axis_size("path"), lax.axis_index("path")
    group_lon, group_lat = group_sizes()
    row_part, col_part = rows // NEAR, cols // NEAR
    ring = [(i, (i + 1) % points) for i in range(points)]

    def whole_weight(part):
        held = jnp.zeros((part.shape[0], points) + part.shape[1:], part.dtype)
        for step in range(points):
            held = lax.dynamic_update_slice_in_dim(held, part[:, None], (point - step) % points, 1)
            if step < points - 1:
                part = lax.ppermute(part, "path", ring)
        return held.reshape(held.shape[0], -1, held.shape[3])

    first_full, second_full = whole_weight(first_weight), whole_weight(second_weight)
    diff = observed.astype(jnp.float32) - baseline.astype(jnp.float32)
    mix = (point.astype(jnp.float32) + 0.5) / points
    field = (baseline.astype(jnp.float32) + mix * diff).astype(jnp.bfloat16)
    sent = jnp.stack([to_classes(field), to_classes(cotangent)], axis=1)
    got = swap(sent).reshape(group_lon, group_lat, 2, row_part, col_part, depth)
    got = got.transpose(2, 0, 3, 1, 4, 5).reshape(2, group_lon * row_part, group_lat * col_part, depth)
    field, upstream = got[0], got[1].astype(jnp.float32)

    first_pre = stencil(field, first_full, 1, True) + first_bias
    hidden = (field.astype(jnp.float32) + smooth_act(first_pre)).astype(jnp.bfloat16)
    second_pre = stencil(hidden, second_full, FAR // NEAR, True) + second_bias
    second_adj = act_adjoint(second_pre, upstream).astype(jnp.bfloat16)
    hidden_adj = upstream + stencil(second_adj, second_full, FAR // NEAR, False)
    first_adj = act_adjoint(first_pre, hidden_adj).astype(jnp.bfloat16)
    grad = hidden_adj + stencil(first_adj, first_full, 1, False)

    part = row_part // points
    grad = grad.reshape(group_lon, points, part, group_lat, col_part, depth).transpose(1, 0, 3, 2, 4, 5)
    grad = grad.reshape(points, group_lon * group_lat, part, col_part, depth)
    total = lax.dynamic_index_in_dim(grad, point, 0, keepdims=False)
    for step in range(1, points):
        other = lax.dynamic_index_in_dim(grad, (point + step) % points, 0, keepdims=False)
        total = total + lax.ppermute(other, "path", [(i, (i + step) % points) for i in range(points)])
    home = swap(total.astype(jnp.bfloat16)).reshape(NEAR, NEAR, part, col_part, depth)
    home = home.transpose(2, 0, 3, 1, 4).reshape(rows // points, cols, depth).astype(jnp.float32)
    diff_rows = lax.dynamic_slice_in_dim(diff, point * (rows // points), rows // points, 0)
    return (diff_rows * home / points).astype(jnp.bfloat16)


def shards(*args):
    if group_sizes() == (lax.axis_size("lon"), lax.axis_size("lat")):
        return one_group(*args)
    return several_groups(*args)


def solution(mesh):
    placed = (
        P("lon", "lat", None),
        P("lon", "lat", None),
        P("lon", "lat", None),
        P(None, "path", None),
        P(),
        P(None, "path", None),
        P(),
    )
    return jax.shard_map(
        shards,
        mesh=mesh,
        in_specs=placed,
        out_specs=P(("lon", "path"), "lat", None),
        check_vma=False,
    )
```

```python
import functools
import math

import jax
import jax.numpy as jnp
import numpy as np
from jax import lax
from jax.experimental import pallas as pl
from jax.experimental.pallas import tpu as pltpu
from jax.sharding import PartitionSpec as P

NEAR = 4
FAR = 16
EDGE = 8
LANES = 128
F32, BF16 = jnp.float32, jnp.bfloat16
VMEM = pl.BlockSpec(memory_space=pltpu.VMEM)
AHEAD = 4 * 10**9


def smooth_act(value):
    return jax.nn.gelu(value, approximate=True)


def act_adjoint(pre_value, upstream):
    unused, pullback = jax.vjp(smooth_act, pre_value)
    return pullback(upstream)[0]


def group_sizes():
    lat = math.gcd(lax.axis_size("lat"), NEAR * NEAR)
    return NEAR * NEAR // lat, lat


def swap(chunks):
    group_lon, group_lat = group_sizes()
    lon, lat = lax.axis_size("lon"), lax.axis_size("lat")
    if (lon, lat) == (group_lon, group_lat):
        return lax.all_to_all(chunks, ("lon", "lat"), 0, 0, tiled=True)
    chunks = chunks.reshape((group_lon, group_lat) + chunks.shape[1:])
    for axis, dim, size in (("lon", 0, group_lon), ("lat", 1, group_lat)):
        count = lax.axis_size(axis)
        groups = [list(range(i, i + size)) for i in range(0, count, size)]
        chunks = lax.all_to_all(chunks, axis, dim, dim, tiled=True, axis_index_groups=groups)
    return chunks.reshape((group_lon * group_lat,) + chunks.shape[2:])


def lon_parts():
    group_lon = group_sizes()[0]
    fast = 2 if group_lon % 2 == 0 else 1
    slow = group_lon // fast
    bits = slow.bit_length() - 1
    listing = [sum(((i ^ (i >> 1)) >> b & 1) << (bits - 1 - b) for b in range(bits)) for i in range(slow)]
    return slow, fast, listing


def listed(points):
    slow, fast, listing = lon_parts()
    lat, path = lax.axis_size("lat"), lax.axis_size("path")
    grid = np.arange(slow * fast * lat * path).reshape(slow, fast, lat, path)[listing]
    if points:
        return [grid.transpose(1, 2, 3, 0).reshape(-1).tolist()]
    return [grid[..., p].transpose(1, 2, 0).reshape(-1).tolist() for p in range(path)]


def swap_listed(chunks, points):
    return lax.all_to_all(chunks, ("lon", "lat", "path"), 0, 0, tiled=True, axis_index_groups=listed(points))


def to_classes(cells):
    rows, cols, depth = cells.shape
    cells = cells.reshape(rows // NEAR, NEAR, cols // NEAR, NEAR, depth).transpose(1, 3, 0, 2, 4)
    return cells.reshape(NEAR * NEAR, rows // NEAR, cols // NEAR, depth)


def padded(cells, width):
    for axis, dim, step in zip(("lon", "lat"), (0, 1), group_sizes()):
        count = lax.axis_size(axis)
        head = lax.slice_in_dim(cells, 0, width, axis=dim)
        tail = lax.slice_in_dim(cells, cells.shape[dim] - width, cells.shape[dim], axis=dim)
        if count == step:
            before, after = jnp.zeros_like(tail), jnp.zeros_like(head)
        else:
            before = lax.ppermute(tail, axis, [(i, i + step) for i in range(count - step)])
            after = lax.ppermute(head, axis, [(i + step, i) for i in range(count - step)])
        cells = jnp.concatenate([before, cells, after], axis=dim)
    return cells


def stencil(cells, weights, step, forward):
    rows, cols, depth = cells.shape
    around = padded(cells, step)
    total = jnp.zeros((rows, cols, depth), jnp.float32)
    for tap in range(9):
        sign = step if forward else -step
        row, col = step + (tap // 3 - 1) * sign, step + (tap % 3 - 1) * sign
        window = around[row : row + rows, col : col + cols]
        dims = (((2,), (0 if forward else 1,)), ((), ()))
        total = total + lax.dot_general(window, weights[tap], dims, preferred_element_type=jnp.float32)
    return total


def digit(place, stride, size):
    if size & (size - 1) or stride & (stride - 1):
        return lax.rem(lax.div(place, jnp.int32(stride)), jnp.int32(size))
    return lax.shift_right_logical(place, jnp.int32(stride.bit_length() - 1)) & (size - 1)


def ordering(dims, axes, listing=(None, ())):
    cells, runs = math.prod(dims), []
    for axis in axes:
        if runs and runs[-1][-1] == axis - 1 and listing[0] not in (axis, axis - 1):
            runs[-1].append(axis)
        else:
            runs.append([axis])
    place = lax.broadcasted_iota(jnp.int32, (cells, 1), 0)
    source, stride = jnp.zeros((cells, 1), jnp.int32), 1
    for run in reversed(runs):
        size = math.prod(dims[axis] for axis in run)
        here = digit(place, stride, size)
        if run == [listing[0]]:
            here = sum(jnp.where(here == i, value, 0) for i, value in enumerate(listing[1]) if value)
        source += here * math.prod(dims[run[-1] + 1 :])
        stride *= size
    return (lax.broadcasted_iota(jnp.int32, (cells, cells), 1) == source).astype(F32).astype(BF16)


def gelu_and_slope(value):
    scale, cubic = math.sqrt(2 / math.pi), 0.044715
    square = value * value
    bent = jnp.tanh(scale * value * (1 + cubic * square))
    half = 0.5 * (1 + bent)
    return value * half, half + 0.5 * value * (1 - bent * bent) * (scale * (1 + 3 * cubic * square))


def call(kernel, outs, scratch, name, megabytes, *args, flops=0):
    args = [pltpu.with_memory_space_constraint(x, pltpu.VMEM) for x in args]
    size = sum(x.size * x.dtype.itemsize for x in args)
    return pl.pallas_call(
        kernel,
        out_shape=[pltpu.VMEM(shape, dtype) for shape, dtype in outs],
        in_specs=[VMEM] * len(args),
        out_specs=[VMEM] * len(outs),
        scratch_shapes=scratch,
        compiler_params=pltpu.CompilerParams(vmem_limit_bytes=megabytes << 20),
        cost_estimate=pl.CostEstimate(flops=flops, bytes_accessed=size, transcendentals=0),
        name=name,
    )(*args)


def row_orders(rows, cols, sizes):
    group_lon, group_lat, row_part, col_part = sizes
    cells = rows * cols

    def kernel(to_classes, to_grid):
        to_classes[...] = ordering((row_part, NEAR, col_part, NEAR), (1, 3, 0, 2))
        slow, fast, listing = lon_parts()
        found = [listing.index(i) for i in range(slow)]
        to_grid[...] = ordering((fast, group_lat, slow, row_part, col_part), (1, 4, 2, 0, 3), (2, found))

    return call(kernel, [((cells, cells), BF16)] * 2, [], "row_orders", 4, flops=AHEAD)


def pack_classes(order, observed, baseline, cotangent):
    rows, cols, depth = observed.shape
    points = lax.axis_size("path")
    cells, part = rows * cols, rows * cols // (NEAR * NEAR)

    def kernel(order, observed, baseline, cotangent, sent, diff_rows):
        mine = lax.axis_index("path")
        mix = (mine.astype(F32) + 0.5) / points
        base = baseline[...].astype(F32)
        diff = observed[...].astype(F32) - base
        field = (base + mix * diff).astype(BF16)
        moved = jnp.dot(order[...], field, preferred_element_type=F32)
        sent[:, :part, :] = moved.reshape(NEAR * NEAR, part, depth).astype(BF16)
        moved = jnp.dot(order[...], cotangent[...], preferred_element_type=F32)
        moved = moved.reshape(NEAR * NEAR, points, part // points, depth)
        own = moved[:, 0]
        for k in range(1, points):
            own = jnp.where(mine == k, moved[:, k], own)
        sent[:, part:, :] = own.astype(BF16)
        half = pl.ds(pl.multiple_of(mine * (cells // points), cells // points), cells // points)
        diff_rows[...] = (observed[half, :].astype(F32) - baseline[half, :].astype(F32)) * (1 / points)

    return call(
        kernel,
        [((NEAR * NEAR, part + part // points, depth), BF16), ((cells // points, depth), F32)],
        [],
        "pack_classes",
        8,
        order,
        *(x.reshape(cells, depth) for x in (observed, baseline, cotangent)),
        flops=AHEAD,
    )


def class_tools(sizes, depth, edged):
    group_lon, group_lat, row_part, col_part = sizes
    rows, cols = group_lon * row_part, group_lat * col_part
    cells = rows * cols

    def spread(values, step, at, target):
        span = slice(at, at + values.shape[1])
        edged[:, EDGE : EDGE + rows, span] = values.reshape(cols, rows, -1)
        for i in range(3):
            start = EDGE + (i - 1) * step
            shifted = edged[:, start : start + rows, span].reshape(cells, -1)
            target[:, i * depth + at : i * depth + at + values.shape[1]] = shifted.astype(BF16)

    def convolution(source, weights, step):
        shift = step * rows

        def products(values, *columns):
            blocks = [
                jnp.concatenate([part[i, col] for i in range(3) for part in weights], axis=0) for col in columns
            ]
            joint = jnp.dot(values, jnp.concatenate(blocks, axis=1), preferred_element_type=F32)
            return [joint[:, i * depth : (i + 1) * depth] for i in range(len(columns))]

        if 2 * shift == cells:
            same_low, before = products(source[:shift, :], 1, 0)
            same_high, after = products(source[shift:, :], 1, 2)
            return jnp.concatenate([same_low + after, same_high + before], axis=0)
        before, same, after = products(source[...], 0, 1, 2)
        fill = jnp.zeros((shift, depth), F32)
        after = jnp.concatenate([after[shift:], fill], axis=0)
        return same + after + jnp.concatenate([fill, before[: cells - shift]], axis=0)

    def transposed_part(source, weights, step, at, end):
        def weigh(values, col):
            taps_of = [jnp.concatenate([part[2 - i, 2 - col] for part in weights], axis=0)[at:end] for i in range(3)]
            return lax.dot_general(
                values, jnp.concatenate(taps_of, axis=1), (((1,), (1,)), ((), ())), preferred_element_type=F32
            )

        shift = step * rows
        fill = jnp.zeros((shift, end - at), F32)
        same = weigh(source[...], 1)
        after = weigh(source[shift:, :], 2)
        before = weigh(source[: cells - shift, :], 0)
        return same + jnp.concatenate([after, fill], axis=0) + jnp.concatenate([fill, before], axis=0)

    edged[:, :EDGE, :] = jnp.zeros((cols, EDGE, depth), F32)
    edged[:, EDGE + rows :, :] = jnp.zeros((cols, EDGE, depth), F32)
    return spread, convolution, transposed_part


def by_place(points, run, *halves):
    for place in range(points):
        owners = [(place - k) % points for k in range(points)]
        lists = [[parts[k] for k in owners] for parts in halves]
        pl.when(lax.axis_index("path") == place)(functools.partial(run, place, *lists))


def channel_parts(depth):
    return [(at, min(at + 2 * LANES, depth)) for at in range(0, depth, 2 * LANES)]


def slopes_of_class(order, got, first_halves, first_bias, second_halves, second_bias, sizes):
    group_lon, group_lat, row_part, col_part = sizes
    points, depth = len(first_halves), got.shape[-1]
    rows, cols, part = group_lon * row_part, group_lat * col_part, row_part * col_part
    cells = rows * cols

    def kernel(order, got, first_bias, second_bias, *refs):
        first_slope, second_slope, edged, near_taps, far_taps = refs[2 * points :]

        def run(place, first, second):
            spread, convolution, _ = class_tools(sizes, depth, edged)
            field = jnp.dot(order[...], got[:, :part, :].reshape(cells, depth), preferred_element_type=F32)
            spread(field, 1, 0, near_taps)
            act, first_slope[...] = gelu_and_slope(convolution(near_taps, first, 1) + first_bias[...].reshape(1, -1))
            spread(field + act, FAR // NEAR, 0, far_taps)
            pre = convolution(far_taps, second, FAR // NEAR) + second_bias[...].reshape(1, -1)
            second_slope[...] = gelu_and_slope(pre)[1]

        by_place(points, run, refs[:points], refs[points : 2 * points])

    return call(
        kernel,
        [((cells, depth), F32)] * 2,
        [pltpu.VMEM((cols, rows + 2 * EDGE, depth), F32)] + [pltpu.VMEM((cells, 3 * depth), BF16)] * 2,
        "slopes_of_class",
        16,
        order,
        got,
        first_bias,
        second_bias,
        *first_halves,
        *second_halves,
    )


def adjoint_of_class(order, cotangents, first_slope, second_slope, first_halves, second_halves, sizes):
    group_lon, group_lat, row_part, col_part = sizes
    points, depth = len(first_halves), first_slope.shape[-1]
    rows, cols = group_lon * row_part, group_lat * col_part
    cells = rows * cols

    def kernel(order, first_slope, second_slope, *refs):
        sent, edged, near_taps, far_taps, grad = refs[3 * points :]

        def run(place, cotangent, first, second):
            spread, _, transposed_part = class_tools(sizes, depth, edged)
            upstream = jnp.concatenate([share[...].astype(F32) for share in cotangent], axis=1)
            upstream = jnp.dot(order[...], upstream.reshape(cells, depth).astype(BF16), preferred_element_type=F32)
            spread(second_slope[...] * upstream, FAR // NEAR, 0, far_taps)
            for at, end in channel_parts(depth):
                hidden_adj = upstream[:, at:end] + transposed_part(far_taps, second, FAR // NEAR, at, end)
                grad[:, at:end] = hidden_adj
                spread(first_slope[:, at:end] * hidden_adj, 1, at, near_taps)
            slow, fast, listing = lon_parts()
            dims = (group_lat, col_part, slow, fast, points, row_part // points)
            home = ordering(dims, (3, 0, 4, 2, 5, 1), (2, listing))
            for at, end in channel_parts(depth):
                grad[:, at:end] += transposed_part(near_taps, first, 1, at, end)
            sent[...] = jnp.dot(home, grad[...].astype(BF16), preferred_element_type=F32).astype(BF16)

        by_place(points, run, refs[:points], refs[points : 2 * points], refs[2 * points : 3 * points])

    return call(
        kernel,
        [((cells, depth), BF16)],
        [pltpu.VMEM((cols, rows + 2 * EDGE, depth), F32)]
        + [pltpu.VMEM((cells, 3 * depth), BF16)] * 2
        + [pltpu.VMEM((cells, depth), F32)],
        "adjoint_of_class",
        16,
        order,
        first_slope,
        second_slope,
        *cotangents,
        *first_halves,
        *second_halves,
    )[0]


def attribution_rows(home, diff_rows, rows, cols):
    points, depth = lax.axis_size("path"), home.shape[-1]
    cells, group_lat = rows * cols, group_sizes()[1]

    def kernel(home, diff_rows, out):
        bits, ahead = (NEAR * NEAR).bit_length() - 1, (group_lat * lon_parts()[1]).bit_length() - 1
        of_class = tuple(i + (i >= ahead) for i in range(bits))
        dims = (2,) * ahead + (points,) + (2,) * (bits - ahead) + (rows // NEAR, cols // NEAR)
        row_bits, col_bits = of_class[: bits // 2], of_class[bits // 2 :]
        order = ordering(dims, (ahead, bits + 1) + row_bits + (bits + 2,) + col_bits)
        order = sum(order[k * cells : (k + 1) * cells] for k in range(points))
        moved = jnp.dot(order, home[...], preferred_element_type=F32)
        out[...] = (diff_rows[...] * moved).reshape(rows, cols, depth).astype(BF16)

    return call(kernel, [((rows, cols, depth), BF16)], [], "attribution_rows", 4, home, diff_rows)[0]


def one_group(observed, baseline, cotangent, first_weight, first_bias, second_weight, second_bias):
    rows, cols, depth = observed.shape
    points = lax.axis_size("path")
    sizes = group_sizes() + (rows // NEAR, cols // NEAR)

    def turned(values, step):
        return lax.ppermute(values, "path", [(i, (i + step) % points) for i in range(points)])

    side = math.isqrt(first_weight.shape[0])
    halves = [
        [x.reshape((side, side) + x.shape[1:]) for x in [part] + [turned(part, step) for step in range(1, points)]]
        for part in (first_weight, second_weight)
    ]
    to_classes, to_grid = row_orders(rows, cols, sizes)
    sent, diff_rows = pack_classes(to_classes, observed, baseline, cotangent)
    got = swap_listed(sent, points=False)
    own = got[:, sizes[2] * sizes[3] :, :]
    cotangents = [own] + [turned(own, step) for step in range(1, points)]
    first_slope, second_slope = slopes_of_class(to_grid, got, halves[0], first_bias, halves[1], second_bias, sizes)
    grad = adjoint_of_class(to_grid, cotangents, first_slope, second_slope, *halves, sizes)
    chunks = grad.reshape(NEAR * NEAR * points, -1, depth)
    home = swap_listed(chunks, points=True)
    return attribution_rows(home.reshape(grad.shape), diff_rows, rows // points, cols)


def several_groups(observed, baseline, cotangent, first_weight, first_bias, second_weight, second_bias):
    rows, cols, depth = observed.shape
    points, point = lax.axis_size("path"), lax.axis_index("path")
    group_lon, group_lat = group_sizes()
    row_part, col_part = rows // NEAR, cols // NEAR
    ring = [(i, (i + 1) % points) for i in range(points)]

    def whole_weight(part):
        held = jnp.zeros((part.shape[0], points) + part.shape[1:], part.dtype)
        for step in range(points):
            held = lax.dynamic_update_slice_in_dim(held, part[:, None], (point - step) % points, 1)
            if step < points - 1:
                part = lax.ppermute(part, "path", ring)
        return held.reshape(held.shape[0], -1, held.shape[3])

    first_full, second_full = whole_weight(first_weight), whole_weight(second_weight)
    diff = observed.astype(jnp.float32) - baseline.astype(jnp.float32)
    mix = (point.astype(jnp.float32) + 0.5) / points
    field = (baseline.astype(jnp.float32) + mix * diff).astype(jnp.bfloat16)
    sent = jnp.stack([to_classes(field), to_classes(cotangent)], axis=1)
    got = swap(sent).reshape(group_lon, group_lat, 2, row_part, col_part, depth)
    got = got.transpose(2, 0, 3, 1, 4, 5).reshape(2, group_lon * row_part, group_lat * col_part, depth)
    field, upstream = got[0], got[1].astype(jnp.float32)

    first_pre = stencil(field, first_full, 1, True) + first_bias
    hidden = (field.astype(jnp.float32) + smooth_act(first_pre)).astype(jnp.bfloat16)
    second_pre = stencil(hidden, second_full, FAR // NEAR, True) + second_bias
    second_adj = act_adjoint(second_pre, upstream).astype(jnp.bfloat16)
    hidden_adj = upstream + stencil(second_adj, second_full, FAR // NEAR, False)
    first_adj = act_adjoint(first_pre, hidden_adj).astype(jnp.bfloat16)
    grad = hidden_adj + stencil(first_adj, first_full, 1, False)

    part = row_part // points
    grad = grad.reshape(group_lon, points, part, group_lat, col_part, depth).transpose(1, 0, 3, 2, 4, 5)
    grad = grad.reshape(points, group_lon * group_lat, part, col_part, depth)
    total = lax.dynamic_index_in_dim(grad, point, 0, keepdims=False)
    for step in range(1, points):
        other = lax.dynamic_index_in_dim(grad, (point + step) % points, 0, keepdims=False)
        total = total + lax.ppermute(other, "path", [(i, (i + step) % points) for i in range(points)])
    home = swap(total.astype(jnp.bfloat16)).reshape(NEAR, NEAR, part, col_part, depth)
    home = home.transpose(2, 0, 3, 1, 4).reshape(rows // points, cols, depth).astype(jnp.float32)
    diff_rows = lax.dynamic_slice_in_dim(diff, point * (rows // points), rows // points, 0)
    return (diff_rows * home / points).astype(jnp.bfloat16)


def shards(*args):
    if group_sizes() == (lax.axis_size("lon"), lax.axis_size("lat")):
        return one_group(*args)
    return several_groups(*args)


def solution(mesh):
    placed = (
        P("lon", "lat", None),
        P("lon", "lat", None),
        P("lon", "lat", None),
        P(None, "path", None),
        P(),
        P(None, "path", None),
        P(),
    )
    return jax.shard_map(
        shards,
        mesh=mesh,
        in_specs=placed,
        out_specs=P(("lon", "path"), "lat", None),
        check_vma=False,
    )
```

```python
import functools
import math

import jax
import jax.numpy as jnp
import numpy as np
from jax import lax
from jax.experimental import pallas as pl
from jax.experimental.pallas import tpu as pltpu
from jax.sharding import PartitionSpec as P

NEAR = 4
FAR = 16
EDGE = 8
LANES = 128
F32, BF16 = jnp.float32, jnp.bfloat16
VMEM = pl.BlockSpec(memory_space=pltpu.VMEM)
AHEAD = 4 * 10**9


def smooth_act(value):
    return jax.nn.gelu(value, approximate=True)


def act_adjoint(pre_value, upstream):
    unused, pullback = jax.vjp(smooth_act, pre_value)
    return pullback(upstream)[0]


def group_sizes():
    lat = math.gcd(lax.axis_size("lat"), NEAR * NEAR)
    return NEAR * NEAR // lat, lat


def swap(chunks):
    group_lon, group_lat = group_sizes()
    lon, lat = lax.axis_size("lon"), lax.axis_size("lat")
    if (lon, lat) == (group_lon, group_lat):
        return lax.all_to_all(chunks, ("lon", "lat"), 0, 0, tiled=True)
    chunks = chunks.reshape((group_lon, group_lat) + chunks.shape[1:])
    for axis, dim, size in (("lon", 0, group_lon), ("lat", 1, group_lat)):
        count = lax.axis_size(axis)
        groups = [list(range(i, i + size)) for i in range(0, count, size)]
        chunks = lax.all_to_all(chunks, axis, dim, dim, tiled=True, axis_index_groups=groups)
    return chunks.reshape((group_lon * group_lat,) + chunks.shape[2:])


def lon_parts():
    group_lon = group_sizes()[0]
    fast = 2 if group_lon % 2 == 0 else 1
    slow = group_lon // fast
    bits = slow.bit_length() - 1
    listing = [sum(((i ^ (i >> 1)) >> b & 1) << (bits - 1 - b) for b in range(bits)) for i in range(slow)]
    return slow, fast, listing[-1:] + listing[:-1]


def listed(points):
    slow, fast, listing = lon_parts()
    lat, path = lax.axis_size("lat"), lax.axis_size("path")
    grid = np.arange(slow * fast * lat * path).reshape(slow, fast, lat, path)[listing]
    if points:
        return [grid.transpose(1, 2, 3, 0).reshape(-1).tolist()]
    return [grid[..., p].transpose(1, 2, 0).reshape(-1).tolist() for p in range(path)]


def swap_listed(chunks, points):
    return lax.all_to_all(chunks, ("lon", "lat", "path"), 0, 0, tiled=True, axis_index_groups=listed(points))


def to_classes(cells):
    rows, cols, depth = cells.shape
    cells = cells.reshape(rows // NEAR, NEAR, cols // NEAR, NEAR, depth).transpose(1, 3, 0, 2, 4)
    return cells.reshape(NEAR * NEAR, rows // NEAR, cols // NEAR, depth)


def padded(cells, width):
    for axis, dim, step in zip(("lon", "lat"), (0, 1), group_sizes()):
        count = lax.axis_size(axis)
        head = lax.slice_in_dim(cells, 0, width, axis=dim)
        tail = lax.slice_in_dim(cells, cells.shape[dim] - width, cells.shape[dim], axis=dim)
        if count == step:
            before, after = jnp.zeros_like(tail), jnp.zeros_like(head)
        else:
            before = lax.ppermute(tail, axis, [(i, i + step) for i in range(count - step)])
            after = lax.ppermute(head, axis, [(i + step, i) for i in range(count - step)])
        cells = jnp.concatenate([before, cells, after], axis=dim)
    return cells


def stencil(cells, weights, step, forward):
    rows, cols, depth = cells.shape
    around = padded(cells, step)
    total = jnp.zeros((rows, cols, depth), jnp.float32)
    for tap in range(9):
        sign = step if forward else -step
        row, col = step + (tap // 3 - 1) * sign, step + (tap % 3 - 1) * sign
        window = around[row : row + rows, col : col + cols]
        dims = (((2,), (0 if forward else 1,)), ((), ()))
        total = total + lax.dot_general(window, weights[tap], dims, preferred_element_type=jnp.float32)
    return total


def digit(place, stride, size):
    if size & (size - 1) or stride & (stride - 1):
        return lax.rem(lax.div(place, jnp.int32(stride)), jnp.int32(size))
    return lax.shift_right_logical(place, jnp.int32(stride.bit_length() - 1)) & (size - 1)


def ordering(dims, axes, listing=(None, ())):
    cells, runs = math.prod(dims), []
    for axis in axes:
        if runs and runs[-1][-1] == axis - 1 and listing[0] not in (axis, axis - 1):
            runs[-1].append(axis)
        else:
            runs.append([axis])
    place = lax.broadcasted_iota(jnp.int32, (cells, 1), 0)
    source, stride = jnp.zeros((cells, 1), jnp.int32), 1
    for run in reversed(runs):
        size = math.prod(dims[axis] for axis in run)
        here = digit(place, stride, size)
        if run == [listing[0]]:
            here = sum(jnp.where(here == i, value, 0) for i, value in enumerate(listing[1]) if value)
        source += here * math.prod(dims[run[-1] + 1 :])
        stride *= size
    return (lax.broadcasted_iota(jnp.int32, (cells, cells), 1) == source).astype(F32).astype(BF16)


def gelu_and_slope(value):
    scale, cubic = math.sqrt(2 / math.pi), 0.044715
    square = value * value
    bent = jnp.tanh(scale * value * (1 + cubic * square))
    half = 0.5 * (1 + bent)
    return value * half, half + 0.5 * value * (1 - bent * bent) * (scale * (1 + 3 * cubic * square))


def call(kernel, outs, scratch, name, megabytes, *args, flops=0):
    args = [pltpu.with_memory_space_constraint(x, pltpu.VMEM) for x in args]
    size = sum(x.size * x.dtype.itemsize for x in args)
    return pl.pallas_call(
        kernel,
        out_shape=[pltpu.VMEM(shape, dtype) for shape, dtype in outs],
        in_specs=[VMEM] * len(args),
        out_specs=[VMEM] * len(outs),
        scratch_shapes=scratch,
        compiler_params=pltpu.CompilerParams(vmem_limit_bytes=megabytes << 20),
        cost_estimate=pl.CostEstimate(flops=flops, bytes_accessed=size, transcendentals=0),
        name=name,
    )(*args)


def row_orders(rows, cols, sizes):
    group_lon, group_lat, row_part, col_part = sizes
    cells = rows * cols

    def kernel(to_classes, to_grid):
        to_classes[...] = ordering((row_part, NEAR, col_part, NEAR), (1, 3, 0, 2))
        slow, fast, listing = lon_parts()
        found = [listing.index(i) for i in range(slow)]
        to_grid[...] = ordering((fast, group_lat, slow, row_part, col_part), (1, 4, 2, 0, 3), (2, found))

    return call(kernel, [((cells, cells), BF16)] * 2, [], "row_orders", 4, flops=AHEAD)


def pack_classes(order, observed, baseline, cotangent):
    rows, cols, depth = observed.shape
    points = lax.axis_size("path")
    cells, part = rows * cols, rows * cols // (NEAR * NEAR)

    def kernel(order, observed, baseline, cotangent, sent, diff_rows):
        mine = lax.axis_index("path")
        mix = (mine.astype(F32) + 0.5) / points
        base = baseline[...].astype(F32)
        diff = observed[...].astype(F32) - base
        field = (base + mix * diff).astype(BF16)
        moved = jnp.dot(order[...], field, preferred_element_type=F32)
        sent[:, :part, :] = moved.reshape(NEAR * NEAR, part, depth).astype(BF16)
        moved = jnp.dot(order[...], cotangent[...], preferred_element_type=F32)
        moved = moved.reshape(NEAR * NEAR, points, part // points, depth)
        own = moved[:, 0]
        for k in range(1, points):
            own = jnp.where(mine == k, moved[:, k], own)
        sent[:, part:, :] = own.astype(BF16)
        half = pl.ds(pl.multiple_of(mine * (cells // points), cells // points), cells // points)
        diff_rows[...] = (observed[half, :].astype(F32) - baseline[half, :].astype(F32)) * (1 / points)

    return call(
        kernel,
        [((NEAR * NEAR, part + part // points, depth), BF16), ((cells // points, depth), F32)],
        [],
        "pack_classes",
        8,
        order,
        *(x.reshape(cells, depth) for x in (observed, baseline, cotangent)),
        flops=AHEAD,
    )


def class_tools(sizes, depth, edged):
    group_lon, group_lat, row_part, col_part = sizes
    rows, cols = group_lon * row_part, group_lat * col_part
    cells = rows * cols

    def spread(values, step, at, target):
        span = slice(at, at + values.shape[1])
        edged[:, EDGE : EDGE + rows, span] = values.reshape(cols, rows, -1)
        for i in range(3):
            start = EDGE + (i - 1) * step
            shifted = edged[:, start : start + rows, span].reshape(cells, -1)
            target[:, i * depth + at : i * depth + at + values.shape[1]] = shifted.astype(BF16)

    def convolution(source, weights, step):
        shift = step * rows

        def products(values, *columns):
            blocks = [
                jnp.concatenate([part[i, col] for i in range(3) for part in weights], axis=0) for col in columns
            ]
            joint = jnp.dot(values, jnp.concatenate(blocks, axis=1), preferred_element_type=F32)
            return [joint[:, i * depth : (i + 1) * depth] for i in range(len(columns))]

        if 2 * shift == cells:
            same_low, before = products(source[:shift, :], 1, 0)
            same_high, after = products(source[shift:, :], 1, 2)
            return jnp.concatenate([same_low + after, same_high + before], axis=0)
        before, same, after = products(source[...], 0, 1, 2)
        fill = jnp.zeros((shift, depth), F32)
        after = jnp.concatenate([after[shift:], fill], axis=0)
        return same + after + jnp.concatenate([fill, before[: cells - shift]], axis=0)

    def transposed_part(source, weights, step, at, end):
        def weigh(values, col):
            taps_of = [jnp.concatenate([part[2 - i, 2 - col] for part in weights], axis=0)[at:end] for i in range(3)]
            return lax.dot_general(
                values, jnp.concatenate(taps_of, axis=1), (((1,), (1,)), ((), ())), preferred_element_type=F32
            )

        shift = step * rows
        fill = jnp.zeros((shift, end - at), F32)
        same = weigh(source[...], 1)
        after = weigh(source[shift:, :], 2)
        before = weigh(source[: cells - shift, :], 0)
        return same + jnp.concatenate([after, fill], axis=0) + jnp.concatenate([fill, before], axis=0)

    edged[:, :EDGE, :] = jnp.zeros((cols, EDGE, depth), F32)
    edged[:, EDGE + rows :, :] = jnp.zeros((cols, EDGE, depth), F32)
    return spread, convolution, transposed_part


def by_place(points, run, *halves):
    for place in range(points):
        owners = [(place - k) % points for k in range(points)]
        lists = [[parts[k] for k in owners] for parts in halves]
        pl.when(lax.axis_index("path") == place)(functools.partial(run, place, *lists))


def channel_parts(depth):
    return [(at, min(at + 2 * LANES, depth)) for at in range(0, depth, 2 * LANES)]


def slopes_of_class(order, got, first_halves, first_bias, second_halves, second_bias, sizes):
    group_lon, group_lat, row_part, col_part = sizes
    points, depth = len(first_halves), got.shape[-1]
    rows, cols, part = group_lon * row_part, group_lat * col_part, row_part * col_part
    cells = rows * cols

    def kernel(order, got, first_bias, second_bias, *refs):
        first_slope, second_slope, edged, near_taps, far_taps = refs[2 * points :]

        def run(place, first, second):
            spread, convolution, _ = class_tools(sizes, depth, edged)
            field = jnp.dot(order[...], got[:, :part, :].reshape(cells, depth), preferred_element_type=F32)
            spread(field, 1, 0, near_taps)
            act, first_slope[...] = gelu_and_slope(convolution(near_taps, first, 1) + first_bias[...].reshape(1, -1))
            spread(field + act, FAR // NEAR, 0, far_taps)
            pre = convolution(far_taps, second, FAR // NEAR) + second_bias[...].reshape(1, -1)
            second_slope[...] = gelu_and_slope(pre)[1]

        by_place(points, run, refs[:points], refs[points : 2 * points])

    return call(
        kernel,
        [((cells, depth), F32)] * 2,
        [pltpu.VMEM((cols, rows + 2 * EDGE, depth), F32)] + [pltpu.VMEM((cells, 3 * depth), BF16)] * 2,
        "slopes_of_class",
        16,
        order,
        got,
        first_bias,
        second_bias,
        *first_halves,
        *second_halves,
    )


def adjoint_of_class(order, cotangents, first_slope, second_slope, first_halves, second_halves, sizes):
    group_lon, group_lat, row_part, col_part = sizes
    points, depth = len(first_halves), first_slope.shape[-1]
    rows, cols = group_lon * row_part, group_lat * col_part
    cells = rows * cols

    def kernel(order, first_slope, second_slope, *refs):
        sent, edged, near_taps, far_taps, grad = refs[3 * points :]

        def run(place, cotangent, first, second):
            spread, _, transposed_part = class_tools(sizes, depth, edged)
            upstream = jnp.concatenate([share[...].astype(F32) for share in cotangent], axis=1)
            upstream = jnp.dot(order[...], upstream.reshape(cells, depth).astype(BF16), preferred_element_type=F32)
            spread(second_slope[...] * upstream, FAR // NEAR, 0, far_taps)
            for at, end in channel_parts(depth):
                hidden_adj = upstream[:, at:end] + transposed_part(far_taps, second, FAR // NEAR, at, end)
                grad[:, at:end] = hidden_adj
                spread(first_slope[:, at:end] * hidden_adj, 1, at, near_taps)
            slow, fast, listing = lon_parts()
            dims = (group_lat, col_part, slow, fast, points, row_part // points)
            home = ordering(dims, (3, 0, 4, 2, 5, 1), (2, listing))
            for at, end in channel_parts(depth):
                grad[:, at:end] += transposed_part(near_taps, first, 1, at, end)
            sent[...] = jnp.dot(home, grad[...].astype(BF16), preferred_element_type=F32).astype(BF16)

        by_place(points, run, refs[:points], refs[points : 2 * points], refs[2 * points : 3 * points])

    return call(
        kernel,
        [((cells, depth), BF16)],
        [pltpu.VMEM((cols, rows + 2 * EDGE, depth), F32)]
        + [pltpu.VMEM((cells, 3 * depth), BF16)] * 2
        + [pltpu.VMEM((cells, depth), F32)],
        "adjoint_of_class",
        16,
        order,
        first_slope,
        second_slope,
        *cotangents,
        *first_halves,
        *second_halves,
    )[0]


def attribution_rows(home, diff_rows, rows, cols):
    points, depth = lax.axis_size("path"), home.shape[-1]
    cells, group_lat = rows * cols, group_sizes()[1]

    def kernel(home, diff_rows, out):
        bits, ahead = (NEAR * NEAR).bit_length() - 1, (group_lat * lon_parts()[1]).bit_length() - 1
        of_class = tuple(i + (i >= ahead) for i in range(bits))
        dims = (2,) * ahead + (points,) + (2,) * (bits - ahead) + (rows // NEAR, cols // NEAR)
        row_bits, col_bits = of_class[: bits // 2], of_class[bits // 2 :]
        order = ordering(dims, (ahead, bits + 1) + row_bits + (bits + 2,) + col_bits)
        order = sum(order[k * cells : (k + 1) * cells] for k in range(points))
        moved = jnp.dot(order, home[...], preferred_element_type=F32)
        out[...] = (diff_rows[...] * moved).reshape(rows, cols, depth).astype(BF16)

    return call(kernel, [((rows, cols, depth), BF16)], [], "attribution_rows", 4, home, diff_rows)[0]


def one_group(observed, baseline, cotangent, first_weight, first_bias, second_weight, second_bias):
    rows, cols, depth = observed.shape
    points = lax.axis_size("path")
    sizes = group_sizes() + (rows // NEAR, cols // NEAR)

    def turned(values, step):
        return lax.ppermute(values, "path", [(i, (i + step) % points) for i in range(points)])

    side = math.isqrt(first_weight.shape[0])
    halves = [
        [x.reshape((side, side) + x.shape[1:]) for x in [part] + [turned(part, step) for step in range(1, points)]]
        for part in (first_weight, second_weight)
    ]
    to_classes, to_grid = row_orders(rows, cols, sizes)
    sent, diff_rows = pack_classes(to_classes, observed, baseline, cotangent)
    got = swap_listed(sent, points=False)
    own = got[:, sizes[2] * sizes[3] :, :]
    cotangents = [own] + [turned(own, step) for step in range(1, points)]
    first_slope, second_slope = slopes_of_class(to_grid, got, halves[0], first_bias, halves[1], second_bias, sizes)
    grad = adjoint_of_class(to_grid, cotangents, first_slope, second_slope, *halves, sizes)
    chunks = grad.reshape(NEAR * NEAR * points, -1, depth)
    home = swap_listed(chunks, points=True)
    return attribution_rows(home.reshape(grad.shape), diff_rows, rows // points, cols)


def several_groups(observed, baseline, cotangent, first_weight, first_bias, second_weight, second_bias):
    rows, cols, depth = observed.shape
    points, point = lax.axis_size("path"), lax.axis_index("path")
    group_lon, group_lat = group_sizes()
    row_part, col_part = rows // NEAR, cols // NEAR
    ring = [(i, (i + 1) % points) for i in range(points)]

    def whole_weight(part):
        held = jnp.zeros((part.shape[0], points) + part.shape[1:], part.dtype)
        for step in range(points):
            held = lax.dynamic_update_slice_in_dim(held, part[:, None], (point - step) % points, 1)
            if step < points - 1:
                part = lax.ppermute(part, "path", ring)
        return held.reshape(held.shape[0], -1, held.shape[3])

    first_full, second_full = whole_weight(first_weight), whole_weight(second_weight)
    diff = observed.astype(jnp.float32) - baseline.astype(jnp.float32)
    mix = (point.astype(jnp.float32) + 0.5) / points
    field = (baseline.astype(jnp.float32) + mix * diff).astype(jnp.bfloat16)
    sent = jnp.stack([to_classes(field), to_classes(cotangent)], axis=1)
    got = swap(sent).reshape(group_lon, group_lat, 2, row_part, col_part, depth)
    got = got.transpose(2, 0, 3, 1, 4, 5).reshape(2, group_lon * row_part, group_lat * col_part, depth)
    field, upstream = got[0], got[1].astype(jnp.float32)

    first_pre = stencil(field, first_full, 1, True) + first_bias
    hidden = (field.astype(jnp.float32) + smooth_act(first_pre)).astype(jnp.bfloat16)
    second_pre = stencil(hidden, second_full, FAR // NEAR, True) + second_bias
    second_adj = act_adjoint(second_pre, upstream).astype(jnp.bfloat16)
    hidden_adj = upstream + stencil(second_adj, second_full, FAR // NEAR, False)
    first_adj = act_adjoint(first_pre, hidden_adj).astype(jnp.bfloat16)
    grad = hidden_adj + stencil(first_adj, first_full, 1, False)

    part = row_part // points
    grad = grad.reshape(group_lon, points, part, group_lat, col_part, depth).transpose(1, 0, 3, 2, 4, 5)
    grad = grad.reshape(points, group_lon * group_lat, part, col_part, depth)
    total = lax.dynamic_index_in_dim(grad, point, 0, keepdims=False)
    for step in range(1, points):
        other = lax.dynamic_index_in_dim(grad, (point + step) % points, 0, keepdims=False)
        total = total + lax.ppermute(other, "path", [(i, (i + step) % points) for i in range(points)])
    home = swap(total.astype(jnp.bfloat16)).reshape(NEAR, NEAR, part, col_part, depth)
    home = home.transpose(2, 0, 3, 1, 4).reshape(rows // points, cols, depth).astype(jnp.float32)
    diff_rows = lax.dynamic_slice_in_dim(diff, point * (rows // points), rows // points, 0)
    return (diff_rows * home / points).astype(jnp.bfloat16)


def shards(*args):
    if group_sizes() == (lax.axis_size("lon"), lax.axis_size("lat")):
        return one_group(*args)
    return several_groups(*args)


def solution(mesh):
    placed = (
        P("lon", "lat", None),
        P("lon", "lat", None),
        P("lon", "lat", None),
        P(None, "path", None),
        P(),
        P(None, "path", None),
        P(),
    )
    return jax.shard_map(
        shards,
        mesh=mesh,
        in_specs=placed,
        out_specs=P(("lon", "path"), "lat", None),
        check_vma=False,
    )
```

```python
import functools
import math

import jax
import jax.numpy as jnp
import numpy as np
from jax import lax
from jax.experimental import pallas as pl
from jax.experimental.pallas import tpu as pltpu
from jax.sharding import PartitionSpec as P

NEAR = 4
FAR = 16
EDGE = 8
LANES = 128
F32, BF16 = jnp.float32, jnp.bfloat16
VMEM = pl.BlockSpec(memory_space=pltpu.VMEM)
AHEAD = 4 * 10**9


def smooth_act(value):
    return jax.nn.gelu(value, approximate=True)


def act_adjoint(pre_value, upstream):
    unused, pullback = jax.vjp(smooth_act, pre_value)
    return pullback(upstream)[0]


def group_sizes():
    lat = math.gcd(lax.axis_size("lat"), NEAR * NEAR)
    return NEAR * NEAR // lat, lat


def swap(chunks):
    group_lon, group_lat = group_sizes()
    lon, lat = lax.axis_size("lon"), lax.axis_size("lat")
    if (lon, lat) == (group_lon, group_lat):
        return lax.all_to_all(chunks, ("lon", "lat"), 0, 0, tiled=True)
    chunks = chunks.reshape((group_lon, group_lat) + chunks.shape[1:])
    for axis, dim, size in (("lon", 0, group_lon), ("lat", 1, group_lat)):
        count = lax.axis_size(axis)
        groups = [list(range(i, i + size)) for i in range(0, count, size)]
        chunks = lax.all_to_all(chunks, axis, dim, dim, tiled=True, axis_index_groups=groups)
    return chunks.reshape((group_lon * group_lat,) + chunks.shape[2:])


def lon_parts():
    group_lon = group_sizes()[0]
    fast = 2 if group_lon % 2 == 0 else 1
    slow = group_lon // fast
    bits = slow.bit_length() - 1
    listing = [sum(((i ^ (i >> 1)) >> b & 1) << (bits - 1 - b) for b in range(bits)) for i in range(slow)]
    return slow, fast, listing[-1:] + listing[:-1]


def listed(points):
    slow, fast, listing = lon_parts()
    lat, path = lax.axis_size("lat"), lax.axis_size("path")
    grid = np.arange(slow * fast * lat * path).reshape(slow, fast, lat, path)[listing]
    if points:
        return [grid.transpose(1, 2, 3, 0).reshape(-1).tolist()]
    return [grid[..., p].transpose(1, 2, 0).reshape(-1).tolist() for p in range(path)]


def swap_listed(chunks, points):
    return lax.all_to_all(chunks, ("lon", "lat", "path"), 0, 0, tiled=True, axis_index_groups=listed(points))


def to_classes(cells):
    rows, cols, depth = cells.shape
    cells = cells.reshape(rows // NEAR, NEAR, cols // NEAR, NEAR, depth).transpose(1, 3, 0, 2, 4)
    return cells.reshape(NEAR * NEAR, rows // NEAR, cols // NEAR, depth)


def padded(cells, width):
    for axis, dim, step in zip(("lon", "lat"), (0, 1), group_sizes()):
        count = lax.axis_size(axis)
        head = lax.slice_in_dim(cells, 0, width, axis=dim)
        tail = lax.slice_in_dim(cells, cells.shape[dim] - width, cells.shape[dim], axis=dim)
        if count == step:
            before, after = jnp.zeros_like(tail), jnp.zeros_like(head)
        else:
            before = lax.ppermute(tail, axis, [(i, i + step) for i in range(count - step)])
            after = lax.ppermute(head, axis, [(i + step, i) for i in range(count - step)])
        cells = jnp.concatenate([before, cells, after], axis=dim)
    return cells


def stencil(cells, weights, step, forward):
    rows, cols, depth = cells.shape
    around = padded(cells, step)
    total = jnp.zeros((rows, cols, depth), jnp.float32)
    for tap in range(9):
        sign = step if forward else -step
        row, col = step + (tap // 3 - 1) * sign, step + (tap % 3 - 1) * sign
        window = around[row : row + rows, col : col + cols]
        dims = (((2,), (0 if forward else 1,)), ((), ()))
        total = total + lax.dot_general(window, weights[tap], dims, preferred_element_type=jnp.float32)
    return total


def digit(place, stride, size):
    if size & (size - 1) or stride & (stride - 1):
        return lax.rem(lax.div(place, jnp.int32(stride)), jnp.int32(size))
    return lax.shift_right_logical(place, jnp.int32(stride.bit_length() - 1)) & (size - 1)


def ordering(dims, axes, listing=(None, ())):
    cells, runs = math.prod(dims), []
    for axis in axes:
        if runs and runs[-1][-1] == axis - 1 and listing[0] not in (axis, axis - 1):
            runs[-1].append(axis)
        else:
            runs.append([axis])
    place = lax.broadcasted_iota(jnp.int32, (cells, 1), 0)
    source, stride = jnp.zeros((cells, 1), jnp.int32), 1
    for run in reversed(runs):
        size = math.prod(dims[axis] for axis in run)
        here = digit(place, stride, size)
        if run == [listing[0]]:
            here = sum(jnp.where(here == i, value, 0) for i, value in enumerate(listing[1]) if value)
        source += here * math.prod(dims[run[-1] + 1 :])
        stride *= size
    return (lax.broadcasted_iota(jnp.int32, (cells, cells), 1) == source).astype(F32).astype(BF16)


def gelu_and_slope(value):
    scale, cubic = math.sqrt(2 / math.pi), 0.044715
    square = value * value
    bent = jnp.tanh(scale * value * (1 + cubic * square))
    half = 0.5 * (1 + bent)
    return value * half, half + 0.5 * value * (1 - bent * bent) * (scale * (1 + 3 * cubic * square))


def call(kernel, outs, scratch, name, megabytes, *args, flops=0):
    args = [pltpu.with_memory_space_constraint(x, pltpu.VMEM) for x in args]
    size = sum(x.size * x.dtype.itemsize for x in args)
    return pl.pallas_call(
        kernel,
        out_shape=[pltpu.VMEM(shape, dtype) for shape, dtype in outs],
        in_specs=[VMEM] * len(args),
        out_specs=[VMEM] * len(outs),
        scratch_shapes=scratch,
        compiler_params=pltpu.CompilerParams(vmem_limit_bytes=megabytes << 20),
        cost_estimate=pl.CostEstimate(flops=flops, bytes_accessed=size, transcendentals=0),
        name=name,
    )(*args)


def row_orders(rows, cols, sizes):
    group_lon, group_lat, row_part, col_part = sizes
    cells = rows * cols

    def kernel(to_classes, to_grid):
        to_classes[...] = ordering((row_part, NEAR, col_part, NEAR), (1, 3, 0, 2))
        slow, fast, listing = lon_parts()
        found = [listing.index(i) for i in range(slow)]
        to_grid[...] = ordering((fast, group_lat, slow, row_part, col_part), (1, 4, 2, 0, 3), (2, found))

    return call(kernel, [((cells, cells), BF16)] * 2, [], "row_orders", 4, flops=AHEAD)


def pack_classes(order, observed, baseline, cotangent):
    rows, cols, depth = observed.shape
    points = lax.axis_size("path")
    cells, part = rows * cols, rows * cols // (NEAR * NEAR)

    def kernel(order, observed, baseline, cotangent, sent, diff_rows):
        mine = lax.axis_index("path")
        mix = (mine.astype(F32) + 0.5) / points
        base = baseline[...].astype(F32)
        diff = observed[...].astype(F32) - base
        field = (base + mix * diff).astype(BF16)
        moved = jnp.dot(order[...], field, preferred_element_type=F32)
        sent[:, :part, :] = moved.reshape(NEAR * NEAR, part, depth).astype(BF16)
        moved = jnp.dot(order[...], cotangent[...], preferred_element_type=F32)
        moved = moved.reshape(NEAR * NEAR, points, part // points, depth)
        own = moved[:, 0]
        for k in range(1, points):
            own = jnp.where(mine == k, moved[:, k], own)
        sent[:, part:, :] = own.astype(BF16)
        half = pl.ds(pl.multiple_of(mine * (cells // points), cells // points), cells // points)
        diff_rows[...] = (observed[half, :].astype(F32) - baseline[half, :].astype(F32)) * (1 / points)

    return call(
        kernel,
        [((NEAR * NEAR, part + part // points, depth), BF16), ((cells // points, depth), F32)],
        [],
        "pack_classes",
        8,
        order,
        *(x.reshape(cells, depth) for x in (observed, baseline, cotangent)),
        flops=AHEAD,
    )


def class_tools(sizes, depth, edged):
    group_lon, group_lat, row_part, col_part = sizes
    rows, cols = group_lon * row_part, group_lat * col_part
    cells = rows * cols

    def spread(values, step, at, target):
        span = slice(at, at + values.shape[1])
        edged[:, EDGE : EDGE + rows, span] = values.reshape(cols, rows, -1)
        for i in range(3):
            start = EDGE + (i - 1) * step
            shifted = edged[:, start : start + rows, span].reshape(cells, -1)
            target[:, i * depth + at : i * depth + at + values.shape[1]] = shifted.astype(BF16)

    def convolution(source, weights, step):
        shift = step * rows

        def products(values, *columns):
            blocks = [
                jnp.concatenate([part[i, col] for i in range(3) for part in weights], axis=0) for col in columns
            ]
            joint = jnp.dot(values, jnp.concatenate(blocks, axis=1), preferred_element_type=F32)
            return [joint[:, i * depth : (i + 1) * depth] for i in range(len(columns))]

        if 2 * shift == cells:
            same_low, before = products(source[:shift, :], 1, 0)
            same_high, after = products(source[shift:, :], 1, 2)
            return jnp.concatenate([same_low + after, same_high + before], axis=0)
        before, same, after = products(source[...], 0, 1, 2)
        fill = jnp.zeros((shift, depth), F32)
        after = jnp.concatenate([after[shift:], fill], axis=0)
        return same + after + jnp.concatenate([fill, before[: cells - shift]], axis=0)

    def transposed_part(source, weights, step, at, end):
        def weigh(values, col):
            taps_of = [jnp.concatenate([part[2 - i, 2 - col] for part in weights], axis=0)[at:end] for i in range(3)]
            return lax.dot_general(
                values, jnp.concatenate(taps_of, axis=1), (((1,), (1,)), ((), ())), preferred_element_type=F32
            )

        shift = step * rows
        fill = jnp.zeros((shift, end - at), F32)
        same = weigh(source[...], 1)
        after = weigh(source[shift:, :], 2)
        before = weigh(source[: cells - shift, :], 0)
        return same + jnp.concatenate([after, fill], axis=0) + jnp.concatenate([fill, before], axis=0)

    edged[:, :EDGE, :] = jnp.zeros((cols, EDGE, depth), F32)
    edged[:, EDGE + rows :, :] = jnp.zeros((cols, EDGE, depth), F32)
    return spread, convolution, transposed_part


def by_place(points, run, *halves):
    for place in range(points):
        owners = [(place - k) % points for k in range(points)]
        lists = [[parts[k] for k in owners] for parts in halves]
        pl.when(lax.axis_index("path") == place)(functools.partial(run, place, *lists))


def channel_parts(depth):
    return [(at, min(at + 2 * LANES, depth)) for at in range(0, depth, 2 * LANES)]


def slopes_of_class(order, got, first_halves, first_bias, second_halves, second_bias, sizes):
    group_lon, group_lat, row_part, col_part = sizes
    points, depth = len(first_halves), got.shape[-1]
    rows, cols, part = group_lon * row_part, group_lat * col_part, row_part * col_part
    cells = rows * cols

    def kernel(order, got, first_bias, second_bias, *refs):
        first_slope, second_slope, edged, near_taps, far_taps = refs[2 * points :]

        def run(place, first, second):
            spread, convolution, _ = class_tools(sizes, depth, edged)
            field = jnp.dot(order[...], got[:, :part, :].reshape(cells, depth), preferred_element_type=F32)
            spread(field, 1, 0, near_taps)
            act, first_slope[...] = gelu_and_slope(convolution(near_taps, first, 1) + first_bias[...].reshape(1, -1))
            spread(field + act, FAR // NEAR, 0, far_taps)
            pre = convolution(far_taps, second, FAR // NEAR) + second_bias[...].reshape(1, -1)
            second_slope[...] = gelu_and_slope(pre)[1]

        by_place(points, run, refs[:points], refs[points : 2 * points])

    return call(
        kernel,
        [((cells, depth), F32)] * 2,
        [pltpu.VMEM((cols, rows + 2 * EDGE, depth), F32)] + [pltpu.VMEM((cells, 3 * depth), BF16)] * 2,
        "slopes_of_class",
        16,
        order,
        got,
        first_bias,
        second_bias,
        *first_halves,
        *second_halves,
    )


def adjoint_of_class(order, cotangents, first_slope, second_slope, first_halves, second_halves, sizes):
    group_lon, group_lat, row_part, col_part = sizes
    points, depth = len(first_halves), first_slope.shape[-1]
    rows, cols = group_lon * row_part, group_lat * col_part
    cells = rows * cols

    def kernel(order, first_slope, second_slope, *refs):
        sent, edged, near_taps, far_taps, grad = refs[3 * points :]

        def run(place, cotangent, first, second):
            spread, _, transposed_part = class_tools(sizes, depth, edged)
            def near_part(at, end):
                sides = [near_taps[j * rows : j * rows + cells, :] for j in range(3)]
                blocks = [
                    jnp.concatenate([part[2 - i, 2 - j] for part in first], axis=0)[at:end]
                    for j in range(3)
                    for i in range(3)
                ]
                dims = (((1,), (1,)), ((), ()))
                joint, weights = jnp.concatenate(sides, axis=1), jnp.concatenate(blocks, axis=1)
                return lax.dot_general(joint, weights, dims, preferred_element_type=F32)

            near_taps[:rows, :] = jnp.zeros((rows, 3 * depth), BF16)
            near_taps[rows + cells :, :] = jnp.zeros((rows, 3 * depth), BF16)
            upstream = jnp.concatenate([share[...].astype(F32) for share in cotangent], axis=1)
            upstream = jnp.dot(order[...], upstream.reshape(cells, depth).astype(BF16), preferred_element_type=F32)
            spread(second_slope[...] * upstream, FAR // NEAR, 0, far_taps)
            for at, end in channel_parts(depth):
                hidden_adj = upstream[:, at:end] + transposed_part(far_taps, second, FAR // NEAR, at, end)
                grad[:, at:end] = hidden_adj
                spread(first_slope[:, at:end] * hidden_adj, 1, at, near_taps.at[rows : rows + cells])
            slow, fast, listing = lon_parts()
            dims = (group_lat, col_part, slow, fast, points, row_part // points)
            home = ordering(dims, (3, 0, 4, 2, 5, 1), (2, listing))
            for at, end in channel_parts(depth):
                grad[:, at:end] += near_part(at, end)
            sent[...] = jnp.dot(home, grad[...].astype(BF16), preferred_element_type=F32).astype(BF16)

        by_place(points, run, refs[:points], refs[points : 2 * points], refs[2 * points : 3 * points])

    return call(
        kernel,
        [((cells, depth), BF16)],
        [pltpu.VMEM((cols, rows + 2 * EDGE, depth), F32)]
        + [pltpu.VMEM((cells + 2 * rows, 3 * depth), BF16), pltpu.VMEM((cells, 3 * depth), BF16)]
        + [pltpu.VMEM((cells, depth), F32)],
        "adjoint_of_class",
        16,
        order,
        first_slope,
        second_slope,
        *cotangents,
        *first_halves,
        *second_halves,
    )[0]


def attribution_rows(home, diff_rows, rows, cols):
    points, depth = lax.axis_size("path"), home.shape[-1]
    cells, group_lat = rows * cols, group_sizes()[1]

    def kernel(home, diff_rows, out):
        bits, ahead = (NEAR * NEAR).bit_length() - 1, (group_lat * lon_parts()[1]).bit_length() - 1
        of_class = tuple(i + (i >= ahead) for i in range(bits))
        dims = (2,) * ahead + (points,) + (2,) * (bits - ahead) + (rows // NEAR, cols // NEAR)
        row_bits, col_bits = of_class[: bits // 2], of_class[bits // 2 :]
        order = ordering(dims, (ahead, bits + 1) + row_bits + (bits + 2,) + col_bits)
        order = sum(order[k * cells : (k + 1) * cells] for k in range(points))
        moved = jnp.dot(order, home[...], preferred_element_type=F32)
        out[...] = (diff_rows[...] * moved).reshape(rows, cols, depth).astype(BF16)

    return call(kernel, [((rows, cols, depth), BF16)], [], "attribution_rows", 4, home, diff_rows)[0]


def one_group(observed, baseline, cotangent, first_weight, first_bias, second_weight, second_bias):
    rows, cols, depth = observed.shape
    points = lax.axis_size("path")
    sizes = group_sizes() + (rows // NEAR, cols // NEAR)

    def turned(values, step):
        return lax.ppermute(values, "path", [(i, (i + step) % points) for i in range(points)])

    side = math.isqrt(first_weight.shape[0])
    halves = [
        [x.reshape((side, side) + x.shape[1:]) for x in [part] + [turned(part, step) for step in range(1, points)]]
        for part in (first_weight, second_weight)
    ]
    to_classes, to_grid = row_orders(rows, cols, sizes)
    sent, diff_rows = pack_classes(to_classes, observed, baseline, cotangent)
    got = swap_listed(sent, points=False)
    own = got[:, sizes[2] * sizes[3] :, :]
    cotangents = [own] + [turned(own, step) for step in range(1, points)]
    first_slope, second_slope = slopes_of_class(to_grid, got, halves[0], first_bias, halves[1], second_bias, sizes)
    grad = adjoint_of_class(to_grid, cotangents, first_slope, second_slope, *halves, sizes)
    chunks = grad.reshape(NEAR * NEAR * points, -1, depth)
    home = swap_listed(chunks, points=True)
    return attribution_rows(home.reshape(grad.shape), diff_rows, rows // points, cols)


def several_groups(observed, baseline, cotangent, first_weight, first_bias, second_weight, second_bias):
    rows, cols, depth = observed.shape
    points, point = lax.axis_size("path"), lax.axis_index("path")
    group_lon, group_lat = group_sizes()
    row_part, col_part = rows // NEAR, cols // NEAR
    ring = [(i, (i + 1) % points) for i in range(points)]

    def whole_weight(part):
        held = jnp.zeros((part.shape[0], points) + part.shape[1:], part.dtype)
        for step in range(points):
            held = lax.dynamic_update_slice_in_dim(held, part[:, None], (point - step) % points, 1)
            if step < points - 1:
                part = lax.ppermute(part, "path", ring)
        return held.reshape(held.shape[0], -1, held.shape[3])

    first_full, second_full = whole_weight(first_weight), whole_weight(second_weight)
    diff = observed.astype(jnp.float32) - baseline.astype(jnp.float32)
    mix = (point.astype(jnp.float32) + 0.5) / points
    field = (baseline.astype(jnp.float32) + mix * diff).astype(jnp.bfloat16)
    sent = jnp.stack([to_classes(field), to_classes(cotangent)], axis=1)
    got = swap(sent).reshape(group_lon, group_lat, 2, row_part, col_part, depth)
    got = got.transpose(2, 0, 3, 1, 4, 5).reshape(2, group_lon * row_part, group_lat * col_part, depth)
    field, upstream = got[0], got[1].astype(jnp.float32)

    first_pre = stencil(field, first_full, 1, True) + first_bias
    hidden = (field.astype(jnp.float32) + smooth_act(first_pre)).astype(jnp.bfloat16)
    second_pre = stencil(hidden, second_full, FAR // NEAR, True) + second_bias
    second_adj = act_adjoint(second_pre, upstream).astype(jnp.bfloat16)
    hidden_adj = upstream + stencil(second_adj, second_full, FAR // NEAR, False)
    first_adj = act_adjoint(first_pre, hidden_adj).astype(jnp.bfloat16)
    grad = hidden_adj + stencil(first_adj, first_full, 1, False)

    part = row_part // points
    grad = grad.reshape(group_lon, points, part, group_lat, col_part, depth).transpose(1, 0, 3, 2, 4, 5)
    grad = grad.reshape(points, group_lon * group_lat, part, col_part, depth)
    total = lax.dynamic_index_in_dim(grad, point, 0, keepdims=False)
    for step in range(1, points):
        other = lax.dynamic_index_in_dim(grad, (point + step) % points, 0, keepdims=False)
        total = total + lax.ppermute(other, "path", [(i, (i + step) % points) for i in range(points)])
    home = swap(total.astype(jnp.bfloat16)).reshape(NEAR, NEAR, part, col_part, depth)
    home = home.transpose(2, 0, 3, 1, 4).reshape(rows // points, cols, depth).astype(jnp.float32)
    diff_rows = lax.dynamic_slice_in_dim(diff, point * (rows // points), rows // points, 0)
    return (diff_rows * home / points).astype(jnp.bfloat16)


def shards(*args):
    if group_sizes() == (lax.axis_size("lon"), lax.axis_size("lat")):
        return one_group(*args)
    return several_groups(*args)


def solution(mesh):
    placed = (
        P("lon", "lat", None),
        P("lon", "lat", None),
        P("lon", "lat", None),
        P(None, "path", None),
        P(),
        P(None, "path", None),
        P(),
    )
    return jax.shard_map(
        shards,
        mesh=mesh,
        in_specs=placed,
        out_specs=P(("lon", "path"), "lat", None),
        check_vma=False,
    )
```

```python
import functools
import math

import jax
import jax.numpy as jnp
import numpy as np
from jax import lax
from jax.experimental import pallas as pl
from jax.experimental.pallas import tpu as pltpu
from jax.sharding import PartitionSpec as P

NEAR = 4
FAR = 16
EDGE = 8
LANES = 128
F32, BF16 = jnp.float32, jnp.bfloat16
VMEM = pl.BlockSpec(memory_space=pltpu.VMEM)
AHEAD = 4 * 10**9


def smooth_act(value):
    return jax.nn.gelu(value, approximate=True)


def act_adjoint(pre_value, upstream):
    unused, pullback = jax.vjp(smooth_act, pre_value)
    return pullback(upstream)[0]


def group_sizes():
    lat = math.gcd(lax.axis_size("lat"), NEAR * NEAR)
    return NEAR * NEAR // lat, lat


def swap(chunks):
    group_lon, group_lat = group_sizes()
    lon, lat = lax.axis_size("lon"), lax.axis_size("lat")
    if (lon, lat) == (group_lon, group_lat):
        return lax.all_to_all(chunks, ("lon", "lat"), 0, 0, tiled=True)
    chunks = chunks.reshape((group_lon, group_lat) + chunks.shape[1:])
    for axis, dim, size in (("lon", 0, group_lon), ("lat", 1, group_lat)):
        count = lax.axis_size(axis)
        groups = [list(range(i, i + size)) for i in range(0, count, size)]
        chunks = lax.all_to_all(chunks, axis, dim, dim, tiled=True, axis_index_groups=groups)
    return chunks.reshape((group_lon * group_lat,) + chunks.shape[2:])


def lon_parts():
    group_lon = group_sizes()[0]
    fast = 2 if group_lon % 2 == 0 else 1
    slow = group_lon // fast
    bits = slow.bit_length() - 1
    listing = [sum(((i ^ (i >> 1)) >> b & 1) << (bits - 1 - b) for b in range(bits)) for i in range(slow)]
    return slow, fast, listing[-1:] + listing[:-1]


def listed(points):
    slow, fast, listing = lon_parts()
    lat, path = lax.axis_size("lat"), lax.axis_size("path")
    grid = np.arange(slow * fast * lat * path).reshape(slow, fast, lat, path)[listing]
    if points:
        return [grid.transpose(1, 2, 3, 0).reshape(-1).tolist()]
    return [grid[..., p].transpose(1, 2, 0).reshape(-1).tolist() for p in range(path)]


def swap_listed(chunks, points):
    return lax.all_to_all(chunks, ("lon", "lat", "path"), 0, 0, tiled=True, axis_index_groups=listed(points))


def to_classes(cells):
    rows, cols, depth = cells.shape
    cells = cells.reshape(rows // NEAR, NEAR, cols // NEAR, NEAR, depth).transpose(1, 3, 0, 2, 4)
    return cells.reshape(NEAR * NEAR, rows // NEAR, cols // NEAR, depth)


def padded(cells, width):
    for axis, dim, step in zip(("lon", "lat"), (0, 1), group_sizes()):
        count = lax.axis_size(axis)
        head = lax.slice_in_dim(cells, 0, width, axis=dim)
        tail = lax.slice_in_dim(cells, cells.shape[dim] - width, cells.shape[dim], axis=dim)
        if count == step:
            before, after = jnp.zeros_like(tail), jnp.zeros_like(head)
        else:
            before = lax.ppermute(tail, axis, [(i, i + step) for i in range(count - step)])
            after = lax.ppermute(head, axis, [(i + step, i) for i in range(count - step)])
        cells = jnp.concatenate([before, cells, after], axis=dim)
    return cells


def stencil(cells, weights, step, forward):
    rows, cols, depth = cells.shape
    around = padded(cells, step)
    total = jnp.zeros((rows, cols, depth), jnp.float32)
    for tap in range(9):
        sign = step if forward else -step
        row, col = step + (tap // 3 - 1) * sign, step + (tap % 3 - 1) * sign
        window = around[row : row + rows, col : col + cols]
        dims = (((2,), (0 if forward else 1,)), ((), ()))
        total = total + lax.dot_general(window, weights[tap], dims, preferred_element_type=jnp.float32)
    return total


def digit(place, stride, size):
    if size & (size - 1) or stride & (stride - 1):
        return lax.rem(lax.div(place, jnp.int32(stride)), jnp.int32(size))
    return lax.shift_right_logical(place, jnp.int32(stride.bit_length() - 1)) & (size - 1)


def ordering(dims, axes, listing=(None, ())):
    cells, runs = math.prod(dims), []
    for axis in axes:
        if runs and runs[-1][-1] == axis - 1 and listing[0] not in (axis, axis - 1):
            runs[-1].append(axis)
        else:
            runs.append([axis])
    place = lax.broadcasted_iota(jnp.int32, (cells, 1), 0)
    source, stride = jnp.zeros((cells, 1), jnp.int32), 1
    for run in reversed(runs):
        size = math.prod(dims[axis] for axis in run)
        here = digit(place, stride, size)
        if run == [listing[0]]:
            here = sum(jnp.where(here == i, value, 0) for i, value in enumerate(listing[1]) if value)
        source += here * math.prod(dims[run[-1] + 1 :])
        stride *= size
    return (lax.broadcasted_iota(jnp.int32, (cells, cells), 1) == source).astype(F32).astype(BF16)


def gelu_and_slope(value):
    scale, cubic = math.sqrt(2 / math.pi), 0.044715
    square = value * value
    bent = jnp.tanh(scale * value * (1 + cubic * square))
    half = 0.5 * (1 + bent)
    return value * half, half + 0.5 * value * (1 - bent * bent) * (scale * (1 + 3 * cubic * square))


def call(kernel, outs, scratch, name, megabytes, *args, flops=0):
    args = [pltpu.with_memory_space_constraint(x, pltpu.VMEM) for x in args]
    size = sum(x.size * x.dtype.itemsize for x in args)
    return pl.pallas_call(
        kernel,
        out_shape=[pltpu.VMEM(shape, dtype) for shape, dtype in outs],
        in_specs=[VMEM] * len(args),
        out_specs=[VMEM] * len(outs),
        scratch_shapes=scratch,
        compiler_params=pltpu.CompilerParams(vmem_limit_bytes=megabytes << 20),
        cost_estimate=pl.CostEstimate(flops=flops, bytes_accessed=size, transcendentals=0),
        name=name,
    )(*args)


def row_orders(rows, cols, sizes):
    group_lon, group_lat, row_part, col_part = sizes
    cells = rows * cols

    def kernel(to_classes, to_grid):
        to_classes[...] = ordering((row_part, NEAR, col_part, NEAR), (1, 3, 0, 2))
        slow, fast, listing = lon_parts()
        found = [listing.index(i) for i in range(slow)]
        to_grid[...] = ordering((fast, group_lat, slow, row_part, col_part), (1, 4, 2, 0, 3), (2, found))

    return call(kernel, [((cells, cells), BF16)] * 2, [], "row_orders", 4, flops=AHEAD)


def pack_classes(order, observed, baseline, cotangent):
    rows, cols, depth = observed.shape
    points = lax.axis_size("path")
    cells, part = rows * cols, rows * cols // (NEAR * NEAR)

    def kernel(order, observed, baseline, cotangent, sent, diff_rows):
        mine = lax.axis_index("path")
        mix = (mine.astype(F32) + 0.5) / points
        base = baseline[...].astype(F32)
        diff = observed[...].astype(F32) - base
        field = (base + mix * diff).astype(BF16)
        moved = jnp.dot(order[...], field, preferred_element_type=F32)
        sent[:, :part, :] = moved.reshape(NEAR * NEAR, part, depth).astype(BF16)
        moved = jnp.dot(order[...], cotangent[...], preferred_element_type=F32)
        moved = moved.reshape(NEAR * NEAR, points, part // points, depth)
        own = moved[:, 0]
        for k in range(1, points):
            own = jnp.where(mine == k, moved[:, k], own)
        sent[:, part:, :] = own.astype(BF16)
        half = pl.ds(pl.multiple_of(mine * (cells // points), cells // points), cells // points)
        diff_rows[...] = (observed[half, :].astype(F32) - baseline[half, :].astype(F32)) * (1 / points)

    return call(
        kernel,
        [((NEAR * NEAR, part + part // points, depth), BF16), ((cells // points, depth), F32)],
        [],
        "pack_classes",
        8,
        order,
        *(x.reshape(cells, depth) for x in (observed, baseline, cotangent)),
        flops=AHEAD,
    )


def class_tools(sizes, depth, edged):
    group_lon, group_lat, row_part, col_part = sizes
    rows, cols = group_lon * row_part, group_lat * col_part
    cells = rows * cols

    def spread(values, step, at, target):
        span = slice(at, at + values.shape[1])
        edged[:, EDGE : EDGE + rows, span] = values.reshape(cols, rows, -1)
        for i in range(3):
            start = EDGE + (i - 1) * step
            shifted = edged[:, start : start + rows, span].reshape(cells, -1)
            target[:, i * depth + at : i * depth + at + values.shape[1]] = shifted.astype(BF16)

    def convolution(source, weights, step):
        shift = step * rows

        def products(values, *columns):
            blocks = [
                jnp.concatenate([part[i, col] for i in range(3) for part in weights], axis=0) for col in columns
            ]
            joint = jnp.dot(values, jnp.concatenate(blocks, axis=1), preferred_element_type=F32)
            return [joint[:, i * depth : (i + 1) * depth] for i in range(len(columns))]

        if 2 * shift == cells:
            same_low, before = products(source[:shift, :], 1, 0)
            same_high, after = products(source[shift:, :], 1, 2)
            return jnp.concatenate([same_low + after, same_high + before], axis=0)
        before, same, after = products(source[...], 0, 1, 2)
        fill = jnp.zeros((shift, depth), F32)
        after = jnp.concatenate([after[shift:], fill], axis=0)
        return same + after + jnp.concatenate([fill, before[: cells - shift]], axis=0)

    def transposed_part(source, weights, step, at, end):
        def weigh(values, col):
            taps_of = [jnp.concatenate([part[2 - i, 2 - col] for part in weights], axis=0)[at:end] for i in range(3)]
            return lax.dot_general(
                values, jnp.concatenate(taps_of, axis=1), (((1,), (1,)), ((), ())), preferred_element_type=F32
            )

        shift = step * rows
        fill = jnp.zeros((shift, end - at), F32)
        same = weigh(source[...], 1)
        after = weigh(source[shift:, :], 2)
        before = weigh(source[: cells - shift, :], 0)
        return same + jnp.concatenate([after, fill], axis=0) + jnp.concatenate([fill, before], axis=0)

    edged[:, :EDGE, :] = jnp.zeros((cols, EDGE, depth), F32)
    edged[:, EDGE + rows :, :] = jnp.zeros((cols, EDGE, depth), F32)
    return spread, convolution, transposed_part


def by_place(points, run, *halves):
    for place in range(points):
        owners = [(place - k) % points for k in range(points)]
        lists = [[parts[k] for k in owners] for parts in halves]
        pl.when(lax.axis_index("path") == place)(functools.partial(run, place, *lists))


def channel_parts(depth):
    return [(at, min(at + 2 * LANES, depth)) for at in range(0, depth, 2 * LANES)]


def slopes_of_class(order, got, first_halves, first_bias, second_halves, second_bias, sizes):
    group_lon, group_lat, row_part, col_part = sizes
    points, depth = len(first_halves), got.shape[-1]
    rows, cols, part = group_lon * row_part, group_lat * col_part, row_part * col_part
    cells = rows * cols

    def kernel(order, got, first_bias, second_bias, *refs):
        first_slope, second_slope, edged, near_taps, far_taps = refs[2 * points :]

        def run(place, first, second):
            spread, convolution, _ = class_tools(sizes, depth, edged)
            field = jnp.dot(order[...], got[:, :part, :].reshape(cells, depth), preferred_element_type=F32)
            spread(field, 1, 0, near_taps)
            act, first_slope[...] = gelu_and_slope(convolution(near_taps, first, 1) + first_bias[...].reshape(1, -1))
            spread(field + act, FAR // NEAR, 0, far_taps)
            pre = convolution(far_taps, second, FAR // NEAR) + second_bias[...].reshape(1, -1)
            second_slope[...] = gelu_and_slope(pre)[1]

        by_place(points, run, refs[:points], refs[points : 2 * points])

    return call(
        kernel,
        [((cells, depth), F32)] * 2,
        [pltpu.VMEM((cols, rows + 2 * EDGE, depth), F32)] + [pltpu.VMEM((cells, 3 * depth), BF16)] * 2,
        "slopes_of_class",
        16,
        order,
        got,
        first_bias,
        second_bias,
        *first_halves,
        *second_halves,
    )


def adjoint_of_class(order, cotangents, first_slope, second_slope, first_halves, second_halves, sizes):
    group_lon, group_lat, row_part, col_part = sizes
    points, depth = len(first_halves), first_slope.shape[-1]
    rows, cols = group_lon * row_part, group_lat * col_part
    cells = rows * cols

    def kernel(order, first_slope, second_slope, *refs):
        sent, edged, near_taps, far_taps, grad = refs[3 * points :]

        def run(place, cotangent, first, second):
            spread, _, transposed_part = class_tools(sizes, depth, edged)
            def near_part(at, end):
                sides = [near_taps[j * rows : j * rows + cells, :] for j in range(3)]
                blocks = [
                    jnp.concatenate([part[2 - i, 2 - j] for part in first], axis=0)[at:end]
                    for j in range(3)
                    for i in range(3)
                ]
                dims = (((1,), (1,)), ((), ()))
                joint, weights = jnp.concatenate(sides, axis=1), jnp.concatenate(blocks, axis=1)
                return lax.dot_general(joint, weights, dims, preferred_element_type=F32)

            near_taps[:rows, :] = jnp.zeros((rows, 3 * depth), BF16)
            near_taps[rows + cells :, :] = jnp.zeros((rows, 3 * depth), BF16)
            upstream = jnp.concatenate([share[...].astype(F32) for share in cotangent], axis=1)
            upstream = jnp.dot(order[...], upstream.reshape(cells, depth).astype(BF16), preferred_element_type=F32)
            spread(second_slope[...] * upstream, FAR // NEAR, 0, far_taps)
            for at, end in channel_parts(depth):
                hidden_adj = upstream[:, at:end] + transposed_part(far_taps, second, FAR // NEAR, at, end)
                grad[:, at:end] = hidden_adj
                spread(first_slope[:, at:end] * hidden_adj, 1, at, near_taps.at[rows : rows + cells])
            slow, fast, listing = lon_parts()
            dims = (group_lat, col_part, slow, fast, points, row_part // points)
            home = ordering(dims, (3, 0, 4, 2, 5, 1), (2, listing))
            for at, end in channel_parts(depth):
                grad[:, at:end] += near_part(at, end)
            sent[...] = jnp.dot(home, grad[...].astype(BF16), preferred_element_type=F32).astype(BF16)

        by_place(points, run, refs[:points], refs[points : 2 * points], refs[2 * points : 3 * points])

    return call(
        kernel,
        [((cells, depth), BF16)],
        [pltpu.VMEM((cols, rows + 2 * EDGE, depth), F32)]
        + [pltpu.VMEM((cells + 2 * rows, 3 * depth), BF16), pltpu.VMEM((cells, 3 * depth), BF16)]
        + [pltpu.VMEM((cells, depth), F32)],
        "adjoint_of_class",
        16,
        order,
        first_slope,
        second_slope,
        *cotangents,
        *first_halves,
        *second_halves,
    )[0]


def attribution_rows(home, diff_rows, rows, cols):
    points, depth = lax.axis_size("path"), home.shape[-1]
    cells, group_lat = rows * cols, group_sizes()[1]

    def kernel(home, diff_rows, out, held, sems):
        bits, ahead = (NEAR * NEAR).bit_length() - 1, (group_lat * lon_parts()[1]).bit_length() - 1
        of_class = tuple(i + (i >= ahead) for i in range(bits))
        dims = (2,) * ahead + (points,) + (2,) * (bits - ahead) + (rows // NEAR, cols // NEAR)
        row_bits, col_bits = of_class[: bits // 2], of_class[bits // 2 :]
        order = ordering(dims, (ahead, bits + 1) + row_bits + (bits + 2,) + col_bits)
        order = sum(order[k * cells : (k + 1) * cells] for k in range(points))
        copies = []
        for i in range(2):
            span = slice(i * cells // 2, (i + 1) * cells // 2)
            moved = jnp.dot(order[span], home[...], preferred_element_type=F32)
            place = pl.ds(i * rows // 2, rows // 2)
            held[place] = (diff_rows[span, :] * moved).reshape(rows // 2, cols, depth).astype(BF16)
            copies.append(pltpu.make_async_copy(held.at[place], out.at[place], sems.at[i]))
            copies[-1].start()
        for copy in copies:
            copy.wait()

    args = [pltpu.with_memory_space_constraint(x, pltpu.VMEM) for x in (home, diff_rows)]
    return pl.pallas_call(
        kernel,
        out_shape=pltpu.HBM((rows, cols, depth), BF16),
        in_specs=[VMEM] * 2,
        out_specs=pl.BlockSpec(memory_space=pltpu.HBM),
        scratch_shapes=[pltpu.VMEM((rows, cols, depth), BF16), pltpu.SemaphoreType.DMA((2,))],
        compiler_params=pltpu.CompilerParams(vmem_limit_bytes=4 << 20),
        name="attribution_rows",
    )(*args)


def one_group(observed, baseline, cotangent, first_weight, first_bias, second_weight, second_bias):
    rows, cols, depth = observed.shape
    points = lax.axis_size("path")
    sizes = group_sizes() + (rows // NEAR, cols // NEAR)

    def turned(values, step):
        return lax.ppermute(values, "path", [(i, (i + step) % points) for i in range(points)])

    side = math.isqrt(first_weight.shape[0])
    halves = [
        [x.reshape((side, side) + x.shape[1:]) for x in [part] + [turned(part, step) for step in range(1, points)]]
        for part in (first_weight, second_weight)
    ]
    to_classes, to_grid = row_orders(rows, cols, sizes)
    sent, diff_rows = pack_classes(to_classes, observed, baseline, cotangent)
    got = swap_listed(sent, points=False)
    own = got[:, sizes[2] * sizes[3] :, :]
    cotangents = [own] + [turned(own, step) for step in range(1, points)]
    first_slope, second_slope = slopes_of_class(to_grid, got, halves[0], first_bias, halves[1], second_bias, sizes)
    grad = adjoint_of_class(to_grid, cotangents, first_slope, second_slope, *halves, sizes)
    chunks = grad.reshape(NEAR * NEAR * points, -1, depth)
    home = swap_listed(chunks, points=True)
    return attribution_rows(home.reshape(grad.shape), diff_rows, rows // points, cols)


def several_groups(observed, baseline, cotangent, first_weight, first_bias, second_weight, second_bias):
    rows, cols, depth = observed.shape
    points, point = lax.axis_size("path"), lax.axis_index("path")
    group_lon, group_lat = group_sizes()
    row_part, col_part = rows // NEAR, cols // NEAR
    ring = [(i, (i + 1) % points) for i in range(points)]

    def whole_weight(part):
        held = jnp.zeros((part.shape[0], points) + part.shape[1:], part.dtype)
        for step in range(points):
            held = lax.dynamic_update_slice_in_dim(held, part[:, None], (point - step) % points, 1)
            if step < points - 1:
                part = lax.ppermute(part, "path", ring)
        return held.reshape(held.shape[0], -1, held.shape[3])

    first_full, second_full = whole_weight(first_weight), whole_weight(second_weight)
    diff = observed.astype(jnp.float32) - baseline.astype(jnp.float32)
    mix = (point.astype(jnp.float32) + 0.5) / points
    field = (baseline.astype(jnp.float32) + mix * diff).astype(jnp.bfloat16)
    sent = jnp.stack([to_classes(field), to_classes(cotangent)], axis=1)
    got = swap(sent).reshape(group_lon, group_lat, 2, row_part, col_part, depth)
    got = got.transpose(2, 0, 3, 1, 4, 5).reshape(2, group_lon * row_part, group_lat * col_part, depth)
    field, upstream = got[0], got[1].astype(jnp.float32)

    first_pre = stencil(field, first_full, 1, True) + first_bias
    hidden = (field.astype(jnp.float32) + smooth_act(first_pre)).astype(jnp.bfloat16)
    second_pre = stencil(hidden, second_full, FAR // NEAR, True) + second_bias
    second_adj = act_adjoint(second_pre, upstream).astype(jnp.bfloat16)
    hidden_adj = upstream + stencil(second_adj, second_full, FAR // NEAR, False)
    first_adj = act_adjoint(first_pre, hidden_adj).astype(jnp.bfloat16)
    grad = hidden_adj + stencil(first_adj, first_full, 1, False)

    part = row_part // points
    grad = grad.reshape(group_lon, points, part, group_lat, col_part, depth).transpose(1, 0, 3, 2, 4, 5)
    grad = grad.reshape(points, group_lon * group_lat, part, col_part, depth)
    total = lax.dynamic_index_in_dim(grad, point, 0, keepdims=False)
    for step in range(1, points):
        other = lax.dynamic_index_in_dim(grad, (point + step) % points, 0, keepdims=False)
        total = total + lax.ppermute(other, "path", [(i, (i + step) % points) for i in range(points)])
    home = swap(total.astype(jnp.bfloat16)).reshape(NEAR, NEAR, part, col_part, depth)
    home = home.transpose(2, 0, 3, 1, 4).reshape(rows // points, cols, depth).astype(jnp.float32)
    diff_rows = lax.dynamic_slice_in_dim(diff, point * (rows // points), rows // points, 0)
    return (diff_rows * home / points).astype(jnp.bfloat16)


def shards(*args):
    if group_sizes() == (lax.axis_size("lon"), lax.axis_size("lat")):
        return one_group(*args)
    return several_groups(*args)


def solution(mesh):
    placed = (
        P("lon", "lat", None),
        P("lon", "lat", None),
        P("lon", "lat", None),
        P(None, "path", None),
        P(),
        P(None, "path", None),
        P(),
    )
    return jax.shard_map(
        shards,
        mesh=mesh,
        in_specs=placed,
        out_specs=P(("lon", "path"), "lat", None),
        check_vma=False,
    )
```
